256 devices in a mesh: stream: 32 (over y_hi, z, core), et: 8 (over x, y_lo).
Axes of the slice: x: 4, y: 4 (y_hi: 2, y_lo: 2; y = y_hi * 2 + y_lo), z: 8, core: 2. Of those that a mesh axis runs over, the one named last changes fastest.
Arguments:
- residual_in: bfloat16 [512, 2048], P('stream', 'et'), may hold values from -3 to 3
- attn_gain: bfloat16 [2048], replicated, may hold values from 0.099609375 to 1.8984375
- q_gain: bfloat16 [128], replicated, may hold values from 0.099609375 to 1.8984375
- key_norm_gain: bfloat16 [128], replicated, may hold values from 0.099609375 to 1.8984375
- w_q: bfloat16 [2048, 4096], P(None, 'et'), may hold values from -0.125 to 0.125
- key_value_weight: bfloat16 [2048, 1024], P(None, 'et'), may hold values from -0.125 to 0.125
- w_o: bfloat16 [4096, 2048], P(None, 'et'), may hold values from -0.09375 to 0.09375
- key_value_cache: bfloat16 [512, 768, 2, 512], P(('stream', 'et')), may hold values from -4 to 4
- cache_length: int32 [512], P('stream'), may hold values from 1 to 768, as said below
- moe_gain: bfloat16 [2048], P('et'), may hold values from 0.099609375 to 1.8984375
- route_ids: int32 [512, 8], P('stream'), may hold values from 0 to 127, all different within a row; in each aligned block of 16 rows (0 to 15, 16 to 31, ...) at most 2 rows name the same one
- route_gates: float32 [512, 8], P('stream'), may hold values from 0.05 to 1
- w_gate_up: bfloat16 [128, 2, 2048, 768], P('stream', None, 'et'), may hold values from -0.125 to 0.125
- w_down: bfloat16 [128, 768, 2048], P('stream', None, 'et'), may hold values from -0.21875 to 0.21875
Outputs:
- layer_out: bfloat16 [512, 2048], P('stream', 'et')
The draws below stay inside these ranges and needn't reach their ends.
Inputs may be any that keep to these rules, and one draw needn't show every extreme that they name: `route_ids`: each row names 8 different experts. Within each aligned block of 16 rows no expert is named more than 2 times, a bound that some block reaches. `cache_length`: some stream holds exactly 768 cached positions.
All inputs are finite; a program needn't handle non-finite values.
Results may differ from the reference program's by a relative error of at most 0.02.
Values may be sent and summed in bfloat16 or wider, within the bound.
A program may use at most 64 MiB of HBM per device.

```python
import math
import jax
import jax.numpy as jnp
import numpy as np
from jax import lax

MODEL_WIDTH = 2048
QUERY_HEADS = 32
KEY_VALUE_HEADS = 4
HEAD_SIZE = 128
F = 768
TOP = 8
CAP = 2
STREAMS_PER_PART = 16
CACHE_LENGTH = 768
EXPERTS = 128
TOKEN_COUNT = 512
N_STREAM = 32


def draw_cache_length(key, part):
    key = jax.random.fold_in(key, 7)
    first, second = jax.random.split(key)
    lengths = jax.random.randint(first, (TOKEN_COUNT,), 1, CACHE_LENGTH + 1)
    spot = jax.random.randint(second, (), 0, TOKEN_COUNT)
    lengths = jnp.where(jnp.arange(TOKEN_COUNT) == spot, CACHE_LENGTH, lengths)
    return lengths.astype(jnp.int32)


def level_of(rng, extent, shards, smallest, largest):
    def one(dim, shards_of):
        steps = jax.random.uniform(jax.random.fold_in(jax.random.fold_in(rng, 6), dim), (shards_of,), jnp.float32, smallest / len(shards), largest / len(shards))
        return jnp.repeat(jnp.exp(steps), extent[dim] // shards_of).reshape((-1,) + (1,) * (len(extent) - dim - 1))

    loudness = one(*shards[0])
    for cut in shards[1:]:
        loudness = loudness * one(*cut)
    return loudness


def assign_block(key, own, number, rows, number_of, top, most, lean):
    ranking = jax.random.permutation(key, number_of)
    heavy_load, usual = load_shares(number_of, rows * top, most, lean, True), load_shares(number_of, rows * top, most, lean, False)
    places = jnp.arange(number_of)

    def named(sizes, rotation):
        used = int((sizes > 0).sum())
        fixed = max(1, used // 4)
        passed = fixed + (places - fixed + rotation * (used - fixed)) % max(1, number_of - fixed)
        return jnp.zeros((number_of,), jnp.int32).at[ranking[jnp.where(places < fixed, places, passed)]].set(jnp.asarray(sizes, jnp.int32))

    sizes = jnp.where(number % 4 == 0, named(heavy_load, number // 4), named(usual, number - number // 4 - 1))
    mixed = jax.random.permutation(jax.random.fold_in(own, 3), number_of)
    giver, sink = mixed[0:number_of // 2 * 2:2], mixed[1:number_of // 2 * 2:2]
    room = jnp.minimum(sizes[giver] - 1, most - sizes[sink]) // 2
    room = jnp.where((giver == ranking[0]) | (sink == ranking[0]) | (sizes[sink] == 0), 0, jnp.maximum(room, 0))
    passed = jax.random.randint(jax.random.fold_in(own, 4), (number_of // 2,), 0, 1 << 20) % (room + 1)
    sizes = sizes.at[giver].add(-passed).at[sink].add(passed)
    members = jnp.searchsorted(jnp.cumsum(sizes), jnp.arange(rows * top), side="right").astype(jnp.int32)
    listing = members.reshape(top, rows).T
    listing = listing[jax.random.permutation(jax.random.fold_in(own, 1), rows)]
    rotation = jax.random.randint(jax.random.fold_in(own, 2), (rows, 1), 0, top)
    return jnp.take_along_axis(listing, (jnp.arange(top)[None, :] + rotation) % top, axis=1)


def load_shares(count, total, bound, skew, full):
    loads = [(1 << 20) // math.isqrt(standing ** skew) + 1 for standing in range(1, count + 1)]
    largest = bound if full else min(bound, max(-(-total // count), total * loads[0] // sum(loads)))
    least = 1 if total - largest >= count - 1 else 0
    given, surplus = [largest] + [least] * (count - 1), total - largest - least * (count - 1)
    while surplus > 0:
        movable = [i for i in range(1, count) if given[i] < largest] or [i for i in range(1, count) if given[i] < bound]
        pool, left = sum([loads[i] for i in movable]), surplus
        for i in movable:
            addition = min(bound - given[i], max(1, left * loads[i] // pool), surplus)
            given[i] = given[i] + addition
            surplus = surplus - addition
    return np.array(given)


def normal_values(rng, dims, spread, reach, pieces=(), held_as=jnp.bfloat16):
    values = spread * jax.random.normal(rng, dims, jnp.float32)
    if pieces:
        values = values * level_of(rng, dims, pieces, -0.22, 0.18)
    return jnp.clip(values, -reach, reach).astype(held_as)


def setup_inputs(seed: int = 0) -> dict:
    keys = jax.random.split(jax.random.key(seed), 15)
    residual_in = normal_values(keys[0], (TOKEN_COUNT, MODEL_WIDTH), 0.5, 3.0, ((0, 32), (1, 8)))
    attn_gain = jnp.clip(1.0 + 0.18 * jax.random.normal(keys[1], (MODEL_WIDTH,), jnp.float32), 0.099609375, 1.8984375).astype(jnp.bfloat16)
    q_gain = jnp.clip(1.0 + 0.18 * jax.random.normal(keys[2], (HEAD_SIZE,), jnp.float32), 0.099609375, 1.8984375).astype(jnp.bfloat16)
    key_norm_gain = jnp.clip(1.0 + 0.18 * jax.random.normal(keys[3], (HEAD_SIZE,), jnp.float32), 0.099609375, 1.8984375).astype(jnp.bfloat16)
    w_q = normal_values(keys[4], (MODEL_WIDTH, QUERY_HEADS * HEAD_SIZE), MODEL_WIDTH ** -0.5, 0.125, ((1, 8),))
    key_value_weight = normal_values(keys[5], (MODEL_WIDTH, 2 * KEY_VALUE_HEADS * HEAD_SIZE), MODEL_WIDTH ** -0.5, 0.125, ((1, 8),))
    w_o = normal_values(keys[6], (QUERY_HEADS * HEAD_SIZE, MODEL_WIDTH), (QUERY_HEADS * HEAD_SIZE) ** -0.5, 0.09375, ((1, 8),))
    key_value_cache = normal_values(keys[7], (TOKEN_COUNT, CACHE_LENGTH, 2, KEY_VALUE_HEADS * HEAD_SIZE), 1.0, 4.0, ((0, 256),))
    cache_length = draw_cache_length(jax.random.fold_in(keys[14], 71), 0)
    moe_gain = jnp.clip(1.0 + 0.18 * jax.random.normal(keys[9], (MODEL_WIDTH,), jnp.float32), 0.099609375, 1.8984375).astype(jnp.bfloat16)
    route_ids_keys = jax.random.split(jax.random.fold_in(keys[10], 1), TOKEN_COUNT // STREAMS_PER_PART)
    route_ids_turns = jax.random.permutation(jax.random.fold_in(keys[10], 3), TOKEN_COUNT // STREAMS_PER_PART)
    route_ids = jax.vmap(lambda own, number: assign_block(jax.random.fold_in(keys[10], 2), own, number, STREAMS_PER_PART, EXPERTS, TOP, CAP, 2))(route_ids_keys, route_ids_turns).reshape((TOKEN_COUNT, TOP))
    route_gates = jnp.clip(jnp.exp(math.log(1.0) - 2.9957323 * jax.random.uniform(keys[11], (TOKEN_COUNT, TOP), jnp.float32) ** level_of(keys[11], (TOKEN_COUNT, TOP), ((0, 32),), -0.2, 0.2)), 0.05, 1.0)
    w_gate_up = normal_values(keys[12], (EXPERTS, 2, MODEL_WIDTH, F), MODEL_WIDTH ** -0.5, 0.125, ((0, 32), (2, 8)))
    w_down = normal_values(keys[13], (EXPERTS, F, MODEL_WIDTH), F ** -0.5, 0.21875, ((0, 32), (2, 8)))
    return dict(residual_in=residual_in, attn_gain=attn_gain, q_gain=q_gain, key_norm_gain=key_norm_gain, w_q=w_q, key_value_weight=key_value_weight, w_o=w_o, key_value_cache=key_value_cache, cache_length=cache_length, moe_gain=moe_gain, route_ids=route_ids, route_gates=route_gates, w_gate_up=w_gate_up, w_down=w_down)


EPS = 1e-06
ROPE_BASE = 1000000.0

def per_head_norm(value_rows, gain):
    return value_rows * lax.rsqrt(lax.optimization_barrier(jnp.mean(value_rows * value_rows, axis=-1, keepdims=True)) + EPS) * gain.astype(jnp.float32)

def rotary_embed(value_rows, positions):
    half = value_rows.shape[-1] // 2
    steps = jnp.arange(half).astype(jnp.float32)
    freq = ROPE_BASE ** (-(2.0 * steps) / value_rows.shape[-1])
    angle = positions.astype(jnp.float32)[:, None, None] * freq
    cosine = jnp.cos(angle)
    sine = jnp.sin(angle)
    lower = value_rows[..., :half]
    upper = value_rows[..., half:]
    return jnp.concatenate([lower * cosine - upper * sine, upper * cosine + lower * sine], axis=-1)

def reference(residual_in, attn_gain, q_gain, key_norm_gain, w_q, key_value_weight, w_o, key_value_cache, cache_length, moe_gain, route_ids, route_gates, w_gate_up, w_down):
    input_f = residual_in.astype(jnp.float32)
    normed_input = (input_f * lax.rsqrt(lax.optimization_barrier(jnp.mean(input_f * input_f, axis=-1, keepdims=True)) + EPS) * attn_gain.astype(jnp.float32)).astype(jnp.bfloat16)
    query_vector = jnp.dot(normed_input, w_q, preferred_element_type=jnp.float32).reshape(TOKEN_COUNT, QUERY_HEADS, HEAD_SIZE)
    query_vector = rotary_embed(per_head_norm(query_vector, q_gain), cache_length).astype(jnp.bfloat16)
    fresh_key_value = jnp.dot(normed_input, key_value_weight, preferred_element_type=jnp.float32).reshape(TOKEN_COUNT, 2 * KEY_VALUE_HEADS, HEAD_SIZE)
    incoming_key = rotary_embed(per_head_norm(fresh_key_value[:, :KEY_VALUE_HEADS], key_norm_gain), cache_length).astype(jnp.bfloat16)
    incoming_value = fresh_key_value[:, KEY_VALUE_HEADS:].astype(jnp.bfloat16)
    query_group = QUERY_HEADS // KEY_VALUE_HEADS
    scale = HEAD_SIZE ** (-0.5)

    def attend_cache(block):
        query_block_part, cache_block_part, block_len, key_block_part, value_block_part = block
        input_rows = query_block_part.shape[0]
        query_rows_all = query_block_part.reshape(input_rows, KEY_VALUE_HEADS, query_group, HEAD_SIZE).astype(jnp.float32)
        key_rows = cache_block_part[:, :, 0].reshape(input_rows, CACHE_LENGTH, KEY_VALUE_HEADS, HEAD_SIZE).astype(jnp.float32)
        value_rows = cache_block_part[:, :, 1].reshape(input_rows, CACHE_LENGTH, KEY_VALUE_HEADS, HEAD_SIZE).astype(jnp.float32)
        scores = jnp.einsum('shgd,slhd->shgl', query_rows_all, key_rows) * scale
        live = (jnp.arange(CACHE_LENGTH)[None, :] < block_len[:, None])[:, None, None, :]
        weights = jnp.where(live, jnp.exp(scores), 0.0)
        total = lax.optimization_barrier(jnp.sum(weights, axis=-1))
        summed = jnp.einsum('shgl,slhd->shgd', weights.astype(jnp.bfloat16).astype(jnp.float32), value_rows)
        updated_keys = key_block_part.reshape(input_rows, KEY_VALUE_HEADS, 1, HEAD_SIZE).astype(jnp.float32)
        updated_values = value_block_part.reshape(input_rows, KEY_VALUE_HEADS, 1, HEAD_SIZE).astype(jnp.float32)
        fresh = jnp.exp(lax.optimization_barrier(jnp.sum(query_rows_all * updated_keys, axis=-1)) * scale)
        summed = summed + fresh[..., None] * updated_values
        total = total + fresh
        return (summed / total[..., None]).astype(jnp.bfloat16).reshape(input_rows, QUERY_HEADS * HEAD_SIZE)
    attention_mixed = lax.map(attend_cache, (query_vector.reshape(N_STREAM, STREAMS_PER_PART, QUERY_HEADS, HEAD_SIZE), key_value_cache.reshape(N_STREAM, STREAMS_PER_PART, CACHE_LENGTH, 2, KEY_VALUE_HEADS * HEAD_SIZE), cache_length.reshape(N_STREAM, STREAMS_PER_PART), incoming_key.reshape(N_STREAM, STREAMS_PER_PART, KEY_VALUE_HEADS, HEAD_SIZE), incoming_value.reshape(N_STREAM, STREAMS_PER_PART, KEY_VALUE_HEADS, HEAD_SIZE)))
    attention_mixed = attention_mixed.reshape(TOKEN_COUNT, QUERY_HEADS * HEAD_SIZE)
    resid = (input_f + jnp.dot(attention_mixed, w_o, preferred_element_type=jnp.float32)).astype(jnp.bfloat16)
    resid_f = resid.astype(jnp.float32)
    expert_in = (resid_f * lax.rsqrt(lax.optimization_barrier(jnp.mean(resid_f * resid_f, axis=-1, keepdims=True)) + EPS) * moe_gain.astype(jnp.float32)).astype(jnp.bfloat16)
    gate_weight = route_gates / lax.optimization_barrier(jnp.sum(route_gates, axis=-1, keepdims=True))
    flat_ids = route_ids.reshape(-1)
    flat_weight = gate_weight.reshape(-1)
    most_rows = CAP * N_STREAM

    def expert_step(total, expert):
        hit = flat_ids == expert
        count = jnp.sum(hit.astype(jnp.int32))
        picks = jnp.nonzero(hit, size=most_rows, fill_value=0)[0]
        token_rows = picks // TOP
        weight = jnp.where(jnp.arange(most_rows) < count, flat_weight[picks], 0.0)
        input_rows = expert_in[token_rows]
        gate = jnp.dot(input_rows, w_gate_up[expert, 0], preferred_element_type=jnp.float32)
        up_part = jnp.dot(input_rows, w_gate_up[expert, 1], preferred_element_type=jnp.float32)
        hidden = (jax.nn.silu(gate) * up_part).astype(jnp.bfloat16)
        out_rows = jnp.dot(hidden, w_down[expert], preferred_element_type=jnp.float32).astype(jnp.bfloat16)
        total = total.at[token_rows].add(weight[:, None] * out_rows.astype(jnp.float32))
        return (total, None)
    total, _ = lax.scan(expert_step, jnp.zeros((TOKEN_COUNT, MODEL_WIDTH), jnp.float32), jnp.arange(EXPERTS))
    return (resid_f + total).astype(jnp.bfloat16)
```

```python
import functools
import math

import jax
import jax.numpy as jnp
from jax import lax
from jax.experimental import pallas as pl
from jax.experimental.pallas import tpu as pltpu
from jax.sharding import PartitionSpec as P

EPS = 1e-06
ROPE_BASE = 1000000.0
CAP = 2
LANES = 128
MESH = pl.DeviceIdType.MESH
F32 = jnp.float32
BF16 = jnp.bfloat16

FEATURES, HEADS, MIXED, PAIRS, HIDDEN = range(5)
OUTWARD, HOME = range(2)


def iota(shape, dim):
    return lax.broadcasted_iota(jnp.int32, shape, dim)


def dot(a, b):
    return jnp.dot(a, b, preferred_element_type=F32)


def dot_nt(a, b):
    return lax.dot_general(a, b, (((1,), (1,)), ((), ())), preferred_element_type=F32)


def dot_tn(a, b):
    return lax.dot_general(a, b, (((0,), (0,)), ((), ())), preferred_element_type=F32)


def kernel(
    n_stream,
    n_et,
    res_hbm,
    attn_gain_hbm,
    q_gain_hbm,
    key_gain_hbm,
    w_q_hbm,
    w_kv_hbm,
    w_o_hbm,
    cache_hbm,
    length_hbm,
    moe_gain_hbm,
    ids_hbm,
    gates_hbm,
    w_gu_hbm,
    w_down_hbm,
    out_ref,
    attn_gain,
    q_gain,
    key_gain,
    w_q,
    w_kv,
    w_o,
    cache,
    length,
    moe_gain,
    ids,
    gates,
    w_gu,
    w_down,
    features,
    heads_out,
    heads_in,
    mixed_out,
    mixed_in,
    mixed_f,
    rows_out,
    rows_in,
    rows_f,
    expert_rows,
    expert_squares,
    pairs_out,
    pairs_own,
    pairs_in,
    hidden_out,
    hidden_in,
    results_f,
    results_out,
    results_in,
    load_sem,
    et_send,
    et_recv,
    stream_send,
    stream_recv,
):
    me_s = lax.axis_index("stream")
    me = lax.axis_index("et")
    tokens = res_hbm.shape[0]
    local = tokens // n_et
    head_dim = q_gain_hbm.shape[1]
    own_heads = w_q_hbm.shape[1] // head_dim
    n_heads = own_heads * n_et
    kv_heads = n_et // 2
    group = n_heads // kv_heads
    width = res_hbm.shape[1] * n_et
    n_local = w_gu_hbm.shape[0]
    slots = n_stream * n_local * CAP
    scale = head_dim**-0.5

    loads = {}
    for name, source, target in (
        ("own", res_hbm, features.at[me]),
        ("length", length_hbm, length),
        ("attn_gain", attn_gain_hbm, attn_gain),
        ("q_gain", q_gain_hbm, q_gain),
        ("key_gain", key_gain_hbm, key_gain),
        ("ids", ids_hbm, ids),
        ("gates", gates_hbm, gates),
        ("moe_gain", moe_gain_hbm, moe_gain),
        ("w_q", w_q_hbm, w_q),
        ("w_kv", w_kv_hbm, w_kv),
        ("cache", cache_hbm, cache),
        ("w_o", w_o_hbm, w_o),
        ("w_gu", w_gu_hbm, w_gu),
        ("w_down", w_down_hbm, w_down),
    ):
        loads[name] = pltpu.make_async_copy(source, target, load_sem.at[len(loads)])
        loads[name].start()

    def et_peer(step):
        return lax.rem(me + step, n_et)

    def stream_peer(step):
        return lax.rem(me_s + step, n_stream)

    def et_copy(exchange, source, target, peer):
        return pltpu.make_async_remote_copy(
            src_ref=source,
            dst_ref=target,
            send_sem=et_send.at[exchange, peer],
            recv_sem=et_recv.at[exchange, me],
            device_id=(me_s, peer),
            device_id_type=MESH,
        )

    def et_arrival(exchange, source, target, peer):
        return pltpu.make_async_remote_copy(
            src_ref=source,
            dst_ref=target,
            send_sem=et_send.at[exchange, peer],
            recv_sem=et_recv.at[exchange, peer],
            device_id=(me_s, peer),
            device_id_type=MESH,
        )

    def stream_copy(exchange, source, target, peer):
        return pltpu.make_async_remote_copy(
            src_ref=source,
            dst_ref=target,
            send_sem=stream_send.at[exchange, peer],
            recv_sem=stream_recv.at[exchange, me_s],
            device_id=(peer, me),
            device_id_type=MESH,
        )

    def stream_arrival(exchange, source, target, peer):
        return pltpu.make_async_remote_copy(
            src_ref=source,
            dst_ref=target,
            send_sem=stream_send.at[exchange, peer],
            recv_sem=stream_recv.at[exchange, peer],
            device_id=(peer, me),
            device_id_type=MESH,
        )

    def loop(n, body):
        def step(i, carry):
            body(i)
            return carry

        lax.fori_loop(1, n, step, 0)

    barrier = pltpu.get_barrier_semaphore()
    loop(
        n_et,
        lambda i: pl.semaphore_signal(
            barrier, inc=1, device_id=(me_s, et_peer(i)), device_id_type=MESH
        ),
    )
    loop(
        n_stream,
        lambda i: pl.semaphore_signal(
            barrier, inc=1, device_id=(stream_peer(i), me), device_id_type=MESH
        ),
    )
    pl.semaphore_wait(barrier, n_et + n_stream - 2)

    loop(
        n_et,
        lambda i: et_copy(FEATURES, res_hbm, features.at[me], et_peer(i)).start(),
    )

    loads["length"].wait()
    lengths = jnp.broadcast_to(length[...], (tokens, tokens)).astype(F32)
    diagonal = iota((tokens, tokens), 0) == iota((tokens, tokens), 1)
    positions = jnp.sum(jnp.where(diagonal, lengths, 0.0), axis=1, keepdims=True)
    half = head_dim // 2
    lane = iota((tokens, head_dim), 1)
    steps = jnp.where(lane < half, lane, lane - half).astype(F32)
    angle = positions * jnp.exp(steps * (-2.0 * math.log(ROPE_BASE) / head_dim))
    cosine = jnp.cos(angle)
    sine = jnp.where(lane < half, -jnp.sin(angle), jnp.sin(angle))

    pad = 16
    row = iota((n_et * pad, LANES), 0)
    col = iota((n_et * pad, LANES), 1)
    peer_of, at = lax.div(row, pad), lax.rem(row, pad)
    n_q = local * own_heads
    picked = jnp.where(
        at < n_q,
        lax.rem(at, own_heads) * tokens + peer_of * local + lax.div(at, own_heads),
        jnp.where(
            at < n_q + local, own_heads * tokens + peer_of * local + at - n_q, -1
        ),
    )
    order_out = jnp.where(col == picked, 1.0, 0.0).astype(BF16)

    per = local * n_heads
    row = iota((3 * per, n_et * pad), 0)
    col = iota((3 * per, n_et * pad), 1)
    kind, at = lax.div(row, per), lax.rem(row, per)
    token, head = lax.div(at, n_heads), lax.rem(at, n_heads)
    picked = jnp.where(
        kind == 0,
        lax.div(head, own_heads) * pad + token * own_heads + lax.rem(head, own_heads),
        (lax.div(head, group) + jnp.where(kind == 2, kv_heads, 0)) * pad + n_q + token,
    )
    order_in = jnp.where(col == picked, 1.0, 0.0).astype(BF16)

    loads["ids"].wait()
    loads["gates"].wait()
    at = iota((slots, tokens), 0)
    place = lax.rem(at, n_local * CAP)
    expert = lax.div(at, n_local * CAP) * n_local + lax.rem(place, n_local)
    which = lax.div(place, n_local)
    gate = gates[...]
    gate = gate / jnp.sum(gate, axis=0, keepdims=True)
    named = jnp.zeros((slots, tokens), F32)
    weight = jnp.zeros((slots, tokens), F32)
    for k in range(ids_hbm.shape[0]):
        hit = expert == ids[k : k + 1, :]
        named = jnp.where(hit, 1.0, named)
        weight = jnp.where(hit, gate[k : k + 1, :], weight)
    before = jnp.where(
        iota((tokens, tokens), 0) < iota((tokens, tokens), 1), 1.0, 0.0
    ).astype(BF16)
    earlier = dot(named.astype(BF16), before)
    placed = jnp.where(earlier == which.astype(F32), named, 0.0)
    mixing = placed * weight
    placed = placed.astype(BF16)
    mixing_high = mixing.astype(BF16)
    mixing_low = (mixing - mixing_high.astype(F32)).astype(BF16)

    loads["own"].wait()
    loads["attn_gain"].wait()
    loop(
        n_et,
        lambda i: et_arrival(
            FEATURES, res_hbm, features.at[et_peer(i)], et_peer(i)
        ).wait_recv(),
    )
    full = jnp.concatenate([features[i].astype(F32) for i in range(n_et)], axis=1)
    gain = attn_gain[...].astype(F32)
    gain = jnp.concatenate([gain[i : i + 1] for i in range(gain.shape[0])], axis=1)
    normed = (
        full
        * lax.rsqrt(jnp.sum(full * full, axis=1, keepdims=True) * (1.0 / width) + EPS)
        * gain
    ).astype(BF16)

    def rotated(v, g):
        v = v * lax.rsqrt(jnp.mean(v * v, axis=1, keepdims=True) + EPS) * g
        return v * cosine + pltpu.roll(v, half, 1) * sine

    loads["q_gain"].wait()
    loads["key_gain"].wait()
    loads["w_q"].wait()
    query = dot(normed, w_q[...])
    loads["w_kv"].wait()
    key_value = dot(normed, w_kv[...])
    query_gain = q_gain[...].astype(F32)
    made = [
        rotated(query[:, i * head_dim : (i + 1) * head_dim], query_gain)
        for i in range(own_heads)
    ]
    made.append(
        jnp.where(me < kv_heads, rotated(key_value, key_gain[...].astype(F32)), key_value)
    )
    made.append(jnp.zeros((LANES - (own_heads + 1) * tokens, head_dim), F32))
    made = jnp.concatenate(made, axis=0).astype(BF16)
    heads_out[...] = dot(order_out, made).astype(BF16).reshape(heads_out.shape)
    heads_in[me] = heads_out[me]
    loop(
        n_et,
        lambda i: et_copy(
            HEADS, heads_out.at[et_peer(i)], heads_in.at[me], et_peer(i)
        ).start(),
    )

    rows_of = cache_hbm.shape[0] // local
    piece = 768
    own_lane = iota((1, tokens), 1)
    lengths = length[...].astype(F32)
    loads["cache"].wait()
    loop(
        n_et,
        lambda i: et_arrival(
            HEADS, heads_out.at[et_peer(i)], heads_in.at[et_peer(i)], et_peer(i)
        ).wait_recv(),
    )
    ordered = dot(order_in, heads_in[...].reshape(n_et * pad, head_dim))
    for t in range(local):
        q = ordered[t * n_heads : (t + 1) * n_heads]
        new_key = ordered[per + t * n_heads : per + (t + 1) * n_heads]
        new_value = ordered[2 * per + t * n_heads : 2 * per + (t + 1) * n_heads]
        fresh = jnp.exp(jnp.sum(q * new_key, axis=1, keepdims=True) * scale)
        limit = (
            jnp.sum(
                jnp.where(own_lane == me * local + t, lengths, 0.0),
                axis=1,
                keepdims=True,
            )
            * float(2 * kv_heads)
        ).astype(jnp.int32)
        q = q.astype(BF16)
        column = iota((n_heads, piece), 1)
        aligned = lax.rem(column, 2 * kv_heads) == 2 * lax.div(
            iota((n_heads, piece), 0), group
        )
        total = fresh
        summed = fresh * new_value
        for p in range(rows_of // piece):
            block = cache[t * rows_of + p * piece : t * rows_of + (p + 1) * piece, :]
            score = dot_nt(q, block)
            live = aligned & (column < limit - p * piece)
            weights = jnp.where(live, jnp.exp(score * scale), 0.0)
            total = total + jnp.sum(weights, axis=1, keepdims=True)
            moved = jnp.concatenate(
                [
                    pltpu.roll(weights[:, i : i + LANES], 1, 1)
                    for i in range(0, piece, LANES)
                ],
                axis=1,
            )
            summed = summed + dot(moved.astype(BF16), block)
        mixed_out[t * n_heads : (t + 1) * n_heads, :] = (summed / total).astype(BF16)
    mixed_in[me] = mixed_out[...]
    loop(
        n_et,
        lambda i: et_copy(MIXED, mixed_out, mixed_in.at[me], et_peer(i)).start(),
    )

    loads["w_o"].wait()
    loop(
        n_et,
        lambda i: et_arrival(
            MIXED, mixed_out, mixed_in.at[et_peer(i)], et_peer(i)
        ).wait_recv(),
    )
    mixed_f[...] = mixed_in[...].reshape(tokens * n_heads, head_dim).astype(F32)
    attended = jnp.concatenate(
        [mixed_f[pl.ds(h, tokens, stride=n_heads), :] for h in range(n_heads)], axis=1
    ).astype(BF16)
    resid = (features[me].astype(F32) + dot(attended, w_o[...])).astype(BF16)

    sent = dot(placed, resid)
    sent = sent.reshape(n_stream, n_local * CAP, 2 * LANES)
    rows_out[...] = jnp.concatenate(
        [sent[:, :, :LANES], sent[:, :, LANES:]], axis=1
    ).astype(BF16)
    rows_in[me_s] = rows_out[me_s]
    loop(
        n_stream,
        lambda i: stream_copy(
            OUTWARD, rows_out.at[stream_peer(i)], rows_in.at[me_s], stream_peer(i)
        ).start(),
    )
    loads["moe_gain"].wait()
    gain = moe_gain[...].astype(F32)
    gain = jnp.concatenate([gain[0:1], gain[1:2]], axis=1)
    loads["w_gu"].wait()
    loop(
        n_stream,
        lambda i: stream_arrival(
            OUTWARD, rows_out.at[stream_peer(i)], rows_in.at[stream_peer(i)], stream_peer(i)
        ).wait_recv(),
    )
    chunk = 2 * n_local * CAP
    rows_f[...] = rows_in[...].reshape(n_stream * chunk, LANES).astype(F32)
    for j in range(n_local):
        taken = []
        for c in range(CAP):
            taken.append(
                jnp.concatenate(
                    [
                        rows_f[
                            pl.ds(h * n_local * CAP + c * n_local + j, n_stream, stride=chunk), :
                        ]
                        for h in range(2)
                    ],
                    axis=1,
                )
            )
        taken = jnp.concatenate(taken, axis=0)
        squares = jnp.sum(taken * taken, axis=1, keepdims=True)
        high = squares.astype(BF16).astype(F32)
        expert_squares[j] = jnp.where(
            iota((CAP * n_stream, LANES), 1) < LANES // 2, high, squares - high
        )
        expert_rows[j] = (taken * gain).astype(BF16)

    hidden_width = w_down_hbm.shape[1]
    for i in range(n_local):
        j = lax.rem(lax.div(me, CAP) + 1 + i, n_local)
        taken = expert_rows[j]
        products = jnp.concatenate(
            [dot(taken, w_gu[j, 0]), dot(taken, w_gu[j, 1]), expert_squares[j]], axis=1
        )
        pairs_out[i] = products.astype(BF16).reshape(pairs_out.shape[1:])
        if i < n_local - 1:
            for c in range(CAP):
                et_copy(
                    PAIRS, pairs_out.at[i, c], pairs_in.at[me], CAP * j + c
                ).start()
        else:
            pairs_own[...] = products.reshape(pairs_own.shape)
            c = 1 - lax.rem(me, CAP)
            et_copy(PAIRS, pairs_out.at[i, c], pairs_in.at[me], CAP * j + c).start()
    pair = pairs_own[lax.rem(me, CAP)]
    for i in range(1, n_et):
        et_arrival(
            PAIRS, pairs_out.at[0, 0], pairs_in.at[et_peer(i)], et_peer(i)
        ).wait_recv()
        pair = pair + pairs_in[et_peer(i)].astype(F32)
    squares = jnp.sum(pair[:, 2 * hidden_width :], axis=1, keepdims=True) * (
        2.0 / LANES / width
    )
    level = lax.rsqrt(squares + EPS)
    first = pair[:, :hidden_width] * level
    second = pair[:, hidden_width : 2 * hidden_width] * level
    hidden_out[...] = (first / (1.0 + jnp.exp(-first)) * second).astype(BF16)
    hidden_in[me] = hidden_out[...]
    loop(
        n_et,
        lambda i: et_copy(HIDDEN, hidden_out, hidden_in.at[me], et_peer(i)).start(),
    )

    loads["w_down"].wait()
    loop(
        n_et,
        lambda i: et_arrival(
            HIDDEN, hidden_out, hidden_in.at[et_peer(i)], et_peer(i)
        ).wait_recv(),
    )
    for j in range(n_local):
        hidden = hidden_in[CAP * j : CAP * (j + 1)].reshape(CAP * n_stream, hidden_width)
        result = dot(hidden, w_down[j])
        for c in range(CAP):
            for h in range(2):
                results_f[
                    pl.ds(h * n_local * CAP + c * n_local + j, n_stream, stride=chunk), :
                ] = result[c * n_stream : (c + 1) * n_stream, h * LANES : (h + 1) * LANES]
    results_out[...] = results_f[...].astype(BF16).reshape(results_out.shape)
    results_in[me_s] = results_out[me_s]
    loop(
        n_stream,
        lambda i: stream_copy(
            HOME, results_out.at[stream_peer(i)], results_in.at[me_s], stream_peer(i)
        ).start(),
    )
    loop(
        n_stream,
        lambda i: stream_arrival(
            HOME, results_out.at[stream_peer(i)], results_in.at[stream_peer(i)], stream_peer(i)
        ).wait_recv(),
    )
    returned = results_in[...].astype(F32)
    returned = (
        jnp.concatenate(
            [returned[:, : n_local * CAP], returned[:, n_local * CAP :]], axis=2
        )
        .reshape(slots, 2 * LANES)
        .astype(BF16)
    )
    routed = dot_tn(mixing_high, returned) + dot_tn(mixing_low, returned)
    out_ref[...] = (resid.astype(F32) + routed).astype(BF16)

    def sent_et(exchange, source, target):
        loop(
            n_et,
            lambda i: et_copy(exchange, source, target, et_peer(i)).wait_send(),
        )

    sent_et(FEATURES, res_hbm, features.at[me])
    sent_et(HEADS, heads_out.at[0], heads_in.at[me])
    sent_et(MIXED, mixed_out, mixed_in.at[me])
    sent_et(PAIRS, pairs_out.at[0, 0], pairs_in.at[me])
    sent_et(HIDDEN, hidden_out, hidden_in.at[me])
    for exchange, source, target in (
        (OUTWARD, rows_out, rows_in),
        (HOME, results_out, results_in),
    ):
        loop(
            n_stream,
            lambda i: stream_copy(
                exchange, source.at[stream_peer(i)], target.at[me_s], stream_peer(i)
            ).wait_send(),
        )


def on_device(
    n_stream,
    n_et,
    residual_in,
    attn_gain,
    q_gain,
    key_norm_gain,
    w_q,
    key_value_weight,
    w_o,
    key_value_cache,
    cache_length,
    moe_gain,
    route_ids,
    route_gates,
    w_gate_up,
    w_down,
):
    tokens, features = residual_in.shape
    head_dim = q_gain.shape[0]
    local, span, _, kv_width = key_value_cache.shape
    kv_heads = kv_width // head_dim
    n_heads = w_q.shape[1] // head_dim * n_et
    n_local = w_gate_up.shape[0]
    hidden = w_down.shape[1]
    cache = (
        key_value_cache.reshape(local, span, 2, kv_heads, head_dim)
        .transpose(0, 1, 3, 2, 4)
        .reshape(local * span * kv_heads * 2, head_dim)
    )
    args = (
        residual_in,
        attn_gain.reshape(-1, LANES),
        q_gain.reshape(1, -1),
        key_norm_gain.reshape(1, -1),
        w_q,
        key_value_weight,
        w_o,
        cache,
        cache_length.reshape(1, -1),
        moe_gain.reshape(-1, LANES),
        route_ids.T,
        route_gates.T,
        w_gate_up,
        w_down,
    )
    chunk = 2 * n_local * CAP
    vmem = pltpu.VMEM
    row_blocks = (n_stream, chunk, LANES)
    flat_rows = (n_stream * chunk, LANES)
    pair_width = 2 * hidden + LANES
    scratch = [vmem(a.shape, a.dtype) for a in args[1:]] + [
        vmem((n_et, tokens, features), BF16),
        vmem((n_et, 16, head_dim), BF16),
        vmem((n_et, 16, head_dim), BF16),
        vmem((local * n_heads, head_dim), BF16),
        vmem((n_et, local * n_heads, head_dim), BF16),
        vmem((tokens * n_heads, head_dim), F32),
        vmem(row_blocks, BF16),
        vmem(row_blocks, BF16),
        vmem(flat_rows, F32),
        vmem((n_local, CAP * n_stream, features), BF16),
        vmem((n_local, CAP * n_stream, LANES), F32),
        vmem((n_local, CAP, n_stream, pair_width), BF16),
        vmem((CAP, n_stream, pair_width), F32),
        vmem((n_et, n_stream, pair_width), BF16),
        vmem((n_stream, hidden), BF16),
        vmem((n_et, n_stream, hidden), BF16),
        vmem(flat_rows, F32),
        vmem(row_blocks, BF16),
        vmem(row_blocks, BF16),
        pltpu.SemaphoreType.DMA((len(args),)),
        pltpu.SemaphoreType.DMA((5, n_et)),
        pltpu.SemaphoreType.DMA((5, n_et)),
        pltpu.SemaphoreType.DMA((2, n_stream)),
        pltpu.SemaphoreType.DMA((2, n_stream)),
    ]
    return pl.pallas_call(
        functools.partial(kernel, n_stream, n_et),
        out_shape=jax.ShapeDtypeStruct(residual_in.shape, residual_in.dtype),
        in_specs=[pl.BlockSpec(memory_space=pl.ANY)] * len(args),
        out_specs=pl.BlockSpec(memory_space=pltpu.VMEM),
        scratch_shapes=scratch,
        compiler_params=pltpu.CompilerParams(
            collective_id=0, has_side_effects=True, vmem_limit_bytes=56 * 1024 * 1024
        ),
    )(*args)


def solution(mesh):
    placed = (
        P("stream", "et"),
        P(),
        P(),
        P(),
        P(None, "et"),
        P(None, "et"),
        P(None, "et"),
        P(("stream", "et"), None, None, None),
        P("stream"),
        P("et"),
        P("stream", None),
        P("stream", None),
        P("stream", None, "et", None),
        P("stream", None, "et"),
    )
    return jax.shard_map(
        functools.partial(on_device, mesh.shape["stream"], mesh.shape["et"]),
        mesh=mesh,
        in_specs=placed,
        out_specs=P("stream", "et"),
        check_vma=False,
    )
```

```python
import functools
import math

import jax
import jax.numpy as jnp
from jax import lax
from jax.experimental import pallas as pl
from jax.experimental.pallas import tpu as pltpu
from jax.sharding import PartitionSpec as P

EPS = 1e-06
ROPE_BASE = 1000000.0
CAP = 2
LANES = 128
MESH = pl.DeviceIdType.MESH
F32 = jnp.float32
BF16 = jnp.bfloat16

FEATURES, HEADS, MIXED, PAIRS, HIDDEN = range(5)
OUTWARD, HOME = range(2)


def iota(shape, dim):
    return lax.broadcasted_iota(jnp.int32, shape, dim)


def dot(a, b):
    return jnp.dot(a, b, preferred_element_type=F32)


def dot_nt(a, b):
    return lax.dot_general(a, b, (((1,), (1,)), ((), ())), preferred_element_type=F32)


def dot_tn(a, b):
    return lax.dot_general(a, b, (((0,), (0,)), ((), ())), preferred_element_type=F32)


def kernel(
    n_stream,
    n_et,
    res_hbm,
    attn_gain_hbm,
    q_gain_hbm,
    key_gain_hbm,
    w_q_hbm,
    w_kv_hbm,
    w_o_hbm,
    cache_hbm,
    length_hbm,
    moe_gain_hbm,
    ids_hbm,
    gates_hbm,
    w_gu_hbm,
    w_down_hbm,
    out_ref,
    attn_gain,
    q_gain,
    key_gain,
    w_q,
    w_kv,
    w_o,
    cache,
    length,
    moe_gain,
    ids,
    gates,
    w_gu,
    w_down,
    features,
    heads_out,
    heads_in,
    mixed_out,
    mixed_in,
    mixed_f,
    rows_out,
    rows_in,
    rows_f,
    expert_rows,
    expert_squares,
    pairs_out,
    pairs_own,
    pairs_in,
    hidden_out,
    hidden_in,
    results_f,
    results_out,
    results_in,
    load_sem,
    et_send,
    et_recv,
    stream_send,
    stream_recv,
):
    me_s = lax.axis_index("stream")
    me = lax.axis_index("et")
    tokens = res_hbm.shape[0]
    local = tokens // n_et
    head_dim = q_gain_hbm.shape[1]
    own_heads = w_q_hbm.shape[1] // head_dim
    n_heads = own_heads * n_et
    kv_heads = n_et // 2
    group = n_heads // kv_heads
    width = res_hbm.shape[1] * n_et
    n_local = w_gu_hbm.shape[0]
    slots = n_stream * n_local * CAP
    scale = head_dim**-0.5

    loads = {}
    for name, source, target in (
        ("own", res_hbm, features.at[me]),
        ("length", length_hbm, length),
        ("attn_gain", attn_gain_hbm, attn_gain),
        ("q_gain", q_gain_hbm, q_gain),
        ("key_gain", key_gain_hbm, key_gain),
        ("ids", ids_hbm, ids),
        ("gates", gates_hbm, gates),
        ("moe_gain", moe_gain_hbm, moe_gain),
        ("w_q", w_q_hbm, w_q),
        ("w_kv", w_kv_hbm, w_kv),
        ("cache", cache_hbm, cache),
        ("w_o", w_o_hbm, w_o),
        ("w_gu", w_gu_hbm, w_gu),
        ("w_down", w_down_hbm, w_down),
    ):
        loads[name] = pltpu.make_async_copy(source, target, load_sem.at[len(loads)])
        loads[name].start()

    def et_peer(step):
        return lax.rem(me + step, n_et)

    def stream_peer(step):
        return lax.rem(me_s + step, n_stream)

    def far_first():
        if n_stream % 4:
            return [stream_peer(i) for i in range(1, n_stream)]
        deep = n_stream // 4
        y, z, core = lax.div(me_s, 2 * deep), lax.rem(lax.div(me_s, 2), deep), lax.rem(me_s, 2)
        away = sorted(range(deep), key=lambda i: -min(i, deep - i))
        return [
            lax.rem(y + dy, 2) * (2 * deep) + lax.rem(z + dz, deep) * 2 + lax.rem(core + dc, 2)
            for dz in away
            for dy in (1, 0)
            for dc in (1, 0)
            if dz or dy or dc
        ]

    def et_copy(exchange, source, target, peer):
        return pltpu.make_async_remote_copy(
            src_ref=source,
            dst_ref=target,
            send_sem=et_send.at[exchange, peer],
            recv_sem=et_recv.at[exchange, me],
            device_id=(me_s, peer),
            device_id_type=MESH,
        )

    def et_arrival(exchange, source, target, peer):
        return pltpu.make_async_remote_copy(
            src_ref=source,
            dst_ref=target,
            send_sem=et_send.at[exchange, peer],
            recv_sem=et_recv.at[exchange, peer],
            device_id=(me_s, peer),
            device_id_type=MESH,
        )

    def stream_copy(exchange, source, target, peer):
        return pltpu.make_async_remote_copy(
            src_ref=source,
            dst_ref=target,
            send_sem=stream_send.at[exchange, peer],
            recv_sem=stream_recv.at[exchange, me_s],
            device_id=(peer, me),
            device_id_type=MESH,
        )

    def stream_arrival(exchange, source, target, peer):
        return pltpu.make_async_remote_copy(
            src_ref=source,
            dst_ref=target,
            send_sem=stream_send.at[exchange, peer],
            recv_sem=stream_recv.at[exchange, peer],
            device_id=(peer, me),
            device_id_type=MESH,
        )

    def loop(n, body):
        def step(i, carry):
            body(i)
            return carry

        lax.fori_loop(1, n, step, 0)

    barrier = pltpu.get_barrier_semaphore()
    loop(
        n_et,
        lambda i: pl.semaphore_signal(
            barrier, inc=1, device_id=(me_s, et_peer(i)), device_id_type=MESH
        ),
    )
    loop(
        n_stream,
        lambda i: pl.semaphore_signal(
            barrier, inc=1, device_id=(stream_peer(i), me), device_id_type=MESH
        ),
    )
    pl.semaphore_wait(barrier, n_et + n_stream - 2)

    loop(
        n_et,
        lambda i: et_copy(FEATURES, res_hbm, features.at[me], et_peer(i)).start(),
    )

    loads["length"].wait()
    lengths = jnp.broadcast_to(length[...], (tokens, tokens)).astype(F32)
    diagonal = iota((tokens, tokens), 0) == iota((tokens, tokens), 1)
    positions = jnp.sum(jnp.where(diagonal, lengths, 0.0), axis=1, keepdims=True)
    half = head_dim // 2
    lane = iota((tokens, head_dim), 1)
    steps = jnp.where(lane < half, lane, lane - half).astype(F32)
    angle = positions * jnp.exp(steps * (-2.0 * math.log(ROPE_BASE) / head_dim))
    cosine = jnp.cos(angle)
    sine = jnp.where(lane < half, -jnp.sin(angle), jnp.sin(angle))

    pad = 16
    row = iota((n_et * pad, LANES), 0)
    col = iota((n_et * pad, LANES), 1)
    peer_of, at = lax.div(row, pad), lax.rem(row, pad)
    n_q = local * own_heads
    picked = jnp.where(
        at < n_q,
        lax.rem(at, own_heads) * tokens + peer_of * local + lax.div(at, own_heads),
        jnp.where(
            at < n_q + local, own_heads * tokens + peer_of * local + at - n_q, -1
        ),
    )
    order_out = jnp.where(col == picked, 1.0, 0.0).astype(BF16)

    per = local * n_heads
    row = iota((3 * per, n_et * pad), 0)
    col = iota((3 * per, n_et * pad), 1)
    kind, at = lax.div(row, per), lax.rem(row, per)
    token, head = lax.div(at, n_heads), lax.rem(at, n_heads)
    picked = jnp.where(
        kind == 0,
        lax.div(head, own_heads) * pad + token * own_heads + lax.rem(head, own_heads),
        (lax.div(head, group) + jnp.where(kind == 2, kv_heads, 0)) * pad + n_q + token,
    )
    order_in = jnp.where(col == picked, 1.0, 0.0).astype(BF16)

    loads["ids"].wait()
    loads["gates"].wait()
    at = iota((slots, tokens), 0)
    place = lax.rem(at, n_local * CAP)
    expert = lax.div(at, n_local * CAP) * n_local + lax.rem(place, n_local)
    which = lax.div(place, n_local)
    gate = gates[...]
    gate = gate / jnp.sum(gate, axis=0, keepdims=True)
    named = jnp.zeros((slots, tokens), F32)
    weight = jnp.zeros((slots, tokens), F32)
    for k in range(ids_hbm.shape[0]):
        hit = expert == ids[k : k + 1, :]
        named = jnp.where(hit, 1.0, named)
        weight = jnp.where(hit, gate[k : k + 1, :], weight)
    before = jnp.where(
        iota((tokens, tokens), 0) < iota((tokens, tokens), 1), 1.0, 0.0
    ).astype(BF16)
    earlier = dot(named.astype(BF16), before)
    placed = jnp.where(earlier == which.astype(F32), named, 0.0)
    mixing = placed * weight
    placed = placed.astype(BF16)
    mixing_high = mixing.astype(BF16)
    mixing_low = (mixing - mixing_high.astype(F32)).astype(BF16)

    loads["own"].wait()
    loads["attn_gain"].wait()
    loop(
        n_et,
        lambda i: et_arrival(
            FEATURES, res_hbm, features.at[et_peer(i)], et_peer(i)
        ).wait_recv(),
    )
    full = jnp.concatenate([features[i].astype(F32) for i in range(n_et)], axis=1)
    gain = attn_gain[...].astype(F32)
    gain = jnp.concatenate([gain[i : i + 1] for i in range(gain.shape[0])], axis=1)
    normed = (
        full
        * lax.rsqrt(jnp.sum(full * full, axis=1, keepdims=True) * (1.0 / width) + EPS)
        * gain
    ).astype(BF16)

    def rotated(v, g):
        v = v * lax.rsqrt(jnp.mean(v * v, axis=1, keepdims=True) + EPS) * g
        return v * cosine + pltpu.roll(v, half, 1) * sine

    loads["q_gain"].wait()
    loads["key_gain"].wait()
    loads["w_q"].wait()
    query = dot(normed, w_q[...])
    loads["w_kv"].wait()
    key_value = dot(normed, w_kv[...])
    query_gain = q_gain[...].astype(F32)
    made = [
        rotated(query[:, i * head_dim : (i + 1) * head_dim], query_gain)
        for i in range(own_heads)
    ]
    made.append(
        jnp.where(me < kv_heads, rotated(key_value, key_gain[...].astype(F32)), key_value)
    )
    made.append(jnp.zeros((LANES - (own_heads + 1) * tokens, head_dim), F32))
    made = jnp.concatenate(made, axis=0).astype(BF16)
    heads_out[...] = dot(order_out, made).astype(BF16).reshape(heads_out.shape)
    heads_in[me] = heads_out[me]
    loop(
        n_et,
        lambda i: et_copy(
            HEADS, heads_out.at[et_peer(i)], heads_in.at[me], et_peer(i)
        ).start(),
    )

    rows_of = cache_hbm.shape[0] // local
    piece = rows_of
    own_lane = iota((1, tokens), 1)
    lengths = length[...].astype(F32)
    loads["cache"].wait()
    loop(
        n_et,
        lambda i: et_arrival(
            HEADS, heads_out.at[et_peer(i)], heads_in.at[et_peer(i)], et_peer(i)
        ).wait_recv(),
    )
    ordered = dot(order_in, heads_in[...].reshape(n_et * pad, head_dim))
    for t in range(local):
        q = ordered[t * n_heads : (t + 1) * n_heads]
        new_key = ordered[per + t * n_heads : per + (t + 1) * n_heads]
        new_value = ordered[2 * per + t * n_heads : 2 * per + (t + 1) * n_heads]
        fresh = jnp.exp(jnp.sum(q * new_key, axis=1, keepdims=True) * scale)
        limit = (
            jnp.sum(
                jnp.where(own_lane == me * local + t, lengths, 0.0),
                axis=1,
                keepdims=True,
            )
            * float(2 * kv_heads)
        ).astype(jnp.int32)
        q = q.astype(BF16)
        column = iota((n_heads, piece), 1)
        aligned = lax.rem(column, 2 * kv_heads) == 2 * lax.div(
            iota((n_heads, piece), 0), group
        )
        total = fresh
        summed = fresh * new_value
        for p in range(rows_of // piece):
            block = cache[t * rows_of + p * piece : t * rows_of + (p + 1) * piece, :]
            score = dot_nt(q, block)
            live = aligned & (column < limit - p * piece)
            weights = jnp.where(live, jnp.exp(score * scale), 0.0)
            total = total + jnp.sum(weights, axis=1, keepdims=True)
            moved = jnp.concatenate(
                [
                    pltpu.roll(weights[:, i : i + LANES], 1, 1)
                    for i in range(0, piece, LANES)
                ],
                axis=1,
            )
            summed = summed + dot(moved.astype(BF16), block)
        mixed_out[t * n_heads : (t + 1) * n_heads, :] = (summed / total).astype(BF16)
    mixed_in[me] = mixed_out[...]
    loop(
        n_et,
        lambda i: et_copy(MIXED, mixed_out, mixed_in.at[me], et_peer(i)).start(),
    )

    loads["w_o"].wait()
    loop(
        n_et,
        lambda i: et_arrival(
            MIXED, mixed_out, mixed_in.at[et_peer(i)], et_peer(i)
        ).wait_recv(),
    )
    mixed_f[...] = mixed_in[...].reshape(tokens * n_heads, head_dim).astype(F32)
    attended = jnp.concatenate(
        [mixed_f[pl.ds(h, tokens, stride=n_heads), :] for h in range(n_heads)], axis=1
    ).astype(BF16)
    resid = (features[me].astype(F32) + dot(attended, w_o[...])).astype(BF16)

    sent = dot(placed, resid)
    sent = sent.reshape(n_stream, n_local * CAP, 2 * LANES)
    rows_out[...] = jnp.concatenate(
        [sent[:, :, :LANES], sent[:, :, LANES:]], axis=1
    ).astype(BF16)
    rows_in[me_s] = rows_out[me_s]
    for peer in far_first():
        stream_copy(OUTWARD, rows_out.at[peer], rows_in.at[me_s], peer).start()
    loads["moe_gain"].wait()
    gain = moe_gain[...].astype(F32)
    gain = jnp.concatenate([gain[0:1], gain[1:2]], axis=1)
    loads["w_gu"].wait()
    loop(
        n_stream,
        lambda i: stream_arrival(
            OUTWARD, rows_out.at[stream_peer(i)], rows_in.at[stream_peer(i)], stream_peer(i)
        ).wait_recv(),
    )
    chunk = 2 * n_local * CAP
    rows_f[...] = rows_in[...].reshape(n_stream * chunk, LANES).astype(F32)
    for j in range(n_local):
        taken = []
        for c in range(CAP):
            taken.append(
                jnp.concatenate(
                    [
                        rows_f[
                            pl.ds(h * n_local * CAP + c * n_local + j, n_stream, stride=chunk), :
                        ]
                        for h in range(2)
                    ],
                    axis=1,
                )
            )
        taken = jnp.concatenate(taken, axis=0)
        squares = jnp.sum(taken * taken, axis=1, keepdims=True)
        high = squares.astype(BF16).astype(F32)
        expert_squares[j] = jnp.where(
            iota((CAP * n_stream, LANES), 1) < LANES // 2, high, squares - high
        )
        expert_rows[j] = (taken * gain).astype(BF16)

    hidden_width = w_down_hbm.shape[1]
    for i in range(n_local):
        j = lax.rem(lax.div(me, CAP) + (2, 1, 3, 0)[i], n_local)
        taken = expert_rows[j]
        products = jnp.concatenate(
            [dot(taken, w_gu[j, 0]), dot(taken, w_gu[j, 1]), expert_squares[j]], axis=1
        )
        pairs_out[i] = products.astype(BF16).reshape(pairs_out.shape[1:])
        if i < n_local - 1:
            for c in range(CAP):
                et_copy(
                    PAIRS, pairs_out.at[i, c], pairs_in.at[me], CAP * j + c
                ).start()
        else:
            pairs_own[...] = products.reshape(pairs_own.shape)
            c = 1 - lax.rem(me, CAP)
            et_copy(PAIRS, pairs_out.at[i, c], pairs_in.at[me], CAP * j + c).start()
    pair = pairs_own[lax.rem(me, CAP)]
    for i in range(1, n_et):
        et_arrival(
            PAIRS, pairs_out.at[0, 0], pairs_in.at[et_peer(i)], et_peer(i)
        ).wait_recv()
        pair = pair + pairs_in[et_peer(i)].astype(F32)
    squares = jnp.sum(pair[:, 2 * hidden_width :], axis=1, keepdims=True) * (
        2.0 / LANES / width
    )
    level = lax.rsqrt(squares + EPS)
    first = pair[:, :hidden_width] * level
    second = pair[:, hidden_width : 2 * hidden_width] * level
    hidden_out[...] = (first / (1.0 + jnp.exp(-first)) * second).astype(BF16)
    hidden_in[me] = hidden_out[...]
    loop(
        n_et,
        lambda i: et_copy(HIDDEN, hidden_out, hidden_in.at[me], et_peer(i)).start(),
    )

    loads["w_down"].wait()
    loop(
        n_et,
        lambda i: et_arrival(
            HIDDEN, hidden_out, hidden_in.at[et_peer(i)], et_peer(i)
        ).wait_recv(),
    )
    for j in range(n_local):
        hidden = hidden_in[CAP * j : CAP * (j + 1)].reshape(CAP * n_stream, hidden_width)
        result = dot(hidden, w_down[j])
        for c in range(CAP):
            for h in range(2):
                results_f[
                    pl.ds(h * n_local * CAP + c * n_local + j, n_stream, stride=chunk), :
                ] = result[c * n_stream : (c + 1) * n_stream, h * LANES : (h + 1) * LANES]
    results_out[...] = results_f[...].astype(BF16).reshape(results_out.shape)
    results_in[me_s] = results_out[me_s]
    for peer in far_first():
        stream_copy(HOME, results_out.at[peer], results_in.at[me_s], peer).start()
    loop(
        n_stream,
        lambda i: stream_arrival(
            HOME, results_out.at[stream_peer(i)], results_in.at[stream_peer(i)], stream_peer(i)
        ).wait_recv(),
    )
    returned = results_in[...].astype(F32)
    returned = (
        jnp.concatenate(
            [returned[:, : n_local * CAP], returned[:, n_local * CAP :]], axis=2
        )
        .reshape(slots, 2 * LANES)
        .astype(BF16)
    )
    routed = dot_tn(mixing_high, returned) + dot_tn(mixing_low, returned)
    out_ref[...] = (resid.astype(F32) + routed).astype(BF16)

    def sent_et(exchange, source, target):
        loop(
            n_et,
            lambda i: et_copy(exchange, source, target, et_peer(i)).wait_send(),
        )

    sent_et(FEATURES, res_hbm, features.at[me])
    sent_et(HEADS, heads_out.at[0], heads_in.at[me])
    sent_et(MIXED, mixed_out, mixed_in.at[me])
    sent_et(PAIRS, pairs_out.at[0, 0], pairs_in.at[me])
    sent_et(HIDDEN, hidden_out, hidden_in.at[me])
    for exchange, source, target in (
        (OUTWARD, rows_out, rows_in),
        (HOME, results_out, results_in),
    ):
        loop(
            n_stream,
            lambda i: stream_copy(
                exchange, source.at[stream_peer(i)], target.at[me_s], stream_peer(i)
            ).wait_send(),
        )


def on_device(
    n_stream,
    n_et,
    residual_in,
    attn_gain,
    q_gain,
    key_norm_gain,
    w_q,
    key_value_weight,
    w_o,
    key_value_cache,
    cache_length,
    moe_gain,
    route_ids,
    route_gates,
    w_gate_up,
    w_down,
):
    tokens, features = residual_in.shape
    head_dim = q_gain.shape[0]
    local, span, _, kv_width = key_value_cache.shape
    kv_heads = kv_width // head_dim
    n_heads = w_q.shape[1] // head_dim * n_et
    n_local = w_gate_up.shape[0]
    hidden = w_down.shape[1]
    cache = (
        key_value_cache.reshape(local, span, 2, kv_heads, head_dim)
        .transpose(0, 1, 3, 2, 4)
        .reshape(local * span * kv_heads * 2, head_dim)
    )
    args = (
        residual_in,
        attn_gain.reshape(-1, LANES),
        q_gain.reshape(1, -1),
        key_norm_gain.reshape(1, -1),
        w_q,
        key_value_weight,
        w_o,
        cache,
        cache_length.reshape(1, -1),
        moe_gain.reshape(-1, LANES),
        route_ids.T,
        route_gates.T,
        w_gate_up,
        w_down,
    )
    chunk = 2 * n_local * CAP
    vmem = pltpu.VMEM
    row_blocks = (n_stream, chunk, LANES)
    flat_rows = (n_stream * chunk, LANES)
    pair_width = 2 * hidden + LANES
    scratch = [vmem(a.shape, a.dtype) for a in args[1:]] + [
        vmem((n_et, tokens, features), BF16),
        vmem((n_et, 16, head_dim), BF16),
        vmem((n_et, 16, head_dim), BF16),
        vmem((local * n_heads, head_dim), BF16),
        vmem((n_et, local * n_heads, head_dim), BF16),
        vmem((tokens * n_heads, head_dim), F32),
        vmem(row_blocks, BF16),
        vmem(row_blocks, BF16),
        vmem(flat_rows, F32),
        vmem((n_local, CAP * n_stream, features), BF16),
        vmem((n_local, CAP * n_stream, LANES), F32),
        vmem((n_local, CAP, n_stream, pair_width), BF16),
        vmem((CAP, n_stream, pair_width), F32),
        vmem((n_et, n_stream, pair_width), BF16),
        vmem((n_stream, hidden), BF16),
        vmem((n_et, n_stream, hidden), BF16),
        vmem(flat_rows, F32),
        vmem(row_blocks, BF16),
        vmem(row_blocks, BF16),
        pltpu.SemaphoreType.DMA((len(args),)),
        pltpu.SemaphoreType.DMA((5, n_et)),
        pltpu.SemaphoreType.DMA((5, n_et)),
        pltpu.SemaphoreType.DMA((2, n_stream)),
        pltpu.SemaphoreType.DMA((2, n_stream)),
    ]
    return pl.pallas_call(
        functools.partial(kernel, n_stream, n_et),
        out_shape=jax.ShapeDtypeStruct(residual_in.shape, residual_in.dtype),
        in_specs=[pl.BlockSpec(memory_space=pl.ANY)] * len(args),
        out_specs=pl.BlockSpec(memory_space=pltpu.VMEM),
        scratch_shapes=scratch,
        compiler_params=pltpu.CompilerParams(
            collective_id=0, has_side_effects=True, vmem_limit_bytes=56 * 1024 * 1024
        ),
    )(*args)


def solution(mesh):
    placed = (
        P("stream", "et"),
        P(),
        P(),
        P(),
        P(None, "et"),
        P(None, "et"),
        P(None, "et"),
        P(("stream", "et"), None, None, None),
        P("stream"),
        P("et"),
        P("stream", None),
        P("stream", None),
        P("stream", None, "et", None),
        P("stream", None, "et"),
    )
    return jax.shard_map(
        functools.partial(on_device, mesh.shape["stream"], mesh.shape["et"]),
        mesh=mesh,
        in_specs=placed,
        out_specs=P("stream", "et"),
        check_vma=False,
    )
```

```python
import functools
import math

import jax
import jax.numpy as jnp
from jax import lax
from jax.experimental import pallas as pl
from jax.experimental.pallas import tpu as pltpu
from jax.sharding import PartitionSpec as P

EPS = 1e-06
ROPE_BASE = 1000000.0
CAP = 2
LANES = 128
MESH = pl.DeviceIdType.MESH
F32 = jnp.float32
BF16 = jnp.bfloat16

FEATURES, HEADS, MIXED, PAIRS, HIDDEN = range(5)
OUTWARD, HOME = range(2)


def iota(shape, dim):
    return lax.broadcasted_iota(jnp.int32, shape, dim)


def dot(a, b):
    return jnp.dot(a, b, preferred_element_type=F32)


def dot_nt(a, b):
    return lax.dot_general(a, b, (((1,), (1,)), ((), ())), preferred_element_type=F32)


def dot_tn(a, b):
    return lax.dot_general(a, b, (((0,), (0,)), ((), ())), preferred_element_type=F32)


def kernel(
    n_stream,
    n_et,
    res_hbm,
    attn_gain_hbm,
    q_gain_hbm,
    key_gain_hbm,
    w_q_hbm,
    w_kv_hbm,
    w_o_hbm,
    cache_hbm,
    length_hbm,
    moe_gain_hbm,
    ids_hbm,
    gates_hbm,
    w_gu_hbm,
    w_down_hbm,
    out_ref,
    attn_gain,
    q_gain,
    key_gain,
    w_q,
    w_kv,
    w_o,
    cache,
    length,
    moe_gain,
    ids,
    gates,
    w_gu,
    w_down,
    features,
    heads_out,
    heads_in,
    mixed_out,
    mixed_in,
    mixed_f,
    rows_out,
    rows_in,
    rows_f,
    expert_rows,
    expert_squares,
    pairs_out,
    pairs_own,
    pairs_in,
    hidden_out,
    hidden_in,
    results_f,
    results_out,
    results_in,
    load_sem,
    et_send,
    et_recv,
    stream_send,
    stream_recv,
    known,
):
    me_s = lax.axis_index("stream")
    me = lax.axis_index("et")
    tokens = res_hbm.shape[0]
    local = tokens // n_et
    head_dim = q_gain_hbm.shape[1]
    own_heads = w_q_hbm.shape[1] // head_dim
    n_heads = own_heads * n_et
    kv_heads = n_et // 2
    group = n_heads // kv_heads
    width = res_hbm.shape[1] * n_et
    n_local = w_gu_hbm.shape[0]
    slots = n_stream * n_local * CAP
    scale = head_dim**-0.5

    def et_peer(step):
        return lax.rem(me + step, n_et)

    def stream_peer(step):
        return lax.rem(me_s + step, n_stream)

    n_y, n_z, n_core = (2, n_stream // 4, 2) if n_stream % 4 == 0 else (1, 1, n_stream)
    y, z, core = lax.div(me_s, n_z * n_core), lax.rem(lax.div(me_s, n_core), n_z), lax.rem(me_s, n_core)

    def stream_at(dy, dz, dc):
        return (
            lax.rem(y + dy, n_y) * (n_z * n_core)
            + lax.rem(z + dz, n_z) * n_core
            + lax.rem(core + dc, n_core)
        )

    across = [(dy, 0, dc) for dy in range(n_y) for dc in range(n_core) if dy or dc]

    def along(reach):
        return [(0, dz, 0) for dz in sorted({reach % n_z, -reach % n_z} - {0})]

    rounds = []
    reach = 1
    while reach < n_z // 2:
        rounds.append(along(reach))
        reach *= 2
    rounds.append(across)

    def tell(number):
        for away in rounds[number] if number < len(rounds) else ():
            pl.semaphore_signal(
                known.at[number],
                inc=1,
                device_id=(stream_at(*away), me),
                device_id_type=MESH,
            )

    def hear(number):
        if number < len(rounds):
            pl.semaphore_wait(known.at[number], len(rounds[number]))

    far_first = [
        stream_at(dy, dz, dc)
        for dz in sorted(range(n_z), key=lambda i: -min(i, n_z - i))
        for dy in reversed(range(n_y))
        for dc in reversed(range(n_core))
        if dy or dz or dc
    ]

    def et_copy(exchange, source, target, peer):
        return pltpu.make_async_remote_copy(
            src_ref=source,
            dst_ref=target,
            send_sem=et_send.at[exchange, peer],
            recv_sem=et_recv.at[exchange, me],
            device_id=(me_s, peer),
            device_id_type=MESH,
        )

    def et_arrival(exchange, source, target, peer):
        return pltpu.make_async_remote_copy(
            src_ref=source,
            dst_ref=target,
            send_sem=et_send.at[exchange, peer],
            recv_sem=et_recv.at[exchange, peer],
            device_id=(me_s, peer),
            device_id_type=MESH,
        )

    def stream_copy(exchange, source, target, peer):
        return pltpu.make_async_remote_copy(
            src_ref=source,
            dst_ref=target,
            send_sem=stream_send.at[exchange, peer],
            recv_sem=stream_recv.at[exchange, me_s],
            device_id=(peer, me),
            device_id_type=MESH,
        )

    def stream_arrival(exchange, source, target, peer):
        return pltpu.make_async_remote_copy(
            src_ref=source,
            dst_ref=target,
            send_sem=stream_send.at[exchange, peer],
            recv_sem=stream_recv.at[exchange, peer],
            device_id=(peer, me),
            device_id_type=MESH,
        )

    def loop(n, body):
        def step(i, carry):
            body(i)
            return carry

        lax.fori_loop(1, n, step, 0)

    barrier = pltpu.get_barrier_semaphore()
    greeted = [(me_s, et_peer(i)) for i in range(1, n_et)]
    greeted += [(stream_at(*away), me) for away in along(1) + across]
    for device in greeted:
        pl.semaphore_signal(barrier, inc=1, device_id=device, device_id_type=MESH)

    loads = {}
    for name, source, target in (
        ("own", res_hbm, features.at[me]),
        ("length", length_hbm, length),
        ("attn_gain", attn_gain_hbm, attn_gain),
        ("q_gain", q_gain_hbm, q_gain),
        ("key_gain", key_gain_hbm, key_gain),
        ("ids", ids_hbm, ids),
        ("gates", gates_hbm, gates),
        ("moe_gain", moe_gain_hbm, moe_gain),
        ("w_q", w_q_hbm, w_q),
        ("w_kv", w_kv_hbm, w_kv),
        ("cache", cache_hbm, cache),
        ("w_o", w_o_hbm, w_o),
        ("w_gu", w_gu_hbm, w_gu),
        ("w_down", w_down_hbm, w_down),
    ):
        loads[name] = pltpu.make_async_copy(source, target, load_sem.at[len(loads)])
        loads[name].start()

    pl.semaphore_wait(barrier, len(greeted))

    loop(
        n_et,
        lambda i: et_copy(FEATURES, res_hbm, features.at[me], et_peer(i)).start(),
    )
    tell(0)

    loads["length"].wait()
    lengths = jnp.broadcast_to(length[...], (tokens, tokens)).astype(F32)
    diagonal = iota((tokens, tokens), 0) == iota((tokens, tokens), 1)
    positions = jnp.sum(jnp.where(diagonal, lengths, 0.0), axis=1, keepdims=True)
    half = head_dim // 2
    lane = iota((tokens, head_dim), 1)
    steps = jnp.where(lane < half, lane, lane - half).astype(F32)
    angle = positions * jnp.exp(steps * (-2.0 * math.log(ROPE_BASE) / head_dim))
    cosine = jnp.cos(angle)
    sine = jnp.where(lane < half, -jnp.sin(angle), jnp.sin(angle))

    pad = 16
    row = iota((n_et * pad, LANES), 0)
    col = iota((n_et * pad, LANES), 1)
    peer_of, at = lax.div(row, pad), lax.rem(row, pad)
    n_q = local * own_heads
    picked = jnp.where(
        at < n_q,
        lax.rem(at, own_heads) * tokens + peer_of * local + lax.div(at, own_heads),
        jnp.where(
            at < n_q + local, own_heads * tokens + peer_of * local + at - n_q, -1
        ),
    )
    order_out = jnp.where(col == picked, 1.0, 0.0).astype(BF16)

    per = local * n_heads
    row = iota((3 * per, n_et * pad), 0)
    col = iota((3 * per, n_et * pad), 1)
    kind, at = lax.div(row, per), lax.rem(row, per)
    token, head = lax.div(at, n_heads), lax.rem(at, n_heads)
    picked = jnp.where(
        kind == 0,
        lax.div(head, own_heads) * pad + token * own_heads + lax.rem(head, own_heads),
        (lax.div(head, group) + jnp.where(kind == 2, kv_heads, 0)) * pad + n_q + token,
    )
    order_in = jnp.where(col == picked, 1.0, 0.0).astype(BF16)

    loads["ids"].wait()
    loads["gates"].wait()
    at = iota((slots, tokens), 0)
    place = lax.rem(at, n_local * CAP)
    expert = lax.div(at, n_local * CAP) * n_local + lax.rem(place, n_local)
    which = lax.div(place, n_local)
    gate = gates[...]
    gate = gate / jnp.sum(gate, axis=0, keepdims=True)
    named = jnp.zeros((slots, tokens), F32)
    weight = jnp.zeros((slots, tokens), F32)
    for k in range(ids_hbm.shape[0]):
        hit = expert == ids[k : k + 1, :]
        named = jnp.where(hit, 1.0, named)
        weight = jnp.where(hit, gate[k : k + 1, :], weight)
    before = jnp.where(
        iota((tokens, tokens), 0) < iota((tokens, tokens), 1), 1.0, 0.0
    ).astype(BF16)
    earlier = dot(named.astype(BF16), before)
    placed = jnp.where(earlier == which.astype(F32), named, 0.0)
    mixing = placed * weight
    placed = placed.astype(BF16)
    mixing_high = mixing.astype(BF16)
    mixing_low = (mixing - mixing_high.astype(F32)).astype(BF16)

    loads["own"].wait()
    loads["attn_gain"].wait()
    loop(
        n_et,
        lambda i: et_arrival(
            FEATURES, res_hbm, features.at[et_peer(i)], et_peer(i)
        ).wait_recv(),
    )
    full = jnp.concatenate([features[i].astype(F32) for i in range(n_et)], axis=1)
    gain = attn_gain[...].astype(F32)
    gain = jnp.concatenate([gain[i : i + 1] for i in range(gain.shape[0])], axis=1)
    normed = (
        full
        * lax.rsqrt(jnp.sum(full * full, axis=1, keepdims=True) * (1.0 / width) + EPS)
        * gain
    ).astype(BF16)

    def rotated(v, g):
        v = v * lax.rsqrt(jnp.mean(v * v, axis=1, keepdims=True) + EPS) * g
        return v * cosine + pltpu.roll(v, half, 1) * sine

    loads["q_gain"].wait()
    loads["key_gain"].wait()
    loads["w_q"].wait()
    query = dot(normed, w_q[...])
    loads["w_kv"].wait()
    key_value = dot(normed, w_kv[...])
    query_gain = q_gain[...].astype(F32)
    made = [
        rotated(query[:, i * head_dim : (i + 1) * head_dim], query_gain)
        for i in range(own_heads)
    ]
    made.append(
        jnp.where(me < kv_heads, rotated(key_value, key_gain[...].astype(F32)), key_value)
    )
    made.append(jnp.zeros((LANES - (own_heads + 1) * tokens, head_dim), F32))
    made = jnp.concatenate(made, axis=0).astype(BF16)
    heads_out[...] = dot(order_out, made).astype(BF16).reshape(heads_out.shape)
    heads_in[me] = heads_out[me]
    loop(
        n_et,
        lambda i: et_copy(
            HEADS, heads_out.at[et_peer(i)], heads_in.at[me], et_peer(i)
        ).start(),
    )
    hear(0)
    tell(1)

    rows_of = cache_hbm.shape[0] // local
    piece = rows_of
    own_lane = iota((1, tokens), 1)
    lengths = length[...].astype(F32)
    loads["cache"].wait()
    loop(
        n_et,
        lambda i: et_arrival(
            HEADS, heads_out.at[et_peer(i)], heads_in.at[et_peer(i)], et_peer(i)
        ).wait_recv(),
    )
    ordered = dot(order_in, heads_in[...].reshape(n_et * pad, head_dim))
    for t in range(local):
        q = ordered[t * n_heads : (t + 1) * n_heads]
        new_key = ordered[per + t * n_heads : per + (t + 1) * n_heads]
        new_value = ordered[2 * per + t * n_heads : 2 * per + (t + 1) * n_heads]
        fresh = jnp.exp(jnp.sum(q * new_key, axis=1, keepdims=True) * scale)
        limit = (
            jnp.sum(
                jnp.where(own_lane == me * local + t, lengths, 0.0),
                axis=1,
                keepdims=True,
            )
            * float(2 * kv_heads)
        ).astype(jnp.int32)
        q = q.astype(BF16)
        column = iota((n_heads, piece), 1)
        aligned = lax.rem(column, 2 * kv_heads) == 2 * lax.div(
            iota((n_heads, piece), 0), group
        )
        total = fresh
        summed = fresh * new_value
        for p in range(rows_of // piece):
            block = cache[t * rows_of + p * piece : t * rows_of + (p + 1) * piece, :]
            score = dot_nt(q, block)
            live = aligned & (column < limit - p * piece)
            weights = jnp.where(live, jnp.exp(score * scale), 0.0)
            total = total + jnp.sum(weights, axis=1, keepdims=True)
            moved = jnp.concatenate(
                [
                    pltpu.roll(weights[:, i : i + LANES], 1, 1)
                    for i in range(0, piece, LANES)
                ],
                axis=1,
            )
            summed = summed + dot(moved.astype(BF16), block)
        mixed_out[t * n_heads : (t + 1) * n_heads, :] = (summed / total).astype(BF16)
    mixed_in[me] = mixed_out[...]
    loop(
        n_et,
        lambda i: et_copy(MIXED, mixed_out, mixed_in.at[me], et_peer(i)).start(),
    )
    hear(1)
    tell(2)

    loads["w_o"].wait()
    loop(
        n_et,
        lambda i: et_arrival(
            MIXED, mixed_out, mixed_in.at[et_peer(i)], et_peer(i)
        ).wait_recv(),
    )
    mixed_f[...] = mixed_in[...].reshape(tokens * n_heads, head_dim).astype(F32)
    attended = jnp.concatenate(
        [mixed_f[pl.ds(h, tokens, stride=n_heads), :] for h in range(n_heads)], axis=1
    ).astype(BF16)
    resid = (features[me].astype(F32) + dot(attended, w_o[...])).astype(BF16)

    sent = dot(placed, resid)
    sent = sent.reshape(n_stream, n_local * CAP, 2 * LANES)
    rows_out[...] = jnp.concatenate(
        [sent[:, :, :LANES], sent[:, :, LANES:]], axis=1
    ).astype(BF16)
    rows_in[me_s] = rows_out[me_s]
    hear(2)
    for peer in far_first:
        stream_copy(OUTWARD, rows_out.at[peer], rows_in.at[me_s], peer).start()
    loads["moe_gain"].wait()
    gain = moe_gain[...].astype(F32)
    gain = jnp.concatenate([gain[0:1], gain[1:2]], axis=1)
    loads["w_gu"].wait()
    loop(
        n_stream,
        lambda i: stream_arrival(
            OUTWARD, rows_out.at[stream_peer(i)], rows_in.at[stream_peer(i)], stream_peer(i)
        ).wait_recv(),
    )
    chunk = 2 * n_local * CAP
    rows_f[...] = rows_in[...].reshape(n_stream * chunk, LANES).astype(F32)
    for j in range(n_local):
        taken = []
        for c in range(CAP):
            taken.append(
                jnp.concatenate(
                    [
                        rows_f[
                            pl.ds(h * n_local * CAP + c * n_local + j, n_stream, stride=chunk), :
                        ]
                        for h in range(2)
                    ],
                    axis=1,
                )
            )
        taken = jnp.concatenate(taken, axis=0)
        squares = jnp.sum(taken * taken, axis=1, keepdims=True)
        high = squares.astype(BF16).astype(F32)
        expert_squares[j] = jnp.where(
            iota((CAP * n_stream, LANES), 1) < LANES // 2, high, squares - high
        )
        expert_rows[j] = (taken * gain).astype(BF16)

    hidden_width = w_down_hbm.shape[1]
    for i in range(n_local):
        j = lax.rem(lax.div(me, CAP) + (2, 1, 3, 0)[i], n_local)
        taken = expert_rows[j]
        products = jnp.concatenate(
            [dot(taken, w_gu[j, 0]), dot(taken, w_gu[j, 1]), expert_squares[j]], axis=1
        )
        pairs_out[i] = products.astype(BF16).reshape(pairs_out.shape[1:])
        if i < n_local - 1:
            for c in range(CAP):
                et_copy(
                    PAIRS, pairs_out.at[i, c], pairs_in.at[me], CAP * j + c
                ).start()
        else:
            pairs_own[...] = products.reshape(pairs_own.shape)
            c = 1 - lax.rem(me, CAP)
            et_copy(PAIRS, pairs_out.at[i, c], pairs_in.at[me], CAP * j + c).start()
    pair = pairs_own[lax.rem(me, CAP)]
    for i in range(1, n_et):
        et_arrival(
            PAIRS, pairs_out.at[0, 0], pairs_in.at[et_peer(i)], et_peer(i)
        ).wait_recv()
        pair = pair + pairs_in[et_peer(i)].astype(F32)
    squares = jnp.sum(pair[:, 2 * hidden_width :], axis=1, keepdims=True) * (
        2.0 / LANES / width
    )
    level = lax.rsqrt(squares + EPS)
    first = pair[:, :hidden_width] * level
    second = pair[:, hidden_width : 2 * hidden_width] * level
    hidden_out[...] = (first / (1.0 + jnp.exp(-first)) * second).astype(BF16)
    hidden_in[me] = hidden_out[...]
    loop(
        n_et,
        lambda i: et_copy(HIDDEN, hidden_out, hidden_in.at[me], et_peer(i)).start(),
    )

    loads["w_down"].wait()
    loop(
        n_et,
        lambda i: et_arrival(
            HIDDEN, hidden_out, hidden_in.at[et_peer(i)], et_peer(i)
        ).wait_recv(),
    )
    for j in range(n_local):
        hidden = hidden_in[CAP * j : CAP * (j + 1)].reshape(CAP * n_stream, hidden_width)
        result = dot(hidden, w_down[j])
        for c in range(CAP):
            for h in range(2):
                results_f[
                    pl.ds(h * n_local * CAP + c * n_local + j, n_stream, stride=chunk), :
                ] = result[c * n_stream : (c + 1) * n_stream, h * LANES : (h + 1) * LANES]
    results_out[...] = results_f[...].astype(BF16).reshape(results_out.shape)
    results_in[me_s] = results_out[me_s]
    for peer in far_first:
        stream_copy(HOME, results_out.at[peer], results_in.at[me_s], peer).start()
    loop(
        n_stream,
        lambda i: stream_arrival(
            HOME, results_out.at[stream_peer(i)], results_in.at[stream_peer(i)], stream_peer(i)
        ).wait_recv(),
    )
    returned = results_in[...].astype(F32)
    returned = (
        jnp.concatenate(
            [returned[:, : n_local * CAP], returned[:, n_local * CAP :]], axis=2
        )
        .reshape(slots, 2 * LANES)
        .astype(BF16)
    )
    routed = dot_tn(mixing_high, returned) + dot_tn(mixing_low, returned)
    out_ref[...] = (resid.astype(F32) + routed).astype(BF16)

    def sent_et(exchange, source, target):
        loop(
            n_et,
            lambda i: et_copy(exchange, source, target, et_peer(i)).wait_send(),
        )

    sent_et(FEATURES, res_hbm, features.at[me])
    sent_et(HEADS, heads_out.at[0], heads_in.at[me])
    sent_et(MIXED, mixed_out, mixed_in.at[me])
    sent_et(PAIRS, pairs_out.at[0, 0], pairs_in.at[me])
    sent_et(HIDDEN, hidden_out, hidden_in.at[me])
    for exchange, source, target in (
        (OUTWARD, rows_out, rows_in),
        (HOME, results_out, results_in),
    ):
        loop(
            n_stream,
            lambda i: stream_copy(
                exchange, source.at[stream_peer(i)], target.at[me_s], stream_peer(i)
            ).wait_send(),
        )


def on_device(
    n_stream,
    n_et,
    residual_in,
    attn_gain,
    q_gain,
    key_norm_gain,
    w_q,
    key_value_weight,
    w_o,
    key_value_cache,
    cache_length,
    moe_gain,
    route_ids,
    route_gates,
    w_gate_up,
    w_down,
):
    tokens, features = residual_in.shape
    head_dim = q_gain.shape[0]
    local, span, _, kv_width = key_value_cache.shape
    kv_heads = kv_width // head_dim
    n_heads = w_q.shape[1] // head_dim * n_et
    n_local = w_gate_up.shape[0]
    hidden = w_down.shape[1]
    cache = (
        key_value_cache.reshape(local, span, 2, kv_heads, head_dim)
        .transpose(0, 1, 3, 2, 4)
        .reshape(local * span * kv_heads * 2, head_dim)
    )
    args = (
        residual_in,
        attn_gain.reshape(-1, LANES),
        q_gain.reshape(1, -1),
        key_norm_gain.reshape(1, -1),
        w_q,
        key_value_weight,
        w_o,
        cache,
        cache_length.reshape(1, -1),
        moe_gain.reshape(-1, LANES),
        route_ids.T,
        route_gates.T,
        w_gate_up,
        w_down,
    )
    chunk = 2 * n_local * CAP
    vmem = pltpu.VMEM
    row_blocks = (n_stream, chunk, LANES)
    flat_rows = (n_stream * chunk, LANES)
    pair_width = 2 * hidden + LANES
    scratch = [vmem(a.shape, a.dtype) for a in args[1:]] + [
        vmem((n_et, tokens, features), BF16),
        vmem((n_et, 16, head_dim), BF16),
        vmem((n_et, 16, head_dim), BF16),
        vmem((local * n_heads, head_dim), BF16),
        vmem((n_et, local * n_heads, head_dim), BF16),
        vmem((tokens * n_heads, head_dim), F32),
        vmem(row_blocks, BF16),
        vmem(row_blocks, BF16),
        vmem(flat_rows, F32),
        vmem((n_local, CAP * n_stream, features), BF16),
        vmem((n_local, CAP * n_stream, LANES), F32),
        vmem((n_local, CAP, n_stream, pair_width), BF16),
        vmem((CAP, n_stream, pair_width), F32),
        vmem((n_et, n_stream, pair_width), BF16),
        vmem((n_stream, hidden), BF16),
        vmem((n_et, n_stream, hidden), BF16),
        vmem(flat_rows, F32),
        vmem(row_blocks, BF16),
        vmem(row_blocks, BF16),
        pltpu.SemaphoreType.DMA((len(args),)),
        pltpu.SemaphoreType.DMA((5, n_et)),
        pltpu.SemaphoreType.DMA((5, n_et)),
        pltpu.SemaphoreType.DMA((2, n_stream)),
        pltpu.SemaphoreType.DMA((2, n_stream)),
        pltpu.SemaphoreType.REGULAR((3,)),
    ]
    return pl.pallas_call(
        functools.partial(kernel, n_stream, n_et),
        out_shape=jax.ShapeDtypeStruct(residual_in.shape, residual_in.dtype),
        in_specs=[pl.BlockSpec(memory_space=pl.ANY)] * len(args),
        out_specs=pl.BlockSpec(memory_space=pltpu.VMEM),
        scratch_shapes=scratch,
        compiler_params=pltpu.CompilerParams(
            collective_id=0, has_side_effects=True, vmem_limit_bytes=56 * 1024 * 1024
        ),
    )(*args)


def solution(mesh):
    placed = (
        P("stream", "et"),
        P(),
        P(),
        P(),
        P(None, "et"),
        P(None, "et"),
        P(None, "et"),
        P(("stream", "et"), None, None, None),
        P("stream"),
        P("et"),
        P("stream", None),
        P("stream", None),
        P("stream", None, "et", None),
        P("stream", None, "et"),
    )
    return jax.shard_map(
        functools.partial(on_device, mesh.shape["stream"], mesh.shape["et"]),
        mesh=mesh,
        in_specs=placed,
        out_specs=P("stream", "et"),
        check_vma=False,
    )
```

```python
import functools
import math

import jax
import jax.numpy as jnp
from jax import lax
from jax.experimental import pallas as pl
from jax.experimental.pallas import tpu as pltpu
from jax.sharding import PartitionSpec as P

EPS = 1e-06
ROPE_BASE = 1000000.0
CAP = 2
LANES = 128
MESH = pl.DeviceIdType.MESH
F32 = jnp.float32
BF16 = jnp.bfloat16

FEATURES, HEADS, MIXED, PAIRS, HIDDEN = range(5)
OUTWARD, HOME = range(2)


def iota(shape, dim):
    return lax.broadcasted_iota(jnp.int32, shape, dim)


def dot(a, b):
    return jnp.dot(a, b, preferred_element_type=F32)


def dot_nt(a, b):
    return lax.dot_general(a, b, (((1,), (1,)), ((), ())), preferred_element_type=F32)


def dot_tn(a, b):
    return lax.dot_general(a, b, (((0,), (0,)), ((), ())), preferred_element_type=F32)


def kernel(
    n_stream,
    n_et,
    res_hbm,
    attn_gain_hbm,
    q_gain_hbm,
    key_gain_hbm,
    w_q_hbm,
    w_kv_hbm,
    w_o_hbm,
    cache_hbm,
    length_hbm,
    moe_gain_hbm,
    ids_hbm,
    gates_hbm,
    w_gu_hbm,
    w_down_hbm,
    out_ref,
    attn_gain,
    q_gain,
    key_gain,
    w_q,
    w_kv,
    w_o,
    cache,
    length,
    moe_gain,
    ids,
    gates,
    w_gu,
    w_down,
    features,
    heads_out,
    heads_in,
    mixed_out,
    mixed_in,
    mixed_f,
    rows_out,
    rows_in,
    rows_f,
    expert_rows,
    expert_squares,
    pairs_out,
    pairs_own,
    pairs_in,
    hidden_out,
    hidden_in,
    results_f,
    results_out,
    results_in,
    load_sem,
    et_send,
    et_recv,
    stream_send,
    stream_recv,
    known,
):
    me_s = lax.axis_index("stream")
    me = lax.axis_index("et")
    tokens = res_hbm.shape[0]
    local = tokens // n_et
    head_dim = q_gain_hbm.shape[1]
    own_heads = w_q_hbm.shape[1] // head_dim
    n_heads = own_heads * n_et
    kv_heads = n_et // 2
    group = n_heads // kv_heads
    width = res_hbm.shape[1] * n_et
    n_local = w_gu_hbm.shape[0]
    slots = n_stream * n_local * CAP
    scale = head_dim**-0.5

    def et_peer(step):
        return lax.rem(me + step, n_et)

    def stream_peer(step):
        return lax.rem(me_s + step, n_stream)

    n_y, n_z, n_core = (2, n_stream // 4, 2) if n_stream % 4 == 0 else (1, 1, n_stream)
    y, z, core = lax.div(me_s, n_z * n_core), lax.rem(lax.div(me_s, n_core), n_z), lax.rem(me_s, n_core)

    def stream_at(dy, dz, dc):
        return (
            lax.rem(y + dy, n_y) * (n_z * n_core)
            + lax.rem(z + dz, n_z) * n_core
            + lax.rem(core + dc, n_core)
        )

    across = [(dy, 0, dc) for dy in range(n_y) for dc in range(n_core) if dy or dc]

    def along(reach):
        return [(0, dz, 0) for dz in sorted({reach % n_z, -reach % n_z} - {0})]

    rounds = []
    reach = 1
    while reach < n_z // 2:
        rounds.append(along(reach))
        reach *= 2
    rounds.append(across)

    def tell(number):
        for away in rounds[number] if number < len(rounds) else ():
            pl.semaphore_signal(
                known.at[number],
                inc=1,
                device_id=(stream_at(*away), me),
                device_id_type=MESH,
            )

    def hear(number):
        if number < len(rounds):
            pl.semaphore_wait(known.at[number], len(rounds[number]))

    far_first = [
        stream_at(dy, dz, dc)
        for dz in sorted(range(n_z), key=lambda i: -min(i, n_z - i))
        for dy in reversed(range(n_y))
        for dc in reversed(range(n_core))
        if dy or dz or dc
    ]

    n_x = n_et // 2
    x, y_low = lax.div(me, 2), lax.rem(me, 2)
    et_far_first = [
        lax.rem(x + dx, n_x) * 2 + lax.rem(y_low + dy, 2)
        for dx in sorted(range(n_x), key=lambda i: -min(i, n_x - i))
        for dy in (1, 0)
        if dx or dy
    ]

    def et_copy(exchange, source, target, peer):
        return pltpu.make_async_remote_copy(
            src_ref=source,
            dst_ref=target,
            send_sem=et_send.at[exchange, peer],
            recv_sem=et_recv.at[exchange, me],
            device_id=(me_s, peer),
            device_id_type=MESH,
        )

    def et_arrival(exchange, source, target, peer):
        return pltpu.make_async_remote_copy(
            src_ref=source,
            dst_ref=target,
            send_sem=et_send.at[exchange, peer],
            recv_sem=et_recv.at[exchange, peer],
            device_id=(me_s, peer),
            device_id_type=MESH,
        )

    def stream_copy(exchange, source, target, peer):
        return pltpu.make_async_remote_copy(
            src_ref=source,
            dst_ref=target,
            send_sem=stream_send.at[exchange, peer],
            recv_sem=stream_recv.at[exchange, me_s],
            device_id=(peer, me),
            device_id_type=MESH,
        )

    def stream_arrival(exchange, source, target, peer):
        return pltpu.make_async_remote_copy(
            src_ref=source,
            dst_ref=target,
            send_sem=stream_send.at[exchange, peer],
            recv_sem=stream_recv.at[exchange, peer],
            device_id=(peer, me),
            device_id_type=MESH,
        )

    def loop(n, body):
        def step(i, carry):
            body(i)
            return carry

        lax.fori_loop(1, n, step, 0)

    barrier = pltpu.get_barrier_semaphore()
    greeted = [(me_s, peer) for peer in et_far_first]
    greeted += [(stream_at(*away), me) for away in along(1) + across]
    for device in greeted:
        pl.semaphore_signal(barrier, inc=1, device_id=device, device_id_type=MESH)

    pl.semaphore_wait(barrier, len(greeted))

    for peer in et_far_first:
        et_copy(FEATURES, res_hbm, features.at[me], peer).start()
    tell(0)

    loads = {}
    for name, source, target in (
        ("own", res_hbm, features.at[me]),
        ("length", length_hbm, length),
        ("attn_gain", attn_gain_hbm, attn_gain),
        ("q_gain", q_gain_hbm, q_gain),
        ("key_gain", key_gain_hbm, key_gain),
        ("ids", ids_hbm, ids),
        ("gates", gates_hbm, gates),
        ("moe_gain", moe_gain_hbm, moe_gain),
        ("w_q", w_q_hbm, w_q),
        ("w_kv", w_kv_hbm, w_kv),
        ("cache", cache_hbm, cache),
        ("w_o", w_o_hbm, w_o),
        ("w_gu", w_gu_hbm, w_gu),
        ("w_down", w_down_hbm, w_down),
    ):
        loads[name] = pltpu.make_async_copy(source, target, load_sem.at[len(loads)])
        loads[name].start()

    loads["length"].wait()
    lengths = jnp.broadcast_to(length[...], (tokens, tokens)).astype(F32)
    diagonal = iota((tokens, tokens), 0) == iota((tokens, tokens), 1)
    positions = jnp.sum(jnp.where(diagonal, lengths, 0.0), axis=1, keepdims=True)
    half = head_dim // 2
    lane = iota((tokens, head_dim), 1)
    steps = jnp.where(lane < half, lane, lane - half).astype(F32)
    angle = positions * jnp.exp(steps * (-2.0 * math.log(ROPE_BASE) / head_dim))
    cosine = jnp.cos(angle)
    sine = jnp.where(lane < half, -jnp.sin(angle), jnp.sin(angle))

    pad = 16
    row = iota((n_et * pad, LANES), 0)
    col = iota((n_et * pad, LANES), 1)
    peer_of, at = lax.div(row, pad), lax.rem(row, pad)
    n_q = local * own_heads
    picked = jnp.where(
        at < n_q,
        lax.rem(at, own_heads) * tokens + peer_of * local + lax.div(at, own_heads),
        jnp.where(
            at < n_q + local, own_heads * tokens + peer_of * local + at - n_q, -1
        ),
    )
    order_out = jnp.where(col == picked, 1.0, 0.0).astype(BF16)

    per = local * n_heads
    row = iota((3 * per, n_et * pad), 0)
    col = iota((3 * per, n_et * pad), 1)
    kind, at = lax.div(row, per), lax.rem(row, per)
    token, head = lax.div(at, n_heads), lax.rem(at, n_heads)
    picked = jnp.where(
        kind == 0,
        lax.div(head, own_heads) * pad + token * own_heads + lax.rem(head, own_heads),
        (lax.div(head, group) + jnp.where(kind == 2, kv_heads, 0)) * pad + n_q + token,
    )
    order_in = jnp.where(col == picked, 1.0, 0.0).astype(BF16)

    loads["ids"].wait()
    loads["gates"].wait()
    at = iota((slots, tokens), 0)
    place = lax.rem(at, n_local * CAP)
    expert = lax.div(at, n_local * CAP) * n_local + lax.rem(place, n_local)
    which = lax.div(place, n_local)
    gate = gates[...]
    gate = gate / jnp.sum(gate, axis=0, keepdims=True)
    named = jnp.zeros((slots, tokens), F32)
    weight = jnp.zeros((slots, tokens), F32)
    for k in range(ids_hbm.shape[0]):
        hit = expert == ids[k : k + 1, :]
        named = jnp.where(hit, 1.0, named)
        weight = jnp.where(hit, gate[k : k + 1, :], weight)
    before = jnp.where(
        iota((tokens, tokens), 0) < iota((tokens, tokens), 1), 1.0, 0.0
    ).astype(BF16)
    earlier = dot(named.astype(BF16), before)
    placed = jnp.where(earlier == which.astype(F32), named, 0.0)
    mixing = placed * weight
    placed = placed.astype(BF16)
    mixing_high = mixing.astype(BF16)
    mixing_low = (mixing - mixing_high.astype(F32)).astype(BF16)

    loads["own"].wait()
    loads["attn_gain"].wait()
    loop(
        n_et,
        lambda i: et_arrival(
            FEATURES, res_hbm, features.at[et_peer(i)], et_peer(i)
        ).wait_recv(),
    )
    full = jnp.concatenate([features[i].astype(F32) for i in range(n_et)], axis=1)
    gain = attn_gain[...].astype(F32)
    gain = jnp.concatenate([gain[i : i + 1] for i in range(gain.shape[0])], axis=1)
    normed = (
        full
        * lax.rsqrt(jnp.sum(full * full, axis=1, keepdims=True) * (1.0 / width) + EPS)
        * gain
    ).astype(BF16)

    def rotated(v, g):
        v = v * lax.rsqrt(jnp.mean(v * v, axis=1, keepdims=True) + EPS) * g
        return v * cosine + pltpu.roll(v, half, 1) * sine

    loads["q_gain"].wait()
    loads["key_gain"].wait()
    loads["w_q"].wait()
    query = dot(normed, w_q[...])
    loads["w_kv"].wait()
    key_value = dot(normed, w_kv[...])
    query_gain = q_gain[...].astype(F32)
    made = [
        rotated(query[:, i * head_dim : (i + 1) * head_dim], query_gain)
        for i in range(own_heads)
    ]
    made.append(
        jnp.where(me < kv_heads, rotated(key_value, key_gain[...].astype(F32)), key_value)
    )
    made.append(jnp.zeros((LANES - (own_heads + 1) * tokens, head_dim), F32))
    made = jnp.concatenate(made, axis=0).astype(BF16)
    heads_out[...] = dot(order_out, made).astype(BF16).reshape(heads_out.shape)
    heads_in[me] = heads_out[me]
    for peer in et_far_first:
        et_copy(HEADS, heads_out.at[peer], heads_in.at[me], peer).start()
    hear(0)
    tell(1)

    rows_of = cache_hbm.shape[0] // local
    piece = rows_of
    own_lane = iota((1, tokens), 1)
    lengths = length[...].astype(F32)
    loads["cache"].wait()
    loop(
        n_et,
        lambda i: et_arrival(
            HEADS, heads_out.at[et_peer(i)], heads_in.at[et_peer(i)], et_peer(i)
        ).wait_recv(),
    )
    ordered = dot(order_in, heads_in[...].reshape(n_et * pad, head_dim))
    for t in range(local):
        q = ordered[t * n_heads : (t + 1) * n_heads]
        new_key = ordered[per + t * n_heads : per + (t + 1) * n_heads]
        new_value = ordered[2 * per + t * n_heads : 2 * per + (t + 1) * n_heads]
        fresh = jnp.exp(jnp.sum(q * new_key, axis=1, keepdims=True) * scale)
        limit = (
            jnp.sum(
                jnp.where(own_lane == me * local + t, lengths, 0.0),
                axis=1,
                keepdims=True,
            )
            * float(2 * kv_heads)
        ).astype(jnp.int32)
        q = q.astype(BF16)
        column = iota((n_heads, piece), 1)
        aligned = lax.rem(column, 2 * kv_heads) == 2 * lax.div(
            iota((n_heads, piece), 0), group
        )
        total = fresh
        summed = fresh * new_value
        for p in range(rows_of // piece):
            block = cache[t * rows_of + p * piece : t * rows_of + (p + 1) * piece, :]
            score = dot_nt(q, block)
            live = aligned & (column < limit - p * piece)
            weights = jnp.where(live, jnp.exp(score * scale), 0.0)
            total = total + jnp.sum(weights, axis=1, keepdims=True)
            moved = jnp.concatenate(
                [
                    pltpu.roll(weights[:, i : i + LANES], 1, 1)
                    for i in range(0, piece, LANES)
                ],
                axis=1,
            )
            summed = summed + dot(moved.astype(BF16), block)
        mixed_out[t * n_heads : (t + 1) * n_heads, :] = (summed / total).astype(BF16)
    mixed_in[me] = mixed_out[...]
    for peer in et_far_first:
        et_copy(MIXED, mixed_out, mixed_in.at[me], peer).start()
    hear(1)
    tell(2)

    loads["w_o"].wait()
    loop(
        n_et,
        lambda i: et_arrival(
            MIXED, mixed_out, mixed_in.at[et_peer(i)], et_peer(i)
        ).wait_recv(),
    )
    mixed_f[...] = mixed_in[...].reshape(tokens * n_heads, head_dim).astype(F32)
    attended = jnp.concatenate(
        [mixed_f[pl.ds(h, tokens, stride=n_heads), :] for h in range(n_heads)], axis=1
    ).astype(BF16)
    resid = (features[me].astype(F32) + dot(attended, w_o[...])).astype(BF16)

    sent = dot(placed, resid)
    sent = sent.reshape(n_stream, n_local * CAP, 2 * LANES)
    rows_out[...] = jnp.concatenate(
        [sent[:, :, :LANES], sent[:, :, LANES:]], axis=1
    ).astype(BF16)
    rows_in[me_s] = rows_out[me_s]
    hear(2)
    for peer in far_first:
        stream_copy(OUTWARD, rows_out.at[peer], rows_in.at[me_s], peer).start()
    loads["moe_gain"].wait()
    gain = moe_gain[...].astype(F32)
    gain = jnp.concatenate([gain[0:1], gain[1:2]], axis=1)
    loads["w_gu"].wait()
    loop(
        n_stream,
        lambda i: stream_arrival(
            OUTWARD, rows_out.at[stream_peer(i)], rows_in.at[stream_peer(i)], stream_peer(i)
        ).wait_recv(),
    )
    chunk = 2 * n_local * CAP
    rows_f[...] = rows_in[...].reshape(n_stream * chunk, LANES).astype(F32)
    for j in range(n_local):
        taken = []
        for c in range(CAP):
            taken.append(
                jnp.concatenate(
                    [
                        rows_f[
                            pl.ds(h * n_local * CAP + c * n_local + j, n_stream, stride=chunk), :
                        ]
                        for h in range(2)
                    ],
                    axis=1,
                )
            )
        taken = jnp.concatenate(taken, axis=0)
        squares = jnp.sum(taken * taken, axis=1, keepdims=True)
        high = squares.astype(BF16).astype(F32)
        expert_squares[j] = jnp.where(
            iota((CAP * n_stream, LANES), 1) < LANES // 2, high, squares - high
        )
        expert_rows[j] = (taken * gain).astype(BF16)

    hidden_width = w_down_hbm.shape[1]
    for i in range(n_local):
        j = lax.rem(lax.div(me, CAP) + (2, 1, 3, 0)[i], n_local)
        taken = expert_rows[j]
        products = jnp.concatenate(
            [dot(taken, w_gu[j, 0]), dot(taken, w_gu[j, 1]), expert_squares[j]], axis=1
        )
        pairs_out[i] = products.astype(BF16).reshape(pairs_out.shape[1:])
        if i < n_local - 1:
            for c in range(CAP):
                et_copy(
                    PAIRS, pairs_out.at[i, c], pairs_in.at[me], CAP * j + c
                ).start()
        else:
            pairs_own[...] = products.reshape(pairs_own.shape)
            c = 1 - lax.rem(me, CAP)
            et_copy(PAIRS, pairs_out.at[i, c], pairs_in.at[me], CAP * j + c).start()
    pair = pairs_own[lax.rem(me, CAP)]
    for i in range(1, n_et):
        et_arrival(
            PAIRS, pairs_out.at[0, 0], pairs_in.at[et_peer(i)], et_peer(i)
        ).wait_recv()
        pair = pair + pairs_in[et_peer(i)].astype(F32)
    squares = jnp.sum(pair[:, 2 * hidden_width :], axis=1, keepdims=True) * (
        2.0 / LANES / width
    )
    level = lax.rsqrt(squares + EPS)
    first = pair[:, :hidden_width] * level
    second = pair[:, hidden_width : 2 * hidden_width] * level
    hidden_out[...] = (first / (1.0 + jnp.exp(-first)) * second).astype(BF16)
    hidden_in[me] = hidden_out[...]
    for peer in et_far_first:
        et_copy(HIDDEN, hidden_out, hidden_in.at[me], peer).start()

    loads["w_down"].wait()
    loop(
        n_et,
        lambda i: et_arrival(
            HIDDEN, hidden_out, hidden_in.at[et_peer(i)], et_peer(i)
        ).wait_recv(),
    )
    for j in range(n_local):
        hidden = hidden_in[CAP * j : CAP * (j + 1)].reshape(CAP * n_stream, hidden_width)
        result = dot(hidden, w_down[j])
        for c in range(CAP):
            for h in range(2):
                results_f[
                    pl.ds(h * n_local * CAP + c * n_local + j, n_stream, stride=chunk), :
                ] = result[c * n_stream : (c + 1) * n_stream, h * LANES : (h + 1) * LANES]
    results_out[...] = results_f[...].astype(BF16).reshape(results_out.shape)
    results_in[me_s] = results_out[me_s]
    for peer in far_first:
        stream_copy(HOME, results_out.at[peer], results_in.at[me_s], peer).start()
    loop(
        n_stream,
        lambda i: stream_arrival(
            HOME, results_out.at[stream_peer(i)], results_in.at[stream_peer(i)], stream_peer(i)
        ).wait_recv(),
    )
    returned = results_in[...].astype(F32)
    returned = (
        jnp.concatenate(
            [returned[:, : n_local * CAP], returned[:, n_local * CAP :]], axis=2
        )
        .reshape(slots, 2 * LANES)
        .astype(BF16)
    )
    routed = dot_tn(mixing_high, returned) + dot_tn(mixing_low, returned)
    out_ref[...] = (resid.astype(F32) + routed).astype(BF16)

    def sent_et(exchange, source, target):
        loop(
            n_et,
            lambda i: et_copy(exchange, source, target, et_peer(i)).wait_send(),
        )

    sent_et(FEATURES, res_hbm, features.at[me])
    sent_et(HEADS, heads_out.at[0], heads_in.at[me])
    sent_et(MIXED, mixed_out, mixed_in.at[me])
    sent_et(PAIRS, pairs_out.at[0, 0], pairs_in.at[me])
    sent_et(HIDDEN, hidden_out, hidden_in.at[me])
    for exchange, source, target in (
        (OUTWARD, rows_out, rows_in),
        (HOME, results_out, results_in),
    ):
        loop(
            n_stream,
            lambda i: stream_copy(
                exchange, source.at[stream_peer(i)], target.at[me_s], stream_peer(i)
            ).wait_send(),
        )


def on_device(
    n_stream,
    n_et,
    residual_in,
    attn_gain,
    q_gain,
    key_norm_gain,
    w_q,
    key_value_weight,
    w_o,
    key_value_cache,
    cache_length,
    moe_gain,
    route_ids,
    route_gates,
    w_gate_up,
    w_down,
):
    tokens, features = residual_in.shape
    head_dim = q_gain.shape[0]
    local, span, _, kv_width = key_value_cache.shape
    kv_heads = kv_width // head_dim
    n_heads = w_q.shape[1] // head_dim * n_et
    n_local = w_gate_up.shape[0]
    hidden = w_down.shape[1]
    cache = (
        key_value_cache.reshape(local, span, 2, kv_heads, head_dim)
        .transpose(0, 1, 3, 2, 4)
        .reshape(local * span * kv_heads * 2, head_dim)
    )
    args = (
        residual_in,
        attn_gain.reshape(-1, LANES),
        q_gain.reshape(1, -1),
        key_norm_gain.reshape(1, -1),
        w_q,
        key_value_weight,
        w_o,
        cache,
        cache_length.reshape(1, -1),
        moe_gain.reshape(-1, LANES),
        route_ids.T,
        route_gates.T,
        w_gate_up,
        w_down,
    )
    chunk = 2 * n_local * CAP
    vmem = pltpu.VMEM
    row_blocks = (n_stream, chunk, LANES)
    flat_rows = (n_stream * chunk, LANES)
    pair_width = 2 * hidden + LANES
    scratch = [vmem(a.shape, a.dtype) for a in args[1:]] + [
        vmem((n_et, tokens, features), BF16),
        vmem((n_et, 16, head_dim), BF16),
        vmem((n_et, 16, head_dim), BF16),
        vmem((local * n_heads, head_dim), BF16),
        vmem((n_et, local * n_heads, head_dim), BF16),
        vmem((tokens * n_heads, head_dim), F32),
        vmem(row_blocks, BF16),
        vmem(row_blocks, BF16),
        vmem(flat_rows, F32),
        vmem((n_local, CAP * n_stream, features), BF16),
        vmem((n_local, CAP * n_stream, LANES), F32),
        vmem((n_local, CAP, n_stream, pair_width), BF16),
        vmem((CAP, n_stream, pair_width), F32),
        vmem((n_et, n_stream, pair_width), BF16),
        vmem((n_stream, hidden), BF16),
        vmem((n_et, n_stream, hidden), BF16),
        vmem(flat_rows, F32),
        vmem(row_blocks, BF16),
        vmem(row_blocks, BF16),
        pltpu.SemaphoreType.DMA((len(args),)),
        pltpu.SemaphoreType.DMA((5, n_et)),
        pltpu.SemaphoreType.DMA((5, n_et)),
        pltpu.SemaphoreType.DMA((2, n_stream)),
        pltpu.SemaphoreType.DMA((2, n_stream)),
        pltpu.SemaphoreType.REGULAR((3,)),
    ]
    return pl.pallas_call(
        functools.partial(kernel, n_stream, n_et),
        out_shape=pltpu.VMEM(residual_in.shape, residual_in.dtype),
        in_specs=[pl.BlockSpec(memory_space=pl.ANY)] * len(args),
        out_specs=pl.BlockSpec(memory_space=pltpu.VMEM),
        scratch_shapes=scratch,
        compiler_params=pltpu.CompilerParams(
            collective_id=0, has_side_effects=True, vmem_limit_bytes=56 * 1024 * 1024
        ),
    )(*args)


def solution(mesh):
    placed = (
        P("stream", "et"),
        P(),
        P(),
        P(),
        P(None, "et"),
        P(None, "et"),
        P(None, "et"),
        P(("stream", "et"), None, None, None),
        P("stream"),
        P("et"),
        P("stream", None),
        P("stream", None),
        P("stream", None, "et", None),
        P("stream", None, "et"),
    )
    return jax.shard_map(
        functools.partial(on_device, mesh.shape["stream"], mesh.shape["et"]),
        mesh=mesh,
        in_specs=placed,
        out_specs=P("stream", "et"),
        check_vma=False,
    )
```

```python
import functools
import math

import jax
import jax.numpy as jnp
from jax import lax
from jax.experimental import pallas as pl
from jax.experimental.pallas import tpu as pltpu
from jax.sharding import PartitionSpec as P

EPS = 1e-06
ROPE_BASE = 1000000.0
CAP = 2
LANES = 128
MESH = pl.DeviceIdType.MESH
F32 = jnp.float32
BF16 = jnp.bfloat16

FEATURES, HEADS, MIXED, PAIRS, HIDDEN = 0, 1, 2, 3, 5
OUTWARD, HOME = range(2)
WAVES = 2


def iota(shape, dim):
    return lax.broadcasted_iota(jnp.int32, shape, dim)


def dot(a, b):
    return jnp.dot(a, b, preferred_element_type=F32)


def dot_nt(a, b):
    return lax.dot_general(a, b, (((1,), (1,)), ((), ())), preferred_element_type=F32)


def dot_tn(a, b):
    return lax.dot_general(a, b, (((0,), (0,)), ((), ())), preferred_element_type=F32)


def kernel(
    n_stream,
    n_et,
    res_hbm,
    attn_gain_hbm,
    q_gain_hbm,
    key_gain_hbm,
    w_q_hbm,
    w_kv_hbm,
    w_o_hbm,
    cache_hbm,
    length_hbm,
    moe_gain_hbm,
    ids_hbm,
    gates_hbm,
    w_gu_hbm,
    w_down_hbm,
    out_ref,
    attn_gain,
    q_gain,
    key_gain,
    w_q,
    w_kv,
    w_o,
    cache,
    length,
    moe_gain,
    ids,
    gates,
    w_gu,
    w_down,
    features,
    heads_out,
    heads_in,
    mixed_out,
    mixed_in,
    mixed_f,
    rows_out,
    rows_in,
    rows_f,
    expert_rows,
    expert_squares,
    pairs_out,
    pairs_own,
    pairs_in,
    hidden_out,
    hidden_in,
    results_f,
    results_out,
    results_in,
    load_sem,
    et_send,
    et_recv,
    stream_send,
    stream_recv,
    known,
):
    me_s = lax.axis_index("stream")
    me = lax.axis_index("et")
    tokens = res_hbm.shape[0]
    local = tokens // n_et
    head_dim = q_gain_hbm.shape[1]
    own_heads = w_q_hbm.shape[1] // head_dim
    n_heads = own_heads * n_et
    kv_heads = n_et // 2
    group = n_heads // kv_heads
    width = res_hbm.shape[1] * n_et
    n_local = w_gu_hbm.shape[0]
    slots = n_stream * n_local * CAP
    scale = head_dim**-0.5

    def et_peer(step):
        return lax.rem(me + step, n_et)

    def stream_peer(step):
        return lax.rem(me_s + step, n_stream)

    n_y, n_z, n_core = (2, n_stream // 4, 2) if n_stream % 4 == 0 else (1, 1, n_stream)
    y, z, core = lax.div(me_s, n_z * n_core), lax.rem(lax.div(me_s, n_core), n_z), lax.rem(me_s, n_core)

    def stream_at(dy, dz, dc):
        return (
            lax.rem(y + dy, n_y) * (n_z * n_core)
            + lax.rem(z + dz, n_z) * n_core
            + lax.rem(core + dc, n_core)
        )

    across = [(dy, 0, dc) for dy in range(n_y) for dc in range(n_core) if dy or dc]

    def along(reach):
        return [(0, dz, 0) for dz in sorted({reach % n_z, -reach % n_z} - {0})]

    rounds = []
    reach = 1
    while reach < n_z // 2:
        rounds.append(along(reach))
        reach *= 2
    rounds.append(across)

    def tell(number):
        for away in rounds[number] if number < len(rounds) else ():
            pl.semaphore_signal(
                known.at[number],
                inc=1,
                device_id=(stream_at(*away), me),
                device_id_type=MESH,
            )

    def hear(number):
        if number < len(rounds):
            pl.semaphore_wait(known.at[number], len(rounds[number]))

    def hops(away):
        return min(away[1], n_z - away[1]) + 2 * away[0]

    def back(away):
        return (-away[0] % n_y, -away[1] % n_z, -away[2] % n_core)

    relative = sorted(
        [(dy, dz, dc) for dy in range(n_y) for dz in range(n_z) for dc in range(n_core)],
        key=lambda away: (hops(away), away != (0, 0, 0)),
    )
    share = n_stream // WAVES
    waves = [
        sorted(relative[w * share : (w + 1) * share], key=lambda away: -hops(away))
        for w in range(WAVES)
    ]
    slot_of = {away: i for i, away in enumerate(waves[0] + waves[1])}
    at_home = slot_of[0, 0, 0]

    n_x = n_et // 2
    x, y_low = lax.div(me, 2), lax.rem(me, 2)
    et_far_first = [
        lax.rem(x + dx, n_x) * 2 + lax.rem(y_low + dy, 2)
        for dx in sorted(range(n_x), key=lambda i: -min(i, n_x - i))
        for dy in (1, 0)
        if dx or dy
    ]

    def et_copy(exchange, source, target, peer):
        return pltpu.make_async_remote_copy(
            src_ref=source,
            dst_ref=target,
            send_sem=et_send.at[exchange, peer],
            recv_sem=et_recv.at[exchange, me],
            device_id=(me_s, peer),
            device_id_type=MESH,
        )

    def et_arrival(exchange, source, target, peer):
        return pltpu.make_async_remote_copy(
            src_ref=source,
            dst_ref=target,
            send_sem=et_send.at[exchange, peer],
            recv_sem=et_recv.at[exchange, peer],
            device_id=(me_s, peer),
            device_id_type=MESH,
        )

    def stream_copy(exchange, source, target, away):
        return pltpu.make_async_remote_copy(
            src_ref=source,
            dst_ref=target,
            send_sem=stream_send.at[exchange, slot_of[away]],
            recv_sem=stream_recv.at[exchange, slot_of[back(away)]],
            device_id=(stream_at(*away), me),
            device_id_type=MESH,
        )

    def stream_arrival(exchange, source, target, away):
        return pltpu.make_async_remote_copy(
            src_ref=source,
            dst_ref=target,
            send_sem=stream_send.at[exchange, slot_of[away]],
            recv_sem=stream_recv.at[exchange, slot_of[away]],
            device_id=(stream_at(*away), me),
            device_id_type=MESH,
        )

    def others(wave):
        return [away for away in waves[wave] if away != (0, 0, 0)]

    def loop(n, body):
        def step(i, carry):
            body(i)
            return carry

        lax.fori_loop(1, n, step, 0)

    barrier = pltpu.get_barrier_semaphore()
    greeted = [(me_s, peer) for peer in et_far_first]
    greeted += [(stream_at(*away), me) for away in along(1) + across]
    for device in greeted:
        pl.semaphore_signal(barrier, inc=1, device_id=device, device_id_type=MESH)

    pl.semaphore_wait(barrier, len(greeted))

    for peer in et_far_first:
        et_copy(FEATURES, res_hbm, features.at[me], peer).start()
    tell(0)

    loads = {}
    for name, source, target in (
        ("own", res_hbm, features.at[me]),
        ("length", length_hbm, length),
        ("attn_gain", attn_gain_hbm, attn_gain),
        ("q_gain", q_gain_hbm, q_gain),
        ("key_gain", key_gain_hbm, key_gain),
        ("ids", ids_hbm, ids),
        ("gates", gates_hbm, gates),
        ("moe_gain", moe_gain_hbm, moe_gain),
        ("w_q", w_q_hbm, w_q),
        ("w_kv", w_kv_hbm, w_kv),
        ("cache", cache_hbm, cache),
        ("w_o", w_o_hbm, w_o),
        ("w_gu", w_gu_hbm, w_gu),
        ("w_down", w_down_hbm, w_down),
    ):
        loads[name] = pltpu.make_async_copy(source, target, load_sem.at[len(loads)])
        loads[name].start()

    loads["length"].wait()
    lengths = jnp.broadcast_to(length[...], (tokens, tokens)).astype(F32)
    diagonal = iota((tokens, tokens), 0) == iota((tokens, tokens), 1)
    positions = jnp.sum(jnp.where(diagonal, lengths, 0.0), axis=1, keepdims=True)
    half = head_dim // 2
    lane = iota((tokens, head_dim), 1)
    steps = jnp.where(lane < half, lane, lane - half).astype(F32)
    angle = positions * jnp.exp(steps * (-2.0 * math.log(ROPE_BASE) / head_dim))
    cosine = jnp.cos(angle)
    sine = jnp.where(lane < half, -jnp.sin(angle), jnp.sin(angle))

    pad = 16
    row = iota((n_et * pad, LANES), 0)
    col = iota((n_et * pad, LANES), 1)
    peer_of, at = lax.div(row, pad), lax.rem(row, pad)
    n_q = local * own_heads
    picked = jnp.where(
        at < n_q,
        lax.rem(at, own_heads) * tokens + peer_of * local + lax.div(at, own_heads),
        jnp.where(
            at < n_q + local, own_heads * tokens + peer_of * local + at - n_q, -1
        ),
    )
    order_out = jnp.where(col == picked, 1.0, 0.0).astype(BF16)

    per = local * n_heads
    row = iota((3 * per, n_et * pad), 0)
    col = iota((3 * per, n_et * pad), 1)
    kind, at = lax.div(row, per), lax.rem(row, per)
    token, head = lax.div(at, n_heads), lax.rem(at, n_heads)
    picked = jnp.where(
        kind == 0,
        lax.div(head, own_heads) * pad + token * own_heads + lax.rem(head, own_heads),
        (lax.div(head, group) + jnp.where(kind == 2, kv_heads, 0)) * pad + n_q + token,
    )
    order_in = jnp.where(col == picked, 1.0, 0.0).astype(BF16)

    loads["ids"].wait()
    loads["gates"].wait()
    at = iota((slots, tokens), 0)
    place = lax.rem(at, n_local * CAP)
    expert = lax.div(at, n_local * CAP) * n_local + lax.rem(place, n_local)
    which = lax.div(place, n_local)
    gate = gates[...]
    gate = gate / jnp.sum(gate, axis=0, keepdims=True)
    named = jnp.zeros((slots, tokens), F32)
    weight = jnp.zeros((slots, tokens), F32)
    for k in range(ids_hbm.shape[0]):
        hit = expert == ids[k : k + 1, :]
        named = jnp.where(hit, 1.0, named)
        weight = jnp.where(hit, gate[k : k + 1, :], weight)
    before = jnp.where(
        iota((tokens, tokens), 0) < iota((tokens, tokens), 1), 1.0, 0.0
    ).astype(BF16)
    earlier = dot(named.astype(BF16), before)
    placed = jnp.where(earlier == which.astype(F32), named, 0.0)
    mixing = placed * weight
    placed = placed.astype(BF16)
    mixing_high = mixing.astype(BF16)
    mixing_low = (mixing - mixing_high.astype(F32)).astype(BF16)

    loads["own"].wait()
    loads["attn_gain"].wait()
    loop(
        n_et,
        lambda i: et_arrival(
            FEATURES, res_hbm, features.at[et_peer(i)], et_peer(i)
        ).wait_recv(),
    )
    full = jnp.concatenate([features[i].astype(F32) for i in range(n_et)], axis=1)
    gain = attn_gain[...].astype(F32)
    gain = jnp.concatenate([gain[i : i + 1] for i in range(gain.shape[0])], axis=1)
    normed = (
        full
        * lax.rsqrt(jnp.sum(full * full, axis=1, keepdims=True) * (1.0 / width) + EPS)
        * gain
    ).astype(BF16)

    def rotated(v, g):
        v = v * lax.rsqrt(jnp.mean(v * v, axis=1, keepdims=True) + EPS) * g
        return v * cosine + pltpu.roll(v, half, 1) * sine

    loads["q_gain"].wait()
    loads["key_gain"].wait()
    loads["w_q"].wait()
    query = dot(normed, w_q[...])
    loads["w_kv"].wait()
    key_value = dot(normed, w_kv[...])
    query_gain = q_gain[...].astype(F32)
    made = [
        rotated(query[:, i * head_dim : (i + 1) * head_dim], query_gain)
        for i in range(own_heads)
    ]
    made.append(
        jnp.where(me < kv_heads, rotated(key_value, key_gain[...].astype(F32)), key_value)
    )
    made.append(jnp.zeros((LANES - (own_heads + 1) * tokens, head_dim), F32))
    made = jnp.concatenate(made, axis=0).astype(BF16)
    heads_out[...] = dot(order_out, made).astype(BF16).reshape(heads_out.shape)
    heads_in[me] = heads_out[me]
    for peer in et_far_first:
        et_copy(HEADS, heads_out.at[peer], heads_in.at[me], peer).start()
    hear(0)
    tell(1)

    rows_of = cache_hbm.shape[0] // local
    piece = rows_of
    own_lane = iota((1, tokens), 1)
    lengths = length[...].astype(F32)
    loads["cache"].wait()
    loop(
        n_et,
        lambda i: et_arrival(
            HEADS, heads_out.at[et_peer(i)], heads_in.at[et_peer(i)], et_peer(i)
        ).wait_recv(),
    )
    ordered = dot(order_in, heads_in[...].reshape(n_et * pad, head_dim))
    for t in range(local):
        q = ordered[t * n_heads : (t + 1) * n_heads]
        new_key = ordered[per + t * n_heads : per + (t + 1) * n_heads]
        new_value = ordered[2 * per + t * n_heads : 2 * per + (t + 1) * n_heads]
        fresh = jnp.exp(jnp.sum(q * new_key, axis=1, keepdims=True) * scale)
        limit = (
            jnp.sum(
                jnp.where(own_lane == me * local + t, lengths, 0.0),
                axis=1,
                keepdims=True,
            )
            * float(2 * kv_heads)
        ).astype(jnp.int32)
        q = q.astype(BF16)
        column = iota((n_heads, piece), 1)
        aligned = lax.rem(column, 2 * kv_heads) == 2 * lax.div(
            iota((n_heads, piece), 0), group
        )
        total = fresh
        summed = fresh * new_value
        for p in range(rows_of // piece):
            block = cache[t * rows_of + p * piece : t * rows_of + (p + 1) * piece, :]
            score = dot_nt(q, block)
            live = aligned & (column < limit - p * piece)
            weights = jnp.where(live, jnp.exp(score * scale), 0.0)
            total = total + jnp.sum(weights, axis=1, keepdims=True)
            moved = jnp.concatenate(
                [
                    pltpu.roll(weights[:, i : i + LANES], 1, 1)
                    for i in range(0, piece, LANES)
                ],
                axis=1,
            )
            summed = summed + dot(moved.astype(BF16), block)
        mixed_out[t * n_heads : (t + 1) * n_heads, :] = (summed / total).astype(BF16)
    mixed_in[me] = mixed_out[...]
    for peer in et_far_first:
        et_copy(MIXED, mixed_out, mixed_in.at[me], peer).start()
    hear(1)
    tell(2)

    loads["w_o"].wait()
    loop(
        n_et,
        lambda i: et_arrival(
            MIXED, mixed_out, mixed_in.at[et_peer(i)], et_peer(i)
        ).wait_recv(),
    )
    mixed_f[...] = mixed_in[...].reshape(tokens * n_heads, head_dim).astype(F32)
    attended = jnp.concatenate(
        [mixed_f[pl.ds(h, tokens, stride=n_heads), :] for h in range(n_heads)], axis=1
    ).astype(BF16)
    resid = (features[me].astype(F32) + dot(attended, w_o[...])).astype(BF16)

    sent = dot(placed, resid)
    sent = sent.reshape(n_stream, n_local * CAP, 2 * LANES)
    rows_out[...] = jnp.concatenate(
        [sent[:, :, :LANES], sent[:, :, LANES:]], axis=1
    ).astype(BF16)
    rows_in[at_home] = rows_out[me_s]
    hear(2)
    for w in range(WAVES):
        for away in others(w):
            stream_copy(
                OUTWARD,
                rows_out.at[stream_at(*away)],
                rows_in.at[slot_of[back(away)]],
                away,
            ).start()
    loads["moe_gain"].wait()
    gain = moe_gain[...].astype(F32)
    gain = jnp.concatenate([gain[0:1], gain[1:2]], axis=1)
    loads["w_gu"].wait()
    chunk = 2 * n_local * CAP
    hidden_width = w_down_hbm.shape[1]

    for w in range(WAVES):
        for away in others(w):
            stream_arrival(
                OUTWARD, rows_out.at[0], rows_in.at[slot_of[away]], away
            ).wait_recv()
        rows_f[w * share * chunk : (w + 1) * share * chunk, :] = (
            rows_in[w * share : (w + 1) * share].reshape(share * chunk, LANES).astype(F32)
        )
        for j in range(n_local):
            taken = []
            for c in range(CAP):
                first = w * share * chunk + c * n_local + j
                taken.append(
                    jnp.concatenate(
                        [
                            rows_f[pl.ds(first + h * n_local * CAP, share, stride=chunk), :]
                            for h in range(2)
                        ],
                        axis=1,
                    )
                )
            taken = jnp.concatenate(taken, axis=0)
            squares = jnp.sum(taken * taken, axis=1, keepdims=True)
            high = squares.astype(BF16).astype(F32)
            expert_squares[w, j] = jnp.where(
                iota((CAP * share, LANES), 1) < LANES // 2, high, squares - high
            )
            expert_rows[w, j] = (taken * gain).astype(BF16)
        for i in range(n_local):
            j = lax.rem(lax.div(me, CAP) + (2, 1, 3, 0)[i], n_local)
            taken = expert_rows[w, j]
            products = jnp.concatenate(
                [dot(taken, w_gu[j, 0]), dot(taken, w_gu[j, 1]), expert_squares[w, j]], axis=1
            )
            pairs_out[w, i] = products.astype(BF16).reshape(pairs_out.shape[2:])
            if i < n_local - 1:
                for c in range(CAP):
                    et_copy(
                        PAIRS + w, pairs_out.at[w, i, c], pairs_in.at[w, me], CAP * j + c
                    ).start()
            else:
                pairs_own[w] = products.reshape(pairs_own.shape[1:])
                c = 1 - lax.rem(me, CAP)
                et_copy(
                    PAIRS + w, pairs_out.at[w, i, c], pairs_in.at[w, me], CAP * j + c
                ).start()
    for w in range(WAVES):
        pair = pairs_own[w, lax.rem(me, CAP)]
        for i in range(1, n_et):
            et_arrival(
                PAIRS + w, pairs_out.at[w, 0, 0], pairs_in.at[w, et_peer(i)], et_peer(i)
            ).wait_recv()
            pair = pair + pairs_in[w, et_peer(i)].astype(F32)
        squares = jnp.sum(pair[:, 2 * hidden_width :], axis=1, keepdims=True) * (
            2.0 / LANES / width
        )
        level = lax.rsqrt(squares + EPS)
        first = pair[:, :hidden_width] * level
        second = pair[:, hidden_width : 2 * hidden_width] * level
        hidden_out[w] = (first / (1.0 + jnp.exp(-first)) * second).astype(BF16)
        for peer in et_far_first:
            et_copy(HIDDEN + w, hidden_out.at[w], hidden_in.at[w, me], peer).start()
        hidden_in[w, me] = hidden_out[w]

    loads["w_down"].wait()
    for w in range(WAVES):
        loop(
            n_et,
            lambda i: et_arrival(
                HIDDEN + w, hidden_out.at[w], hidden_in.at[w, et_peer(i)], et_peer(i)
            ).wait_recv(),
        )
        for j in range(n_local):
            hidden = hidden_in[w, CAP * j : CAP * (j + 1)].reshape(CAP * share, hidden_width)
            result = dot(hidden, w_down[j])
            for c in range(CAP):
                for h in range(2):
                    first = w * share * chunk + h * n_local * CAP + c * n_local + j
                    results_f[pl.ds(first, share, stride=chunk), :] = result[
                        c * share : (c + 1) * share, h * LANES : (h + 1) * LANES
                    ]
        results_out[w * share : (w + 1) * share] = (
            results_f[w * share * chunk : (w + 1) * share * chunk, :]
            .astype(BF16)
            .reshape(share, chunk, LANES)
        )
        for away in others(w):
            stream_copy(
                HOME, results_out.at[slot_of[away]], results_in.at[me_s], away
            ).start()
    results_in[me_s] = results_out[at_home]
    for w in range(WAVES):
        for away in others(w):
            stream_arrival(
                HOME, results_out.at[0], results_in.at[stream_at(*away)], away
            ).wait_recv()
    returned = results_in[...].astype(F32)
    returned = (
        jnp.concatenate(
            [returned[:, : n_local * CAP], returned[:, n_local * CAP :]], axis=2
        )
        .reshape(slots, 2 * LANES)
        .astype(BF16)
    )
    routed = dot_tn(mixing_high, returned) + dot_tn(mixing_low, returned)
    out_ref[...] = (resid.astype(F32) + routed).astype(BF16)

    def sent_et(exchange, source, target):
        loop(
            n_et,
            lambda i: et_copy(exchange, source, target, et_peer(i)).wait_send(),
        )

    sent_et(FEATURES, res_hbm, features.at[me])
    sent_et(HEADS, heads_out.at[0], heads_in.at[me])
    sent_et(MIXED, mixed_out, mixed_in.at[me])
    for w in range(WAVES):
        sent_et(PAIRS + w, pairs_out.at[w, 0, 0], pairs_in.at[w, me])
        sent_et(HIDDEN + w, hidden_out.at[w], hidden_in.at[w, me])
        for away in others(w):
            stream_copy(OUTWARD, rows_out.at[0], rows_in.at[0], away).wait_send()
            stream_copy(HOME, results_out.at[0], results_in.at[0], away).wait_send()


def on_device(
    n_stream,
    n_et,
    residual_in,
    attn_gain,
    q_gain,
    key_norm_gain,
    w_q,
    key_value_weight,
    w_o,
    key_value_cache,
    cache_length,
    moe_gain,
    route_ids,
    route_gates,
    w_gate_up,
    w_down,
):
    tokens, features = residual_in.shape
    head_dim = q_gain.shape[0]
    local, span, _, kv_width = key_value_cache.shape
    kv_heads = kv_width // head_dim
    n_heads = w_q.shape[1] // head_dim * n_et
    n_local = w_gate_up.shape[0]
    hidden = w_down.shape[1]
    cache = (
        key_value_cache.reshape(local, span, 2, kv_heads, head_dim)
        .transpose(0, 1, 3, 2, 4)
        .reshape(local * span * kv_heads * 2, head_dim)
    )
    args = (
        residual_in,
        attn_gain.reshape(-1, LANES),
        q_gain.reshape(1, -1),
        key_norm_gain.reshape(1, -1),
        w_q,
        key_value_weight,
        w_o,
        cache,
        cache_length.reshape(1, -1),
        moe_gain.reshape(-1, LANES),
        route_ids.T,
        route_gates.T,
        w_gate_up,
        w_down,
    )
    chunk = 2 * n_local * CAP
    vmem = pltpu.VMEM
    row_blocks = (n_stream, chunk, LANES)
    flat_rows = (n_stream * chunk, LANES)
    pair_width = 2 * hidden + LANES
    share = n_stream // WAVES
    scratch = [vmem(a.shape, a.dtype) for a in args[1:]] + [
        vmem((n_et, tokens, features), BF16),
        vmem((n_et, 16, head_dim), BF16),
        vmem((n_et, 16, head_dim), BF16),
        vmem((local * n_heads, head_dim), BF16),
        vmem((n_et, local * n_heads, head_dim), BF16),
        vmem((tokens * n_heads, head_dim), F32),
        vmem(row_blocks, BF16),
        vmem(row_blocks, BF16),
        vmem(flat_rows, F32),
        vmem((WAVES, n_local, CAP * share, features), BF16),
        vmem((WAVES, n_local, CAP * share, LANES), F32),
        vmem((WAVES, n_local, CAP, share, pair_width), BF16),
        vmem((WAVES, CAP, share, pair_width), F32),
        vmem((WAVES, n_et, share, pair_width), BF16),
        vmem((WAVES, share, hidden), BF16),
        vmem((WAVES, n_et, share, hidden), BF16),
        vmem(flat_rows, F32),
        vmem(row_blocks, BF16),
        vmem(row_blocks, BF16),
        pltpu.SemaphoreType.DMA((len(args),)),
        pltpu.SemaphoreType.DMA((7, n_et)),
        pltpu.SemaphoreType.DMA((7, n_et)),
        pltpu.SemaphoreType.DMA((2, n_stream)),
        pltpu.SemaphoreType.DMA((2, n_stream)),
        pltpu.SemaphoreType.REGULAR((3,)),
    ]
    return pl.pallas_call(
        functools.partial(kernel, n_stream, n_et),
        out_shape=pltpu.VMEM(residual_in.shape, residual_in.dtype),
        in_specs=[pl.BlockSpec(memory_space=pl.ANY)] * len(args),
        out_specs=pl.BlockSpec(memory_space=pltpu.VMEM),
        scratch_shapes=scratch,
        compiler_params=pltpu.CompilerParams(
            collective_id=0, has_side_effects=True, vmem_limit_bytes=56 * 1024 * 1024
        ),
    )(*args)


def solution(mesh):
    placed = (
        P("stream", "et"),
        P(),
        P(),
        P(),
        P(None, "et"),
        P(None, "et"),
        P(None, "et"),
        P(("stream", "et"), None, None, None),
        P("stream"),
        P("et"),
        P("stream", None),
        P("stream", None),
        P("stream", None, "et", None),
        P("stream", None, "et"),
    )
    return jax.shard_map(
        functools.partial(on_device, mesh.shape["stream"], mesh.shape["et"]),
        mesh=mesh,
        in_specs=placed,
        out_specs=P("stream", "et"),
        check_vma=False,
    )
```

```python
import functools
import math

import jax
import jax.numpy as jnp
from jax import lax
from jax.experimental import pallas as pl
from jax.experimental.pallas import tpu as pltpu
from jax.sharding import PartitionSpec as P

EPS = 1e-06
ROPE_BASE = 1000000.0
CAP = 2
LANES = 128
MESH = pl.DeviceIdType.MESH
F32 = jnp.float32
BF16 = jnp.bfloat16

FEATURES, HEADS, MIXED, PAIRS, HIDDEN = 0, 1, 2, 3, 5
OUTWARD, HOME = range(2)
WAVES = 2


def iota(shape, dim):
    return lax.broadcasted_iota(jnp.int32, shape, dim)


def dot(a, b):
    return jnp.dot(a, b, preferred_element_type=F32)


def dot_nt(a, b):
    return lax.dot_general(a, b, (((1,), (1,)), ((), ())), preferred_element_type=F32)


def dot_tn(a, b):
    return lax.dot_general(a, b, (((0,), (0,)), ((), ())), preferred_element_type=F32)


def kernel(
    n_stream,
    n_et,
    res_hbm,
    attn_gain_hbm,
    q_gain_hbm,
    key_gain_hbm,
    w_q_hbm,
    w_kv_hbm,
    w_o_hbm,
    cache_hbm,
    length_hbm,
    moe_gain_hbm,
    ids_hbm,
    gates_hbm,
    w_gu_hbm,
    w_down_hbm,
    out_ref,
    attn_gain,
    q_gain,
    key_gain,
    w_q,
    w_kv,
    w_o,
    cache,
    length,
    moe_gain,
    ids,
    gates,
    w_gu,
    w_down,
    cache_f,
    split,
    features,
    heads_out,
    heads_in,
    mixed_out,
    mixed_in,
    mixed_f,
    rows_out,
    rows_in,
    rows_f,
    expert_rows,
    expert_squares,
    pairs_out,
    pairs_own,
    pairs_in,
    hidden_out,
    hidden_in,
    results_f,
    results_out,
    results_in,
    load_sem,
    et_send,
    et_recv,
    stream_send,
    stream_recv,
    known,
):
    me_s = lax.axis_index("stream")
    me = lax.axis_index("et")
    tokens = res_hbm.shape[0]
    local = tokens // n_et
    head_dim = q_gain_hbm.shape[1]
    own_heads = w_q_hbm.shape[1] // head_dim
    n_heads = own_heads * n_et
    kv_heads = n_et // 2
    group = n_heads // kv_heads
    width = res_hbm.shape[1] * n_et
    n_local = w_gu_hbm.shape[0]
    slots = n_stream * n_local * CAP
    scale = head_dim**-0.5

    def et_peer(step):
        return lax.rem(me + step, n_et)

    def stream_peer(step):
        return lax.rem(me_s + step, n_stream)

    n_y, n_z, n_core = (2, n_stream // 4, 2) if n_stream % 4 == 0 else (1, 1, n_stream)
    y, z, core = lax.div(me_s, n_z * n_core), lax.rem(lax.div(me_s, n_core), n_z), lax.rem(me_s, n_core)

    def stream_at(dy, dz, dc):
        return (
            lax.rem(y + dy, n_y) * (n_z * n_core)
            + lax.rem(z + dz, n_z) * n_core
            + lax.rem(core + dc, n_core)
        )

    across = [(dy, 0, dc) for dy in range(n_y) for dc in range(n_core) if dy or dc]

    def along(reach):
        return [(0, dz, 0) for dz in sorted({reach % n_z, -reach % n_z} - {0})]

    rounds = []
    reach = 1
    while reach < n_z // 2:
        rounds.append(along(reach))
        reach *= 2
    rounds.append(across)

    def tell(number):
        for away in rounds[number] if number < len(rounds) else ():
            pl.semaphore_signal(
                known.at[number],
                inc=1,
                device_id=(stream_at(*away), me),
                device_id_type=MESH,
            )

    def hear(number):
        if number < len(rounds):
            pl.semaphore_wait(known.at[number], len(rounds[number]))

    def hops(away):
        return min(away[1], n_z - away[1]) + 2 * away[0]

    def back(away):
        return (-away[0] % n_y, -away[1] % n_z, -away[2] % n_core)

    relative = sorted(
        [(dy, dz, dc) for dy in range(n_y) for dz in range(n_z) for dc in range(n_core)],
        key=lambda away: (hops(away), away != (0, 0, 0)),
    )
    share = n_stream // WAVES
    waves = [
        sorted(relative[w * share : (w + 1) * share], key=lambda away: -hops(away))
        for w in range(WAVES)
    ]
    slot_of = {away: i for i, away in enumerate(waves[0] + waves[1])}
    at_home = slot_of[0, 0, 0]

    n_x = n_et // 2
    x, y_low = lax.div(me, 2), lax.rem(me, 2)
    et_far_first = [
        lax.rem(x + dx, n_x) * 2 + lax.rem(y_low + dy, 2)
        for dx in sorted(range(n_x), key=lambda i: -min(i, n_x - i))
        for dy in (1, 0)
        if dx or dy
    ]

    def et_copy(exchange, source, target, peer):
        return pltpu.make_async_remote_copy(
            src_ref=source,
            dst_ref=target,
            send_sem=et_send.at[exchange, peer],
            recv_sem=et_recv.at[exchange, me],
            device_id=(me_s, peer),
            device_id_type=MESH,
        )

    def et_arrival(exchange, source, target, peer):
        return pltpu.make_async_remote_copy(
            src_ref=source,
            dst_ref=target,
            send_sem=et_send.at[exchange, peer],
            recv_sem=et_recv.at[exchange, peer],
            device_id=(me_s, peer),
            device_id_type=MESH,
        )

    def stream_copy(exchange, source, target, away):
        return pltpu.make_async_remote_copy(
            src_ref=source,
            dst_ref=target,
            send_sem=stream_send.at[exchange, slot_of[away]],
            recv_sem=stream_recv.at[exchange, slot_of[back(away)]],
            device_id=(stream_at(*away), me),
            device_id_type=MESH,
        )

    def stream_arrival(exchange, source, target, away):
        return pltpu.make_async_remote_copy(
            src_ref=source,
            dst_ref=target,
            send_sem=stream_send.at[exchange, slot_of[away]],
            recv_sem=stream_recv.at[exchange, slot_of[away]],
            device_id=(stream_at(*away), me),
            device_id_type=MESH,
        )

    def others(wave):
        return [away for away in waves[wave] if away != (0, 0, 0)]

    def loop(n, body):
        def step(i, carry):
            body(i)
            return carry

        lax.fori_loop(1, n, step, 0)

    barrier = pltpu.get_barrier_semaphore()
    greeted = [(me_s, peer) for peer in et_far_first]
    greeted += [(stream_at(*away), me) for away in along(1) + across]
    for device in greeted:
        pl.semaphore_signal(barrier, inc=1, device_id=device, device_id_type=MESH)

    pl.semaphore_wait(barrier, len(greeted))

    for peer in et_far_first:
        et_copy(FEATURES, res_hbm, features.at[me], peer).start()
    tell(0)

    loads = {}

    def load(name, source, target):
        loads[name] = pltpu.make_async_copy(source, target, load_sem.at[len(loads)])
        loads[name].start()

    load("own", res_hbm, features.at[me])
    load("length", length_hbm, length)
    load("cache", cache_hbm, cache)
    load("w_q", w_q_hbm, w_q)
    load("w_kv", w_kv_hbm, w_kv)
    load("attn_gain", attn_gain_hbm, attn_gain)
    load("q_gain", q_gain_hbm, q_gain)
    load("key_gain", key_gain_hbm, key_gain)
    load("ids", ids_hbm, ids)
    load("gates", gates_hbm, gates)
    load("moe_gain", moe_gain_hbm, moe_gain)

    loads["length"].wait()
    lengths = jnp.broadcast_to(length[...], (tokens, tokens)).astype(F32)
    diagonal = iota((tokens, tokens), 0) == iota((tokens, tokens), 1)
    positions = jnp.sum(jnp.where(diagonal, lengths, 0.0), axis=1, keepdims=True)
    half = head_dim // 2
    lane = iota((tokens, head_dim), 1)
    steps = jnp.where(lane < half, lane, lane - half).astype(F32)
    angle = positions * jnp.exp(steps * (-2.0 * math.log(ROPE_BASE) / head_dim))
    cosine = jnp.cos(angle)
    sine = jnp.where(lane < half, -jnp.sin(angle), jnp.sin(angle))

    pad = 16
    row = iota((n_et * pad, LANES), 0)
    col = iota((n_et * pad, LANES), 1)
    peer_of, at = lax.div(row, pad), lax.rem(row, pad)
    n_q = local * own_heads
    picked = jnp.where(
        at < n_q,
        lax.rem(at, own_heads) * tokens + peer_of * local + lax.div(at, own_heads),
        jnp.where(
            at < n_q + local, own_heads * tokens + peer_of * local + at - n_q, -1
        ),
    )
    order_out = jnp.where(col == picked, 1.0, 0.0).astype(BF16)

    per = local * n_heads
    row = iota((3 * per, n_et * pad), 0)
    col = iota((3 * per, n_et * pad), 1)
    kind, at = lax.div(row, per), lax.rem(row, per)
    token, head = lax.div(at, n_heads), lax.rem(at, n_heads)
    picked = jnp.where(
        kind == 0,
        lax.div(head, own_heads) * pad + token * own_heads + lax.rem(head, own_heads),
        (lax.div(head, group) + jnp.where(kind == 2, kv_heads, 0)) * pad + n_q + token,
    )
    order_in = jnp.where(col == picked, 1.0, 0.0).astype(BF16)

    loads["ids"].wait()
    loads["gates"].wait()
    at = iota((slots, tokens), 0)
    place = lax.rem(at, n_local * CAP)
    expert = lax.div(at, n_local * CAP) * n_local + lax.rem(place, n_local)
    which = lax.div(place, n_local)
    gate = gates[...]
    gate = gate / jnp.sum(gate, axis=0, keepdims=True)
    named = jnp.zeros((slots, tokens), F32)
    weight = jnp.zeros((slots, tokens), F32)
    for k in range(ids_hbm.shape[0]):
        hit = expert == ids[k : k + 1, :]
        named = jnp.where(hit, 1.0, named)
        weight = jnp.where(hit, gate[k : k + 1, :], weight)
    before = jnp.where(
        iota((tokens, tokens), 0) < iota((tokens, tokens), 1), 1.0, 0.0
    ).astype(BF16)
    earlier = dot(named.astype(BF16), before)
    placed = jnp.where(earlier == which.astype(F32), named, 0.0)
    mixing = placed * weight
    placed = placed.astype(BF16)
    mixing_high = mixing.astype(BF16)
    mixing_low = (mixing - mixing_high.astype(F32)).astype(BF16)

    loads["cache"].wait()
    rows_of = cache_hbm.shape[0] // local
    span = rows_of // (2 * kv_heads)
    for t in range(local):
        cache_f[...] = cache[t * rows_of : (t + 1) * rows_of, :].astype(F32)
        for kind in range(2):
            for h in range(kv_heads):
                split[t, kind, h // 2, :, h % 2 * head_dim : (h % 2 + 1) * head_dim] = cache_f[
                    pl.ds(2 * h + kind, span, stride=2 * kv_heads), :
                ].astype(BF16)

    loads["own"].wait()
    loads["attn_gain"].wait()
    loop(
        n_et,
        lambda i: et_arrival(
            FEATURES, res_hbm, features.at[et_peer(i)], et_peer(i)
        ).wait_recv(),
    )
    full = jnp.concatenate([features[i].astype(F32) for i in range(n_et)], axis=1)
    gain = attn_gain[...].astype(F32)
    gain = jnp.concatenate([gain[i : i + 1] for i in range(gain.shape[0])], axis=1)
    normed = (
        full
        * lax.rsqrt(jnp.sum(full * full, axis=1, keepdims=True) * (1.0 / width) + EPS)
        * gain
    ).astype(BF16)

    def rotated(v, g):
        v = v * lax.rsqrt(jnp.mean(v * v, axis=1, keepdims=True) + EPS) * g
        return v * cosine + pltpu.roll(v, half, 1) * sine

    loads["q_gain"].wait()
    loads["key_gain"].wait()
    loads["w_q"].wait()
    query = dot(normed, w_q[...])
    loads["w_kv"].wait()
    key_value = dot(normed, w_kv[...])
    query_gain = q_gain[...].astype(F32)
    made = [
        rotated(query[:, i * head_dim : (i + 1) * head_dim], query_gain)
        for i in range(own_heads)
    ]
    made.append(
        jnp.where(me < kv_heads, rotated(key_value, key_gain[...].astype(F32)), key_value)
    )
    made.append(jnp.zeros((LANES - (own_heads + 1) * tokens, head_dim), F32))
    made = jnp.concatenate(made, axis=0).astype(BF16)
    heads_out[...] = dot(order_out, made).astype(BF16).reshape(heads_out.shape)
    heads_in[me] = heads_out[me]
    for peer in et_far_first:
        et_copy(HEADS, heads_out.at[peer], heads_in.at[me], peer).start()
    hear(0)
    tell(1)
    load("w_o", w_o_hbm, w_o)
    load("w_gu", w_gu_hbm, w_gu)
    load("w_down", w_down_hbm, w_down)

    own_lane = iota((1, tokens), 1)
    lengths = length[...].astype(F32)
    pairs = kv_heads // 2
    column = iota((2 * group, span), 1)
    live = []
    for t in range(local):
        limit = jnp.sum(
            jnp.where(own_lane == me * local + t, lengths, 0.0), axis=1, keepdims=True
        ).astype(jnp.int32)
        live.append(column < limit)
    empty = jnp.zeros((group, head_dim), F32)
    loop(
        n_et,
        lambda i: et_arrival(
            HEADS, heads_out.at[et_peer(i)], heads_in.at[et_peer(i)], et_peer(i)
        ).wait_recv(),
    )
    ordered = dot(order_in, heads_in[...].reshape(n_et * pad, head_dim))
    q = ordered[:per]
    blocks = []
    for i in range(local * pairs):
        at = i * 2 * group
        upper = jnp.concatenate([q[at : at + group], empty], axis=1)
        lower = jnp.concatenate([empty, q[at + group : at + 2 * group]], axis=1)
        blocks.append(jnp.concatenate([upper, lower], axis=0).astype(BF16))
    scores = [
        dot_nt(block, split[i // pairs, 0, i % pairs]) for i, block in enumerate(blocks)
    ]
    weights = [
        jnp.where(live[i // pairs], jnp.exp(score * scale), 0.0)
        for i, score in enumerate(scores)
    ]
    summed = [
        dot(weight.astype(BF16), split[i // pairs, 1, i % pairs])
        for i, weight in enumerate(weights)
    ]
    fresh = jnp.exp(jnp.sum(q * ordered[per : 2 * per], axis=1, keepdims=True) * scale)
    total = fresh + jnp.concatenate(
        [jnp.sum(weight, axis=1, keepdims=True) for weight in weights], axis=0
    )
    summed = jnp.concatenate(
        [
            part
            for both in summed
            for part in (both[:group, :head_dim], both[group:, head_dim:])
        ],
        axis=0,
    )
    mixed_out[...] = ((summed + fresh * ordered[2 * per :]) / total).astype(BF16)
    mixed_in[me] = mixed_out[...]
    for peer in et_far_first:
        et_copy(MIXED, mixed_out, mixed_in.at[me], peer).start()
    hear(1)
    tell(2)

    loads["w_o"].wait()
    loop(
        n_et,
        lambda i: et_arrival(
            MIXED, mixed_out, mixed_in.at[et_peer(i)], et_peer(i)
        ).wait_recv(),
    )
    mixed_f[...] = mixed_in[...].reshape(tokens * n_heads, head_dim).astype(F32)
    attended = jnp.concatenate(
        [mixed_f[pl.ds(h, tokens, stride=n_heads), :] for h in range(n_heads)], axis=1
    ).astype(BF16)
    resid = (features[me].astype(F32) + dot(attended, w_o[...])).astype(BF16)

    sent = dot(placed, resid)
    sent = sent.reshape(n_stream, n_local * CAP, 2 * LANES)
    rows_out[...] = jnp.concatenate(
        [sent[:, :, :LANES], sent[:, :, LANES:]], axis=1
    ).astype(BF16)
    rows_in[at_home] = rows_out[me_s]
    hear(2)
    for w in range(WAVES):
        for away in others(w):
            stream_copy(
                OUTWARD,
                rows_out.at[stream_at(*away)],
                rows_in.at[slot_of[back(away)]],
                away,
            ).start()
    loads["moe_gain"].wait()
    gain = moe_gain[...].astype(F32)
    gain = jnp.concatenate([gain[0:1], gain[1:2]], axis=1)
    loads["w_gu"].wait()
    chunk = 2 * n_local * CAP
    hidden_width = w_down_hbm.shape[1]

    for w in range(WAVES):
        for away in others(w):
            stream_arrival(
                OUTWARD, rows_out.at[0], rows_in.at[slot_of[away]], away
            ).wait_recv()
        rows_f[w * share * chunk : (w + 1) * share * chunk, :] = (
            rows_in[w * share : (w + 1) * share].reshape(share * chunk, LANES).astype(F32)
        )
        for j in range(n_local):
            taken = []
            for c in range(CAP):
                first = w * share * chunk + c * n_local + j
                taken.append(
                    jnp.concatenate(
                        [
                            rows_f[pl.ds(first + h * n_local * CAP, share, stride=chunk), :]
                            for h in range(2)
                        ],
                        axis=1,
                    )
                )
            taken = jnp.concatenate(taken, axis=0)
            squares = jnp.sum(taken * taken, axis=1, keepdims=True)
            high = squares.astype(BF16).astype(F32)
            expert_squares[w, j] = jnp.where(
                iota((CAP * share, LANES), 1) < LANES // 2, high, squares - high
            )
            expert_rows[w, j] = (taken * gain).astype(BF16)
        for i in range(n_local):
            j = lax.rem(lax.div(me, CAP) + (2, 1, 3, 0)[i], n_local)
            taken = expert_rows[w, j]
            products = jnp.concatenate(
                [dot(taken, w_gu[j, 0]), dot(taken, w_gu[j, 1]), expert_squares[w, j]], axis=1
            )
            pairs_out[w, i] = products.astype(BF16).reshape(pairs_out.shape[2:])
            if i < n_local - 1:
                for c in range(CAP):
                    et_copy(
                        PAIRS + w, pairs_out.at[w, i, c], pairs_in.at[w, me], CAP * j + c
                    ).start()
            else:
                pairs_own[w] = products.reshape(pairs_own.shape[1:])
                c = 1 - lax.rem(me, CAP)
                et_copy(
                    PAIRS + w, pairs_out.at[w, i, c], pairs_in.at[w, me], CAP * j + c
                ).start()
    for w in range(WAVES):
        pair = pairs_own[w, lax.rem(me, CAP)]
        for i in range(1, n_et):
            et_arrival(
                PAIRS + w, pairs_out.at[w, 0, 0], pairs_in.at[w, et_peer(i)], et_peer(i)
            ).wait_recv()
            pair = pair + pairs_in[w, et_peer(i)].astype(F32)
        squares = jnp.sum(pair[:, 2 * hidden_width :], axis=1, keepdims=True) * (
            2.0 / LANES / width
        )
        level = lax.rsqrt(squares + EPS)
        first = pair[:, :hidden_width] * level
        second = pair[:, hidden_width : 2 * hidden_width] * level
        hidden_out[w] = (first / (1.0 + jnp.exp(-first)) * second).astype(BF16)
        for peer in et_far_first:
            et_copy(HIDDEN + w, hidden_out.at[w], hidden_in.at[w, me], peer).start()
        hidden_in[w, me] = hidden_out[w]

    loads["w_down"].wait()
    for w in range(WAVES):
        loop(
            n_et,
            lambda i: et_arrival(
                HIDDEN + w, hidden_out.at[w], hidden_in.at[w, et_peer(i)], et_peer(i)
            ).wait_recv(),
        )
        for j in range(n_local):
            hidden = hidden_in[w, CAP * j : CAP * (j + 1)].reshape(CAP * share, hidden_width)
            result = dot(hidden, w_down[j])
            for c in range(CAP):
                for h in range(2):
                    first = w * share * chunk + h * n_local * CAP + c * n_local + j
                    results_f[pl.ds(first, share, stride=chunk), :] = result[
                        c * share : (c + 1) * share, h * LANES : (h + 1) * LANES
                    ]
        results_out[w * share : (w + 1) * share] = (
            results_f[w * share * chunk : (w + 1) * share * chunk, :]
            .astype(BF16)
            .reshape(share, chunk, LANES)
        )
        for away in others(w):
            stream_copy(
                HOME, results_out.at[slot_of[away]], results_in.at[me_s], away
            ).start()
    results_in[me_s] = results_out[at_home]

    def sent_et(exchange, source, target):
        loop(
            n_et,
            lambda i: et_copy(exchange, source, target, et_peer(i)).wait_send(),
        )

    sent_et(FEATURES, res_hbm, features.at[me])
    sent_et(HEADS, heads_out.at[0], heads_in.at[me])
    sent_et(MIXED, mixed_out, mixed_in.at[me])
    for w in range(WAVES):
        sent_et(PAIRS + w, pairs_out.at[w, 0, 0], pairs_in.at[w, me])
        sent_et(HIDDEN + w, hidden_out.at[w], hidden_in.at[w, me])
        for away in others(w):
            stream_copy(OUTWARD, rows_out.at[0], rows_in.at[0], away).wait_send()
            stream_copy(HOME, results_out.at[0], results_in.at[0], away).wait_send()

    for w in range(WAVES):
        for away in others(w):
            stream_arrival(
                HOME, results_out.at[0], results_in.at[stream_at(*away)], away
            ).wait_recv()
    returned = results_in[...].astype(F32)
    returned = (
        jnp.concatenate(
            [returned[:, : n_local * CAP], returned[:, n_local * CAP :]], axis=2
        )
        .reshape(slots, 2 * LANES)
        .astype(BF16)
    )
    routed = dot_tn(mixing_high, returned) + dot_tn(mixing_low, returned)
    out_ref[...] = (resid.astype(F32) + routed).astype(BF16)


def on_device(
    n_stream,
    n_et,
    residual_in,
    attn_gain,
    q_gain,
    key_norm_gain,
    w_q,
    key_value_weight,
    w_o,
    key_value_cache,
    cache_length,
    moe_gain,
    route_ids,
    route_gates,
    w_gate_up,
    w_down,
):
    tokens, features = residual_in.shape
    head_dim = q_gain.shape[0]
    local, span, _, kv_width = key_value_cache.shape
    kv_heads = kv_width // head_dim
    n_heads = w_q.shape[1] // head_dim * n_et
    n_local = w_gate_up.shape[0]
    hidden = w_down.shape[1]
    cache = (
        key_value_cache.reshape(local, span, 2, kv_heads, head_dim)
        .transpose(0, 1, 3, 2, 4)
        .reshape(local * span * kv_heads * 2, head_dim)
    )
    args = (
        residual_in,
        attn_gain.reshape(-1, LANES),
        q_gain.reshape(1, -1),
        key_norm_gain.reshape(1, -1),
        w_q,
        key_value_weight,
        w_o,
        cache,
        cache_length.reshape(1, -1),
        moe_gain.reshape(-1, LANES),
        route_ids.T,
        route_gates.T,
        w_gate_up,
        w_down,
    )
    chunk = 2 * n_local * CAP
    vmem = pltpu.VMEM
    row_blocks = (n_stream, chunk, LANES)
    flat_rows = (n_stream * chunk, LANES)
    pair_width = 2 * hidden + LANES
    share = n_stream // WAVES
    scratch = [vmem(a.shape, a.dtype) for a in args[1:]] + [
        vmem((span * kv_heads * 2, head_dim), F32),
        vmem((local, 2, kv_heads // 2, span, 2 * head_dim), BF16),
        vmem((n_et, tokens, features), BF16),
        vmem((n_et, 16, head_dim), BF16),
        vmem((n_et, 16, head_dim), BF16),
        vmem((local * n_heads, head_dim), BF16),
        vmem((n_et, local * n_heads, head_dim), BF16),
        vmem((tokens * n_heads, head_dim), F32),
        vmem(row_blocks, BF16),
        vmem(row_blocks, BF16),
        vmem(flat_rows, F32),
        vmem((WAVES, n_local, CAP * share, features), BF16),
        vmem((WAVES, n_local, CAP * share, LANES), F32),
        vmem((WAVES, n_local, CAP, share, pair_width), BF16),
        vmem((WAVES, CAP, share, pair_width), F32),
        vmem((WAVES, n_et, share, pair_width), BF16),
        vmem((WAVES, share, hidden), BF16),
        vmem((WAVES, n_et, share, hidden), BF16),
        vmem(flat_rows, F32),
        vmem(row_blocks, BF16),
        vmem(row_blocks, BF16),
        pltpu.SemaphoreType.DMA((len(args),)),
        pltpu.SemaphoreType.DMA((7, n_et)),
        pltpu.SemaphoreType.DMA((7, n_et)),
        pltpu.SemaphoreType.DMA((2, n_stream)),
        pltpu.SemaphoreType.DMA((2, n_stream)),
        pltpu.SemaphoreType.REGULAR((3,)),
    ]
    return pl.pallas_call(
        functools.partial(kernel, n_stream, n_et),
        out_shape=pltpu.VMEM(residual_in.shape, residual_in.dtype),
        in_specs=[pl.BlockSpec(memory_space=pl.ANY)] * len(args),
        out_specs=pl.BlockSpec(memory_space=pltpu.VMEM),
        scratch_shapes=scratch,
        compiler_params=pltpu.CompilerParams(
            collective_id=0, has_side_effects=True, vmem_limit_bytes=56 * 1024 * 1024
        ),
    )(*args)


def solution(mesh):
    placed = (
        P("stream", "et"),
        P(),
        P(),
        P(),
        P(None, "et"),
        P(None, "et"),
        P(None, "et"),
        P(("stream", "et"), None, None, None),
        P("stream"),
        P("et"),
        P("stream", None),
        P("stream", None),
        P("stream", None, "et", None),
        P("stream", None, "et"),
    )
    return jax.shard_map(
        functools.partial(on_device, mesh.shape["stream"], mesh.shape["et"]),
        mesh=mesh,
        in_specs=placed,
        out_specs=P("stream", "et"),
        check_vma=False,
    )
```

```python
import functools
import math

import jax
import jax.numpy as jnp
from jax import lax
from jax.experimental import pallas as pl
from jax.experimental.pallas import tpu as pltpu
from jax.sharding import PartitionSpec as P

EPS = 1e-06
ROPE_BASE = 1000000.0
CAP = 2
LANES = 128
MESH = pl.DeviceIdType.MESH
F32 = jnp.float32
BF16 = jnp.bfloat16

FEATURES, HEADS, MIXED, PAIRS, HIDDEN = 0, 1, 2, 3, 5
OUTWARD, HOME = range(2)
WAVES = 2


def iota(shape, dim):
    return lax.broadcasted_iota(jnp.int32, shape, dim)


def dot(a, b):
    return jnp.dot(a, b, preferred_element_type=F32)


def dot_nt(a, b):
    return lax.dot_general(a, b, (((1,), (1,)), ((), ())), preferred_element_type=F32)


def dot_tn(a, b):
    return lax.dot_general(a, b, (((0,), (0,)), ((), ())), preferred_element_type=F32)


def kernel(
    n_stream,
    n_et,
    res_hbm,
    attn_gain_hbm,
    q_gain_hbm,
    key_gain_hbm,
    w_q_hbm,
    w_kv_hbm,
    w_o_hbm,
    cache_hbm,
    length_hbm,
    moe_gain_hbm,
    ids_hbm,
    gates_hbm,
    w_gu_hbm,
    w_down_hbm,
    out_ref,
    attn_gain,
    q_gain,
    key_gain,
    w_q,
    w_kv,
    w_o,
    cache,
    length,
    moe_gain,
    ids,
    gates,
    w_gu,
    w_down,
    cache_f,
    split,
    features,
    heads_out,
    heads_in,
    mixed_out,
    mixed_in,
    mixed_f,
    rows_out,
    rows_in,
    rows_f,
    expert_rows,
    expert_squares,
    pairs_out,
    pairs_own,
    pairs_in,
    hidden_out,
    hidden_in,
    results_f,
    results_out,
    results_in,
    load_sem,
    et_send,
    et_recv,
    stream_send,
    stream_recv,
    known,
):
    me_s = lax.axis_index("stream")
    me = lax.axis_index("et")
    tokens = res_hbm.shape[0]
    local = tokens // n_et
    head_dim = q_gain_hbm.shape[1]
    own_heads = w_q_hbm.shape[1] // head_dim
    n_heads = own_heads * n_et
    kv_heads = n_et // 2
    group = n_heads // kv_heads
    width = res_hbm.shape[1] * n_et
    n_local = w_gu_hbm.shape[0]
    slots = n_stream * n_local * CAP
    scale = head_dim**-0.5

    def et_peer(step):
        return lax.rem(me + step, n_et)

    def stream_peer(step):
        return lax.rem(me_s + step, n_stream)

    n_y, n_z, n_core = (2, n_stream // 4, 2) if n_stream % 4 == 0 else (1, 1, n_stream)
    y, z, core = lax.div(me_s, n_z * n_core), lax.rem(lax.div(me_s, n_core), n_z), lax.rem(me_s, n_core)

    def stream_at(dy, dz, dc):
        return (
            lax.rem(y + dy, n_y) * (n_z * n_core)
            + lax.rem(z + dz, n_z) * n_core
            + lax.rem(core + dc, n_core)
        )

    across = [(dy, 0, dc) for dy in range(n_y) for dc in range(n_core) if dy or dc]

    def along(reach):
        return [(0, dz, 0) for dz in sorted({reach % n_z, -reach % n_z} - {0})]

    rounds = []
    reach = 1
    while reach < n_z // 2:
        rounds.append(along(reach))
        reach *= 2
    rounds.append(across)

    def tell(number):
        for away in rounds[number] if number < len(rounds) else ():
            pl.semaphore_signal(
                known.at[number],
                inc=1,
                device_id=(stream_at(*away), me),
                device_id_type=MESH,
            )

    def hear(number):
        if number < len(rounds):
            pl.semaphore_wait(known.at[number], len(rounds[number]))

    def hops(away):
        return min(away[1], n_z - away[1]) + 2 * away[0]

    def back(away):
        return (-away[0] % n_y, -away[1] % n_z, -away[2] % n_core)

    relative = sorted(
        [(dy, dz, dc) for dy in range(n_y) for dz in range(n_z) for dc in range(n_core)],
        key=lambda away: (hops(away), away != (0, 0, 0)),
    )
    share = n_stream // WAVES
    waves = [
        sorted(relative[w * share : (w + 1) * share], key=lambda away: -hops(away))
        for w in range(WAVES)
    ]
    slot_of = {away: i for i, away in enumerate(waves[0] + waves[1])}
    at_home = slot_of[0, 0, 0]

    n_x = n_et // 2
    x, y_low = lax.div(me, 2), lax.rem(me, 2)
    et_far_first = [
        lax.rem(x + dx, n_x) * 2 + lax.rem(y_low + dy, 2)
        for dx in sorted(range(n_x), key=lambda i: -min(i, n_x - i))
        for dy in (1, 0)
        if dx or dy
    ]

    def et_copy(exchange, source, target, peer):
        return pltpu.make_async_remote_copy(
            src_ref=source,
            dst_ref=target,
            send_sem=et_send.at[exchange, peer],
            recv_sem=et_recv.at[exchange, me],
            device_id=(me_s, peer),
            device_id_type=MESH,
        )

    def et_arrival(exchange, source, target, peer):
        return pltpu.make_async_remote_copy(
            src_ref=source,
            dst_ref=target,
            send_sem=et_send.at[exchange, peer],
            recv_sem=et_recv.at[exchange, peer],
            device_id=(me_s, peer),
            device_id_type=MESH,
        )

    def stream_copy(exchange, source, target, away):
        return pltpu.make_async_remote_copy(
            src_ref=source,
            dst_ref=target,
            send_sem=stream_send.at[exchange, slot_of[away]],
            recv_sem=stream_recv.at[exchange, slot_of[back(away)]],
            device_id=(stream_at(*away), me),
            device_id_type=MESH,
        )

    def stream_arrival(exchange, source, target, away):
        return pltpu.make_async_remote_copy(
            src_ref=source,
            dst_ref=target,
            send_sem=stream_send.at[exchange, slot_of[away]],
            recv_sem=stream_recv.at[exchange, slot_of[away]],
            device_id=(stream_at(*away), me),
            device_id_type=MESH,
        )

    def others(wave):
        return [away for away in waves[wave] if away != (0, 0, 0)]

    def loop(n, body):
        def step(i, carry):
            body(i)
            return carry

        lax.fori_loop(1, n, step, 0)

    barrier = pltpu.get_barrier_semaphore()
    greeted = [(me_s, peer) for peer in et_far_first]
    greeted += [(stream_at(*away), me) for away in along(1) + across]
    for device in greeted:
        pl.semaphore_signal(barrier, inc=1, device_id=device, device_id_type=MESH)

    pl.semaphore_wait(barrier, len(greeted))

    for peer in et_far_first:
        et_copy(FEATURES, res_hbm, features.at[me], peer).start()
    tell(0)

    loads = {}

    def load(name, source, target):
        loads[name] = pltpu.make_async_copy(source, target, load_sem.at[len(loads)])
        loads[name].start()

    load("own", res_hbm, features.at[me])
    load("length", length_hbm, length)
    load("w_q", w_q_hbm, w_q)
    load("w_kv", w_kv_hbm, w_kv)
    load("attn_gain", attn_gain_hbm, attn_gain)
    load("q_gain", q_gain_hbm, q_gain)
    load("key_gain", key_gain_hbm, key_gain)
    load("cache", cache_hbm, cache)

    loads["length"].wait()
    lengths = jnp.broadcast_to(length[...], (tokens, tokens)).astype(F32)
    diagonal = iota((tokens, tokens), 0) == iota((tokens, tokens), 1)
    positions = jnp.sum(jnp.where(diagonal, lengths, 0.0), axis=1, keepdims=True)
    half = head_dim // 2
    lane = iota((tokens, head_dim), 1)
    steps = jnp.where(lane < half, lane, lane - half).astype(F32)
    angle = positions * jnp.exp(steps * (-2.0 * math.log(ROPE_BASE) / head_dim))
    cosine = jnp.cos(angle)
    sine = jnp.where(lane < half, -jnp.sin(angle), jnp.sin(angle))

    pad = 16
    row = iota((n_et * pad, LANES), 0)
    col = iota((n_et * pad, LANES), 1)
    peer_of, at = lax.div(row, pad), lax.rem(row, pad)
    n_q = local * own_heads
    picked = jnp.where(
        at < n_q,
        lax.rem(at, own_heads) * tokens + peer_of * local + lax.div(at, own_heads),
        jnp.where(
            at < n_q + local, own_heads * tokens + peer_of * local + at - n_q, -1
        ),
    )
    order_out = jnp.where(col == picked, 1.0, 0.0).astype(BF16)

    loads["own"].wait()
    loads["attn_gain"].wait()
    loop(
        n_et,
        lambda i: et_arrival(
            FEATURES, res_hbm, features.at[et_peer(i)], et_peer(i)
        ).wait_recv(),
    )
    full = jnp.concatenate([features[i].astype(F32) for i in range(n_et)], axis=1)
    gain = attn_gain[...].astype(F32)
    gain = jnp.concatenate([gain[i : i + 1] for i in range(gain.shape[0])], axis=1)
    normed = (
        full
        * lax.rsqrt(jnp.sum(full * full, axis=1, keepdims=True) * (1.0 / width) + EPS)
        * gain
    ).astype(BF16)

    def rotated(v, g):
        v = v * lax.rsqrt(jnp.mean(v * v, axis=1, keepdims=True) + EPS) * g
        return v * cosine + pltpu.roll(v, half, 1) * sine

    loads["q_gain"].wait()
    loads["key_gain"].wait()
    loads["w_q"].wait()
    query = dot(normed, w_q[...])
    loads["w_kv"].wait()
    key_value = dot(normed, w_kv[...])
    query_gain = q_gain[...].astype(F32)
    made = [
        rotated(query[:, i * head_dim : (i + 1) * head_dim], query_gain)
        for i in range(own_heads)
    ]
    made.append(
        jnp.where(me < kv_heads, rotated(key_value, key_gain[...].astype(F32)), key_value)
    )
    made.append(jnp.zeros((LANES - (own_heads + 1) * tokens, head_dim), F32))
    made = jnp.concatenate(made, axis=0).astype(BF16)
    heads_out[...] = dot(order_out, made).astype(BF16).reshape(heads_out.shape)
    heads_in[me] = heads_out[me]
    for peer in et_far_first:
        et_copy(HEADS, heads_out.at[peer], heads_in.at[me], peer).start()
    hear(0)
    tell(1)
    load("w_o", w_o_hbm, w_o)
    load("ids", ids_hbm, ids)
    load("gates", gates_hbm, gates)
    load("moe_gain", moe_gain_hbm, moe_gain)
    load("w_gu", w_gu_hbm, w_gu)
    load("w_down", w_down_hbm, w_down)

    per = local * n_heads
    row = iota((3 * per, n_et * pad), 0)
    col = iota((3 * per, n_et * pad), 1)
    kind, at = lax.div(row, per), lax.rem(row, per)
    token, head = lax.div(at, n_heads), lax.rem(at, n_heads)
    picked = jnp.where(
        kind == 0,
        lax.div(head, own_heads) * pad + token * own_heads + lax.rem(head, own_heads),
        (lax.div(head, group) + jnp.where(kind == 2, kv_heads, 0)) * pad + n_q + token,
    )
    order_in = jnp.where(col == picked, 1.0, 0.0).astype(BF16)

    loads["cache"].wait()
    rows_of = cache_hbm.shape[0] // local
    span = rows_of // (2 * kv_heads)
    for t in range(local):
        cache_f[...] = cache[t * rows_of : (t + 1) * rows_of, :].astype(F32)
        for kind in range(2):
            for h in range(kv_heads):
                split[t, kind, h // 2, :, h % 2 * head_dim : (h % 2 + 1) * head_dim] = cache_f[
                    pl.ds(2 * h + kind, span, stride=2 * kv_heads), :
                ].astype(BF16)

    own_lane = iota((1, tokens), 1)
    lengths = length[...].astype(F32)
    pairs = kv_heads // 2
    column = iota((2 * group, span), 1)
    live = []
    for t in range(local):
        limit = jnp.sum(
            jnp.where(own_lane == me * local + t, lengths, 0.0), axis=1, keepdims=True
        ).astype(jnp.int32)
        live.append(column < limit)
    empty = jnp.zeros((group, head_dim), F32)
    loop(
        n_et,
        lambda i: et_arrival(
            HEADS, heads_out.at[et_peer(i)], heads_in.at[et_peer(i)], et_peer(i)
        ).wait_recv(),
    )
    ordered = dot(order_in, heads_in[...].reshape(n_et * pad, head_dim))
    q = ordered[:per]
    blocks = []
    for i in range(local * pairs):
        at = i * 2 * group
        upper = jnp.concatenate([q[at : at + group], empty], axis=1)
        lower = jnp.concatenate([empty, q[at + group : at + 2 * group]], axis=1)
        blocks.append(jnp.concatenate([upper, lower], axis=0).astype(BF16))
    scores = [
        dot_nt(block, split[i // pairs, 0, i % pairs]) for i, block in enumerate(blocks)
    ]
    weights = [
        jnp.where(live[i // pairs], jnp.exp(score * scale), 0.0)
        for i, score in enumerate(scores)
    ]
    summed = [
        dot(weight.astype(BF16), split[i // pairs, 1, i % pairs])
        for i, weight in enumerate(weights)
    ]
    fresh = jnp.exp(jnp.sum(q * ordered[per : 2 * per], axis=1, keepdims=True) * scale)
    total = fresh + jnp.concatenate(
        [jnp.sum(weight, axis=1, keepdims=True) for weight in weights], axis=0
    )
    summed = jnp.concatenate(
        [
            part
            for both in summed
            for part in (both[:group, :head_dim], both[group:, head_dim:])
        ],
        axis=0,
    )
    mixed_out[...] = ((summed + fresh * ordered[2 * per :]) / total).astype(BF16)
    mixed_in[me] = mixed_out[...]
    for peer in et_far_first:
        et_copy(MIXED, mixed_out, mixed_in.at[me], peer).start()
    hear(1)
    tell(2)

    loads["ids"].wait()
    loads["gates"].wait()
    at = iota((slots, tokens), 0)
    place = lax.rem(at, n_local * CAP)
    expert = lax.div(at, n_local * CAP) * n_local + lax.rem(place, n_local)
    which = lax.div(place, n_local)
    gate = gates[...]
    gate = gate / jnp.sum(gate, axis=0, keepdims=True)
    named = jnp.zeros((slots, tokens), F32)
    weight = jnp.zeros((slots, tokens), F32)
    for k in range(ids_hbm.shape[0]):
        hit = expert == ids[k : k + 1, :]
        named = jnp.where(hit, 1.0, named)
        weight = jnp.where(hit, gate[k : k + 1, :], weight)
    before = jnp.where(
        iota((tokens, tokens), 0) < iota((tokens, tokens), 1), 1.0, 0.0
    ).astype(BF16)
    earlier = dot(named.astype(BF16), before)
    placed = jnp.where(earlier == which.astype(F32), named, 0.0)
    mixing = placed * weight
    placed = placed.astype(BF16)
    mixing_high = mixing.astype(BF16)
    mixing_low = (mixing - mixing_high.astype(F32)).astype(BF16)

    loads["w_o"].wait()
    loop(
        n_et,
        lambda i: et_arrival(
            MIXED, mixed_out, mixed_in.at[et_peer(i)], et_peer(i)
        ).wait_recv(),
    )
    mixed_f[...] = mixed_in[...].reshape(tokens * n_heads, head_dim).astype(F32)
    attended = jnp.concatenate(
        [mixed_f[pl.ds(h, tokens, stride=n_heads), :] for h in range(n_heads)], axis=1
    ).astype(BF16)
    resid = (features[me].astype(F32) + dot(attended, w_o[...])).astype(BF16)

    sent = dot(placed, resid)
    sent = sent.reshape(n_stream, n_local * CAP, 2 * LANES)
    rows_out[...] = jnp.concatenate(
        [sent[:, :, :LANES], sent[:, :, LANES:]], axis=1
    ).astype(BF16)
    rows_in[at_home] = rows_out[me_s]
    hear(2)
    for w in range(WAVES):
        for away in others(w):
            stream_copy(
                OUTWARD,
                rows_out.at[stream_at(*away)],
                rows_in.at[slot_of[back(away)]],
                away,
            ).start()
    loads["moe_gain"].wait()
    gain = moe_gain[...].astype(F32)
    gain = jnp.concatenate([gain[0:1], gain[1:2]], axis=1)
    loads["w_gu"].wait()
    chunk = 2 * n_local * CAP
    hidden_width = w_down_hbm.shape[1]

    for w in range(WAVES):
        for away in others(w):
            stream_arrival(
                OUTWARD, rows_out.at[0], rows_in.at[slot_of[away]], away
            ).wait_recv()
        rows_f[w * share * chunk : (w + 1) * share * chunk, :] = (
            rows_in[w * share : (w + 1) * share].reshape(share * chunk, LANES).astype(F32)
        )
        for j in range(n_local):
            taken = []
            for c in range(CAP):
                first = w * share * chunk + c * n_local + j
                taken.append(
                    jnp.concatenate(
                        [
                            rows_f[pl.ds(first + h * n_local * CAP, share, stride=chunk), :]
                            for h in range(2)
                        ],
                        axis=1,
                    )
                )
            taken = jnp.concatenate(taken, axis=0)
            squares = jnp.sum(taken * taken, axis=1, keepdims=True)
            high = squares.astype(BF16).astype(F32)
            expert_squares[w, j] = jnp.where(
                iota((CAP * share, LANES), 1) < LANES // 2, high, squares - high
            )
            expert_rows[w, j] = (taken * gain).astype(BF16)
        for i in range(n_local):
            j = lax.rem(lax.div(me, CAP) + (2, 1, 3, 0)[i], n_local)
            taken = expert_rows[w, j]
            products = jnp.concatenate(
                [dot(taken, w_gu[j, 0]), dot(taken, w_gu[j, 1]), expert_squares[w, j]], axis=1
            )
            pairs_out[w, i] = products.astype(BF16).reshape(pairs_out.shape[2:])
            if i < n_local - 1:
                for c in (y_low, 1 - y_low):
                    et_copy(
                        PAIRS + w, pairs_out.at[w, i, c], pairs_in.at[w, me], CAP * j + c
                    ).start()
            else:
                pairs_own[w] = products.reshape(pairs_own.shape[1:])
                c = 1 - lax.rem(me, CAP)
                et_copy(
                    PAIRS + w, pairs_out.at[w, i, c], pairs_in.at[w, me], CAP * j + c
                ).start()
    for w in range(WAVES):
        pair = pairs_own[w, lax.rem(me, CAP)]
        for i in range(1, n_et):
            et_arrival(
                PAIRS + w, pairs_out.at[w, 0, 0], pairs_in.at[w, et_peer(i)], et_peer(i)
            ).wait_recv()
            pair = pair + pairs_in[w, et_peer(i)].astype(F32)
        squares = jnp.sum(pair[:, 2 * hidden_width :], axis=1, keepdims=True) * (
            2.0 / LANES / width
        )
        level = lax.rsqrt(squares + EPS)
        first = pair[:, :hidden_width] * level
        second = pair[:, hidden_width : 2 * hidden_width] * level
        hidden_out[w] = (first / (1.0 + jnp.exp(-first)) * second).astype(BF16)
        for peer in et_far_first:
            et_copy(HIDDEN + w, hidden_out.at[w], hidden_in.at[w, me], peer).start()
        hidden_in[w, me] = hidden_out[w]

    loads["w_down"].wait()
    for w in range(WAVES):
        loop(
            n_et,
            lambda i: et_arrival(
                HIDDEN + w, hidden_out.at[w], hidden_in.at[w, et_peer(i)], et_peer(i)
            ).wait_recv(),
        )
        for j in range(n_local):
            hidden = hidden_in[w, CAP * j : CAP * (j + 1)].reshape(CAP * share, hidden_width)
            result = dot(hidden, w_down[j])
            for c in range(CAP):
                for h in range(2):
                    first = w * share * chunk + h * n_local * CAP + c * n_local + j
                    results_f[pl.ds(first, share, stride=chunk), :] = result[
                        c * share : (c + 1) * share, h * LANES : (h + 1) * LANES
                    ]
        results_out[w * share : (w + 1) * share] = (
            results_f[w * share * chunk : (w + 1) * share * chunk, :]
            .astype(BF16)
            .reshape(share, chunk, LANES)
        )
        for away in others(w):
            stream_copy(
                HOME, results_out.at[slot_of[away]], results_in.at[me_s], away
            ).start()
    results_in[me_s] = results_out[at_home]

    def sent_et(exchange, source, target):
        loop(
            n_et,
            lambda i: et_copy(exchange, source, target, et_peer(i)).wait_send(),
        )

    sent_et(FEATURES, res_hbm, features.at[me])
    sent_et(HEADS, heads_out.at[0], heads_in.at[me])
    sent_et(MIXED, mixed_out, mixed_in.at[me])
    for w in range(WAVES):
        sent_et(PAIRS + w, pairs_out.at[w, 0, 0], pairs_in.at[w, me])
        sent_et(HIDDEN + w, hidden_out.at[w], hidden_in.at[w, me])
        for away in others(w):
            stream_copy(OUTWARD, rows_out.at[0], rows_in.at[0], away).wait_send()
            stream_copy(HOME, results_out.at[0], results_in.at[0], away).wait_send()

    for w in range(WAVES):
        for away in others(w):
            stream_arrival(
                HOME, results_out.at[0], results_in.at[stream_at(*away)], away
            ).wait_recv()
    returned = results_in[...].astype(F32)
    returned = (
        jnp.concatenate(
            [returned[:, : n_local * CAP], returned[:, n_local * CAP :]], axis=2
        )
        .reshape(slots, 2 * LANES)
        .astype(BF16)
    )
    routed = dot_tn(mixing_high, returned) + dot_tn(mixing_low, returned)
    out_ref[...] = (resid.astype(F32) + routed).astype(BF16)


def on_device(
    n_stream,
    n_et,
    residual_in,
    attn_gain,
    q_gain,
    key_norm_gain,
    w_q,
    key_value_weight,
    w_o,
    key_value_cache,
    cache_length,
    moe_gain,
    route_ids,
    route_gates,
    w_gate_up,
    w_down,
):
    tokens, features = residual_in.shape
    head_dim = q_gain.shape[0]
    local, span, _, kv_width = key_value_cache.shape
    kv_heads = kv_width // head_dim
    n_heads = w_q.shape[1] // head_dim * n_et
    n_local = w_gate_up.shape[0]
    hidden = w_down.shape[1]
    cache = (
        key_value_cache.reshape(local, span, 2, kv_heads, head_dim)
        .transpose(0, 1, 3, 2, 4)
        .reshape(local * span * kv_heads * 2, head_dim)
    )
    args = (
        residual_in,
        attn_gain.reshape(-1, LANES),
        q_gain.reshape(1, -1),
        key_norm_gain.reshape(1, -1),
        w_q,
        key_value_weight,
        w_o,
        cache,
        cache_length.reshape(1, -1),
        moe_gain.reshape(-1, LANES),
        route_ids.T,
        route_gates.T,
        w_gate_up,
        w_down,
    )
    chunk = 2 * n_local * CAP
    vmem = pltpu.VMEM
    row_blocks = (n_stream, chunk, LANES)
    flat_rows = (n_stream * chunk, LANES)
    pair_width = 2 * hidden + LANES
    share = n_stream // WAVES
    scratch = [vmem(a.shape, a.dtype) for a in args[1:]] + [
        vmem((span * kv_heads * 2, head_dim), F32),
        vmem((local, 2, kv_heads // 2, span, 2 * head_dim), BF16),
        vmem((n_et, tokens, features), BF16),
        vmem((n_et, 16, head_dim), BF16),
        vmem((n_et, 16, head_dim), BF16),
        vmem((local * n_heads, head_dim), BF16),
        vmem((n_et, local * n_heads, head_dim), BF16),
        vmem((tokens * n_heads, head_dim), F32),
        vmem(row_blocks, BF16),
        vmem(row_blocks, BF16),
        vmem(flat_rows, F32),
        vmem((WAVES, n_local, CAP * share, features), BF16),
        vmem((WAVES, n_local, CAP * share, LANES), F32),
        vmem((WAVES, n_local, CAP, share, pair_width), BF16),
        vmem((WAVES, CAP, share, pair_width), F32),
        vmem((WAVES, n_et, share, pair_width), BF16),
        vmem((WAVES, share, hidden), BF16),
        vmem((WAVES, n_et, share, hidden), BF16),
        vmem(flat_rows, F32),
        vmem(row_blocks, BF16),
        vmem(row_blocks, BF16),
        pltpu.SemaphoreType.DMA((len(args),)),
        pltpu.SemaphoreType.DMA((7, n_et)),
        pltpu.SemaphoreType.DMA((7, n_et)),
        pltpu.SemaphoreType.DMA((2, n_stream)),
        pltpu.SemaphoreType.DMA((2, n_stream)),
        pltpu.SemaphoreType.REGULAR((3,)),
    ]
    return pl.pallas_call(
        functools.partial(kernel, n_stream, n_et),
        out_shape=pltpu.VMEM(residual_in.shape, residual_in.dtype),
        in_specs=[pl.BlockSpec(memory_space=pl.ANY)] * len(args),
        out_specs=pl.BlockSpec(memory_space=pltpu.VMEM),
        scratch_shapes=scratch,
        compiler_params=pltpu.CompilerParams(
            collective_id=0, has_side_effects=True, vmem_limit_bytes=56 * 1024 * 1024
        ),
    )(*args)


def solution(mesh):
    placed = (
        P("stream", "et"),
        P(),
        P(),
        P(),
        P(None, "et"),
        P(None, "et"),
        P(None, "et"),
        P(("stream", "et"), None, None, None),
        P("stream"),
        P("et"),
        P("stream", None),
        P("stream", None),
        P("stream", None, "et", None),
        P("stream", None, "et"),
    )
    return jax.shard_map(
        functools.partial(on_device, mesh.shape["stream"], mesh.shape["et"]),
        mesh=mesh,
        in_specs=placed,
        out_specs=P("stream", "et"),
        check_vma=False,
    )
```

```python
import functools
import math

import jax
import jax.numpy as jnp
from jax import lax
from jax.experimental import pallas as pl
from jax.experimental.pallas import tpu as pltpu
from jax.sharding import PartitionSpec as P

EPS = 1e-06
ROPE_BASE = 1000000.0
CAP = 2
LANES = 128
MESH = pl.DeviceIdType.MESH
F32 = jnp.float32
BF16 = jnp.bfloat16

FEATURES, HEADS, MIXED, PAIRS, HIDDEN = 0, 1, 2, 3, 5
OUTWARD, HOME = range(2)
WAVES = 2


def iota(shape, dim):
    return lax.broadcasted_iota(jnp.int32, shape, dim)


def dot(a, b):
    return jnp.dot(a, b, preferred_element_type=F32)


def dot_nt(a, b):
    return lax.dot_general(a, b, (((1,), (1,)), ((), ())), preferred_element_type=F32)


def dot_tn(a, b):
    return lax.dot_general(a, b, (((0,), (0,)), ((), ())), preferred_element_type=F32)


def kernel(
    n_stream,
    n_et,
    res_hbm,
    attn_gain_hbm,
    q_gain_hbm,
    key_gain_hbm,
    w_q_hbm,
    w_kv_hbm,
    w_o_hbm,
    cache_hbm,
    length_hbm,
    moe_gain_hbm,
    ids_hbm,
    gates_hbm,
    w_gu_hbm,
    w_down_hbm,
    out_ref,
    attn_gain,
    q_gain,
    key_gain,
    w_q,
    w_kv,
    w_o,
    cache,
    length,
    moe_gain,
    ids,
    gates,
    w_gu,
    w_down,
    cache_f,
    split,
    features,
    heads_out,
    heads_in,
    mixed_out,
    mixed_in,
    mixed_f,
    rows_out,
    rows_in,
    rows_f,
    expert_rows,
    expert_squares,
    pairs_out,
    pairs_own,
    pairs_in,
    hidden_out,
    hidden_in,
    results_f,
    results_out,
    results_in,
    load_sem,
    et_send,
    et_recv,
    stream_send,
    stream_recv,
    known,
):
    me_s = lax.axis_index("stream")
    me = lax.axis_index("et")
    tokens = res_hbm.shape[0]
    local = tokens // n_et
    head_dim = q_gain_hbm.shape[1]
    own_heads = w_q_hbm.shape[1] // head_dim
    n_heads = own_heads * n_et
    kv_heads = n_et // 2
    group = n_heads // kv_heads
    width = res_hbm.shape[1] * n_et
    n_local = w_gu_hbm.shape[0]
    slots = n_stream * n_local * CAP
    scale = head_dim**-0.5

    def et_peer(step):
        return lax.rem(me + step, n_et)

    def stream_peer(step):
        return lax.rem(me_s + step, n_stream)

    n_y, n_z, n_core = (2, n_stream // 4, 2) if n_stream % 4 == 0 else (1, 1, n_stream)
    y, z, core = lax.div(me_s, n_z * n_core), lax.rem(lax.div(me_s, n_core), n_z), lax.rem(me_s, n_core)

    def stream_at(dy, dz, dc):
        return (
            lax.rem(y + dy, n_y) * (n_z * n_core)
            + lax.rem(z + dz, n_z) * n_core
            + lax.rem(core + dc, n_core)
        )

    across = [(dy, 0, dc) for dy in range(n_y) for dc in range(n_core) if dy or dc]

    def along(reach):
        return [(0, dz, 0) for dz in sorted({reach % n_z, -reach % n_z} - {0})]

    rounds = []
    reach = 1
    while reach < n_z // 2:
        rounds.append(along(reach))
        reach *= 2
    rounds.append(across)

    def tell(number):
        for away in rounds[number] if number < len(rounds) else ():
            pl.semaphore_signal(
                known.at[number],
                inc=1,
                device_id=(stream_at(*away), me),
                device_id_type=MESH,
            )

    def hear(number):
        if number < len(rounds):
            pl.semaphore_wait(known.at[number], len(rounds[number]))

    def hops(away):
        return min(away[1], n_z - away[1]) + 2 * away[0]

    others = sorted(
        [
            (dy, dz, dc)
            for dy in range(n_y)
            for dz in range(n_z)
            for dc in range(n_core)
            if dy or dz or dc
        ],
        key=lambda away: -hops(away),
    )

    share = n_stream // WAVES
    deep = n_z // WAVES

    def slot_of(stream):
        y, z, core = stream // (n_z * n_core), stream // n_core % n_z, stream % n_core
        return z // deep * share + (y * deep + z % deep) * n_core + core

    stream_in = {slot_of(i): i for i in range(n_stream)}
    at_home = slot_of(me_s)

    def members(w):
        return [
            (
                lax.rem(y + dy, n_y) * (n_z * n_core)
                + (w * deep + lax.rem(z + dz, deep)) * n_core
                + lax.rem(core + dc, n_core)
            )
            for dy in reversed(range(n_y))
            for dz in reversed(range(deep))
            for dc in reversed(range(n_core))
        ]

    n_x = n_et // 2
    x, y_low = lax.div(me, 2), lax.rem(me, 2)
    et_far_first = [
        lax.rem(x + dx, n_x) * 2 + lax.rem(y_low + dy, 2)
        for dx in sorted(range(n_x), key=lambda i: -min(i, n_x - i))
        for dy in (1, 0)
        if dx or dy
    ]

    def et_copy(exchange, source, target, peer):
        return pltpu.make_async_remote_copy(
            src_ref=source,
            dst_ref=target,
            send_sem=et_send.at[exchange, peer],
            recv_sem=et_recv.at[exchange, me],
            device_id=(me_s, peer),
            device_id_type=MESH,
        )

    def et_arrival(exchange, source, target, peer):
        return pltpu.make_async_remote_copy(
            src_ref=source,
            dst_ref=target,
            send_sem=et_send.at[exchange, peer],
            recv_sem=et_recv.at[exchange, peer],
            device_id=(me_s, peer),
            device_id_type=MESH,
        )

    def stream_copy(exchange, source, target, peer):
        return pltpu.make_async_remote_copy(
            src_ref=source,
            dst_ref=target,
            send_sem=stream_send.at[exchange, slot_of(peer)],
            recv_sem=stream_recv.at[exchange, at_home],
            device_id=(peer, me),
            device_id_type=MESH,
        )

    def stream_arrival(exchange, source, target, slot):
        return pltpu.make_async_copy(source, target, stream_recv.at[exchange, slot])

    def unless_home(w, body):
        pl.when(lax.div(z, deep) != w)(body)

    def loop(n, body):
        def step(i, carry):
            body(i)
            return carry

        lax.fori_loop(1, n, step, 0)

    barrier = pltpu.get_barrier_semaphore()
    greeted = [(me_s, peer) for peer in et_far_first]
    greeted += [(stream_at(*away), me) for away in along(1) + across]
    for device in greeted:
        pl.semaphore_signal(barrier, inc=1, device_id=device, device_id_type=MESH)

    pl.semaphore_wait(barrier, len(greeted))

    for peer in et_far_first:
        et_copy(FEATURES, res_hbm, features.at[me], peer).start()
    tell(0)

    loads = {}

    def load(name, source, target):
        loads[name] = pltpu.make_async_copy(source, target, load_sem.at[len(loads)])
        loads[name].start()

    load("own", res_hbm, features.at[me])
    load("length", length_hbm, length)
    load("w_q", w_q_hbm, w_q)
    load("w_kv", w_kv_hbm, w_kv)
    load("attn_gain", attn_gain_hbm, attn_gain)
    load("q_gain", q_gain_hbm, q_gain)
    load("key_gain", key_gain_hbm, key_gain)
    load("cache", cache_hbm, cache)

    loads["length"].wait()
    lengths = jnp.broadcast_to(length[...], (tokens, tokens)).astype(F32)
    diagonal = iota((tokens, tokens), 0) == iota((tokens, tokens), 1)
    positions = jnp.sum(jnp.where(diagonal, lengths, 0.0), axis=1, keepdims=True)
    half = head_dim // 2
    lane = iota((tokens, head_dim), 1)
    steps = jnp.where(lane < half, lane, lane - half).astype(F32)
    angle = positions * jnp.exp(steps * (-2.0 * math.log(ROPE_BASE) / head_dim))
    cosine = jnp.cos(angle)
    sine = jnp.where(lane < half, -jnp.sin(angle), jnp.sin(angle))

    pad = 16
    row = iota((n_et * pad, LANES), 0)
    col = iota((n_et * pad, LANES), 1)
    peer_of, at = lax.div(row, pad), lax.rem(row, pad)
    n_q = local * own_heads
    picked = jnp.where(
        at < n_q,
        lax.rem(at, own_heads) * tokens + peer_of * local + lax.div(at, own_heads),
        jnp.where(
            at < n_q + local, own_heads * tokens + peer_of * local + at - n_q, -1
        ),
    )
    order_out = jnp.where(col == picked, 1.0, 0.0).astype(BF16)

    loads["own"].wait()
    loads["attn_gain"].wait()
    loop(
        n_et,
        lambda i: et_arrival(
            FEATURES, res_hbm, features.at[et_peer(i)], et_peer(i)
        ).wait_recv(),
    )
    full = jnp.concatenate([features[i].astype(F32) for i in range(n_et)], axis=1)
    gain = attn_gain[...].astype(F32)
    gain = jnp.concatenate([gain[i : i + 1] for i in range(gain.shape[0])], axis=1)
    normed = (
        full
        * lax.rsqrt(jnp.sum(full * full, axis=1, keepdims=True) * (1.0 / width) + EPS)
        * gain
    ).astype(BF16)

    def rotated(v, g):
        v = v * lax.rsqrt(jnp.mean(v * v, axis=1, keepdims=True) + EPS) * g
        return v * cosine + pltpu.roll(v, half, 1) * sine

    loads["q_gain"].wait()
    loads["key_gain"].wait()
    loads["w_q"].wait()
    query = dot(normed, w_q[...])
    loads["w_kv"].wait()
    key_value = dot(normed, w_kv[...])
    query_gain = q_gain[...].astype(F32)
    made = [
        rotated(query[:, i * head_dim : (i + 1) * head_dim], query_gain)
        for i in range(own_heads)
    ]
    made.append(
        jnp.where(me < kv_heads, rotated(key_value, key_gain[...].astype(F32)), key_value)
    )
    made.append(jnp.zeros((LANES - (own_heads + 1) * tokens, head_dim), F32))
    made = jnp.concatenate(made, axis=0).astype(BF16)
    heads_out[...] = dot(order_out, made).astype(BF16).reshape(heads_out.shape)
    heads_in[me] = heads_out[me]
    for peer in et_far_first:
        et_copy(HEADS, heads_out.at[peer], heads_in.at[me], peer).start()
    hear(0)
    tell(1)
    load("w_o", w_o_hbm, w_o)
    load("ids", ids_hbm, ids)
    load("gates", gates_hbm, gates)
    load("moe_gain", moe_gain_hbm, moe_gain)
    load("w_gu", w_gu_hbm, w_gu)
    load("w_down", w_down_hbm, w_down)

    per = local * n_heads
    row = iota((3 * per, n_et * pad), 0)
    col = iota((3 * per, n_et * pad), 1)
    kind, at = lax.div(row, per), lax.rem(row, per)
    token, head = lax.div(at, n_heads), lax.rem(at, n_heads)
    picked = jnp.where(
        kind == 0,
        lax.div(head, own_heads) * pad + token * own_heads + lax.rem(head, own_heads),
        (lax.div(head, group) + jnp.where(kind == 2, kv_heads, 0)) * pad + n_q + token,
    )
    order_in = jnp.where(col == picked, 1.0, 0.0).astype(BF16)

    loads["cache"].wait()
    rows_of = cache_hbm.shape[0] // local
    span = rows_of // (2 * kv_heads)
    for t in range(local):
        cache_f[...] = cache[t * rows_of : (t + 1) * rows_of, :].astype(F32)
        for kind in range(2):
            for h in range(kv_heads):
                split[t, kind, h // 2, :, h % 2 * head_dim : (h % 2 + 1) * head_dim] = cache_f[
                    pl.ds(2 * h + kind, span, stride=2 * kv_heads), :
                ].astype(BF16)

    own_lane = iota((1, tokens), 1)
    lengths = length[...].astype(F32)
    pairs = kv_heads // 2
    column = iota((2 * group, span), 1)
    live = []
    for t in range(local):
        limit = jnp.sum(
            jnp.where(own_lane == me * local + t, lengths, 0.0), axis=1, keepdims=True
        ).astype(jnp.int32)
        live.append(column < limit)
    empty = jnp.zeros((group, head_dim), F32)
    loop(
        n_et,
        lambda i: et_arrival(
            HEADS, heads_out.at[et_peer(i)], heads_in.at[et_peer(i)], et_peer(i)
        ).wait_recv(),
    )
    ordered = dot(order_in, heads_in[...].reshape(n_et * pad, head_dim))
    q = ordered[:per]
    blocks = []
    for i in range(local * pairs):
        at = i * 2 * group
        upper = jnp.concatenate([q[at : at + group], empty], axis=1)
        lower = jnp.concatenate([empty, q[at + group : at + 2 * group]], axis=1)
        blocks.append(jnp.concatenate([upper, lower], axis=0).astype(BF16))
    scores = [
        dot_nt(block, split[i // pairs, 0, i % pairs]) for i, block in enumerate(blocks)
    ]
    weights = [
        jnp.where(live[i // pairs], jnp.exp(score * scale), 0.0)
        for i, score in enumerate(scores)
    ]
    summed = [
        dot(weight.astype(BF16), split[i // pairs, 1, i % pairs])
        for i, weight in enumerate(weights)
    ]
    fresh = jnp.exp(jnp.sum(q * ordered[per : 2 * per], axis=1, keepdims=True) * scale)
    total = fresh + jnp.concatenate(
        [jnp.sum(weight, axis=1, keepdims=True) for weight in weights], axis=0
    )
    summed = jnp.concatenate(
        [
            part
            for both in summed
            for part in (both[:group, :head_dim], both[group:, head_dim:])
        ],
        axis=0,
    )
    mixed_out[...] = ((summed + fresh * ordered[2 * per :]) / total).astype(BF16)
    mixed_in[me] = mixed_out[...]
    for peer in et_far_first:
        et_copy(MIXED, mixed_out, mixed_in.at[me], peer).start()
    hear(1)
    tell(2)

    loads["ids"].wait()
    loads["gates"].wait()
    at = iota((slots, tokens), 0)
    place = lax.rem(at, n_local * CAP)
    expert = lax.div(at, n_local * CAP) * n_local + lax.rem(place, n_local)
    which = lax.div(place, n_local)
    gate = gates[...]
    gate = gate / jnp.sum(gate, axis=0, keepdims=True)
    named = jnp.zeros((slots, tokens), F32)
    weight = jnp.zeros((slots, tokens), F32)
    for k in range(ids_hbm.shape[0]):
        hit = expert == ids[k : k + 1, :]
        named = jnp.where(hit, 1.0, named)
        weight = jnp.where(hit, gate[k : k + 1, :], weight)
    before = jnp.where(
        iota((tokens, tokens), 0) < iota((tokens, tokens), 1), 1.0, 0.0
    ).astype(BF16)
    earlier = dot(named.astype(BF16), before)
    placed = jnp.where(earlier == which.astype(F32), named, 0.0)
    mixing = placed * weight
    placed = placed.astype(BF16)
    mixing_high = mixing.astype(BF16)
    mixing_low = (mixing - mixing_high.astype(F32)).astype(BF16)

    loads["w_o"].wait()
    loop(
        n_et,
        lambda i: et_arrival(
            MIXED, mixed_out, mixed_in.at[et_peer(i)], et_peer(i)
        ).wait_recv(),
    )
    mixed_f[...] = mixed_in[...].reshape(tokens * n_heads, head_dim).astype(F32)
    attended = jnp.concatenate(
        [mixed_f[pl.ds(h, tokens, stride=n_heads), :] for h in range(n_heads)], axis=1
    ).astype(BF16)
    resid = (features[me].astype(F32) + dot(attended, w_o[...])).astype(BF16)

    sent = dot(placed, resid)
    sent = sent.reshape(n_stream, n_local * CAP, 2 * LANES)
    rows_out[...] = jnp.concatenate(
        [sent[:, :, :LANES], sent[:, :, LANES:]], axis=1
    ).astype(BF16)
    hear(2)
    for away in others:
        peer = stream_at(*away)
        stream_copy(OUTWARD, rows_out.at[peer], rows_in.at[at_home], peer).start()
    stream_arrival(OUTWARD, rows_out.at[me_s], rows_in.at[at_home], at_home).start()
    loads["moe_gain"].wait()
    gain = moe_gain[...].astype(F32)
    gain = jnp.concatenate([gain[0:1], gain[1:2]], axis=1)
    loads["w_gu"].wait()
    chunk = 2 * n_local * CAP
    hidden_width = w_down_hbm.shape[1]

    for w in range(WAVES):
        for slot in range(w * share, (w + 1) * share):
            stream_arrival(OUTWARD, rows_out.at[0], rows_in.at[slot], slot).wait()
        rows_f[w * share * chunk : (w + 1) * share * chunk, :] = (
            rows_in[w * share : (w + 1) * share].reshape(share * chunk, LANES).astype(F32)
        )
        for j in range(n_local):
            taken = []
            for c in range(CAP):
                first = w * share * chunk + c * n_local + j
                taken.append(
                    jnp.concatenate(
                        [
                            rows_f[pl.ds(first + h * n_local * CAP, share, stride=chunk), :]
                            for h in range(2)
                        ],
                        axis=1,
                    )
                )
            taken = jnp.concatenate(taken, axis=0)
            squares = jnp.sum(taken * taken, axis=1, keepdims=True)
            high = squares.astype(BF16).astype(F32)
            expert_squares[w, j] = jnp.where(
                iota((CAP * share, LANES), 1) < LANES // 2, high, squares - high
            )
            expert_rows[w, j] = (taken * gain).astype(BF16)
        for i in range(n_local):
            j = lax.rem(lax.div(me, CAP) + (2, 1, 3, 0)[i], n_local)
            taken = expert_rows[w, j]
            products = jnp.concatenate(
                [dot(taken, w_gu[j, 0]), dot(taken, w_gu[j, 1]), expert_squares[w, j]], axis=1
            )
            pairs_out[w, i] = products.astype(BF16).reshape(pairs_out.shape[2:])
            if i < n_local - 1:
                for c in (y_low, 1 - y_low):
                    et_copy(
                        PAIRS + w, pairs_out.at[w, i, c], pairs_in.at[w, me], CAP * j + c
                    ).start()
            else:
                pairs_own[w] = products.reshape(pairs_own.shape[1:])
                c = 1 - lax.rem(me, CAP)
                et_copy(
                    PAIRS + w, pairs_out.at[w, i, c], pairs_in.at[w, me], CAP * j + c
                ).start()
    for w in range(WAVES):
        pair = pairs_own[w, lax.rem(me, CAP)]
        for i in range(1, n_et):
            et_arrival(
                PAIRS + w, pairs_out.at[w, 0, 0], pairs_in.at[w, et_peer(i)], et_peer(i)
            ).wait_recv()
            pair = pair + pairs_in[w, et_peer(i)].astype(F32)
        squares = jnp.sum(pair[:, 2 * hidden_width :], axis=1, keepdims=True) * (
            2.0 / LANES / width
        )
        level = lax.rsqrt(squares + EPS)
        first = pair[:, :hidden_width] * level
        second = pair[:, hidden_width : 2 * hidden_width] * level
        hidden_out[w] = (first / (1.0 + jnp.exp(-first)) * second).astype(BF16)
        for peer in et_far_first:
            et_copy(HIDDEN + w, hidden_out.at[w], hidden_in.at[w, me], peer).start()
        hidden_in[w, me] = hidden_out[w]

    loads["w_down"].wait()
    for w in range(WAVES):
        loop(
            n_et,
            lambda i: et_arrival(
                HIDDEN + w, hidden_out.at[w], hidden_in.at[w, et_peer(i)], et_peer(i)
            ).wait_recv(),
        )
        for j in range(n_local):
            hidden = hidden_in[w, CAP * j : CAP * (j + 1)].reshape(CAP * share, hidden_width)
            result = dot(hidden, w_down[j])
            for c in range(CAP):
                for h in range(2):
                    first = w * share * chunk + h * n_local * CAP + c * n_local + j
                    results_f[pl.ds(first, share, stride=chunk), :] = result[
                        c * share : (c + 1) * share, h * LANES : (h + 1) * LANES
                    ]
        results_out[w * share : (w + 1) * share] = (
            results_f[w * share * chunk : (w + 1) * share * chunk, :]
            .astype(BF16)
            .reshape(share, chunk, LANES)
        )
        *rest, last = members(w)
        for peer in rest:
            stream_copy(
                HOME, results_out.at[slot_of(peer)], results_in.at[me_s], peer
            ).start()
        unless_home(
            w,
            lambda: stream_copy(
                HOME, results_out.at[slot_of(last)], results_in.at[me_s], last
            ).start(),
        )
    stream_arrival(HOME, results_out.at[at_home], results_in.at[me_s], at_home).start()

    def sent_et(exchange, source, target):
        loop(
            n_et,
            lambda i: et_copy(exchange, source, target, et_peer(i)).wait_send(),
        )

    sent_et(FEATURES, res_hbm, features.at[me])
    sent_et(HEADS, heads_out.at[0], heads_in.at[me])
    sent_et(MIXED, mixed_out, mixed_in.at[me])
    for w in range(WAVES):
        sent_et(PAIRS + w, pairs_out.at[w, 0, 0], pairs_in.at[w, me])
        sent_et(HIDDEN + w, hidden_out.at[w], hidden_in.at[w, me])
    for away in others:
        stream_copy(
            OUTWARD, rows_out.at[0], rows_in.at[at_home], stream_at(*away)
        ).wait_send()
    for w in range(WAVES):
        *rest, last = members(w)
        for peer in rest:
            stream_copy(HOME, results_out.at[0], results_in.at[me_s], peer).wait_send()
        unless_home(
            w,
            lambda: stream_copy(
                HOME, results_out.at[0], results_in.at[me_s], last
            ).wait_send(),
        )

    for slot in range(n_stream):
        stream_arrival(
            HOME, results_out.at[0], results_in.at[stream_in[slot]], slot
        ).wait()
    returned = results_in[...].astype(F32)
    returned = (
        jnp.concatenate(
            [returned[:, : n_local * CAP], returned[:, n_local * CAP :]], axis=2
        )
        .reshape(slots, 2 * LANES)
        .astype(BF16)
    )
    routed = dot_tn(mixing_high, returned) + dot_tn(mixing_low, returned)
    out_ref[...] = (resid.astype(F32) + routed).astype(BF16)


def on_device(
    n_stream,
    n_et,
    residual_in,
    attn_gain,
    q_gain,
    key_norm_gain,
    w_q,
    key_value_weight,
    w_o,
    key_value_cache,
    cache_length,
    moe_gain,
    route_ids,
    route_gates,
    w_gate_up,
    w_down,
):
    tokens, features = residual_in.shape
    head_dim = q_gain.shape[0]
    local, span, _, kv_width = key_value_cache.shape
    kv_heads = kv_width // head_dim
    n_heads = w_q.shape[1] // head_dim * n_et
    n_local = w_gate_up.shape[0]
    hidden = w_down.shape[1]
    cache = (
        key_value_cache.reshape(local, span, 2, kv_heads, head_dim)
        .transpose(0, 1, 3, 2, 4)
        .reshape(local * span * kv_heads * 2, head_dim)
    )
    args = (
        residual_in,
        attn_gain.reshape(-1, LANES),
        q_gain.reshape(1, -1),
        key_norm_gain.reshape(1, -1),
        w_q,
        key_value_weight,
        w_o,
        cache,
        cache_length.reshape(1, -1),
        moe_gain.reshape(-1, LANES),
        route_ids.T,
        route_gates.T,
        w_gate_up,
        w_down,
    )
    chunk = 2 * n_local * CAP
    vmem = pltpu.VMEM
    row_blocks = (n_stream, chunk, LANES)
    flat_rows = (n_stream * chunk, LANES)
    pair_width = 2 * hidden + LANES
    share = n_stream // WAVES
    scratch = [vmem(a.shape, a.dtype) for a in args[1:]] + [
        vmem((span * kv_heads * 2, head_dim), F32),
        vmem((local, 2, kv_heads // 2, span, 2 * head_dim), BF16),
        vmem((n_et, tokens, features), BF16),
        vmem((n_et, 16, head_dim), BF16),
        vmem((n_et, 16, head_dim), BF16),
        vmem((local * n_heads, head_dim), BF16),
        vmem((n_et, local * n_heads, head_dim), BF16),
        vmem((tokens * n_heads, head_dim), F32),
        vmem(row_blocks, BF16),
        vmem(row_blocks, BF16),
        vmem(flat_rows, F32),
        vmem((WAVES, n_local, CAP * share, features), BF16),
        vmem((WAVES, n_local, CAP * share, LANES), F32),
        vmem((WAVES, n_local, CAP, share, pair_width), BF16),
        vmem((WAVES, CAP, share, pair_width), F32),
        vmem((WAVES, n_et, share, pair_width), BF16),
        vmem((WAVES, share, hidden), BF16),
        vmem((WAVES, n_et, share, hidden), BF16),
        vmem(flat_rows, F32),
        vmem(row_blocks, BF16),
        vmem(row_blocks, BF16),
        pltpu.SemaphoreType.DMA((len(args),)),
        pltpu.SemaphoreType.DMA((7, n_et)),
        pltpu.SemaphoreType.DMA((7, n_et)),
        pltpu.SemaphoreType.DMA((2, n_stream)),
        pltpu.SemaphoreType.DMA((2, n_stream)),
        pltpu.SemaphoreType.REGULAR((3,)),
    ]
    return pl.pallas_call(
        functools.partial(kernel, n_stream, n_et),
        out_shape=pltpu.VMEM(residual_in.shape, residual_in.dtype),
        in_specs=[pl.BlockSpec(memory_space=pl.ANY)] * len(args),
        out_specs=pl.BlockSpec(memory_space=pltpu.VMEM),
        scratch_shapes=scratch,
        compiler_params=pltpu.CompilerParams(
            collective_id=0, has_side_effects=True, vmem_limit_bytes=56 * 1024 * 1024
        ),
    )(*args)


def solution(mesh):
    placed = (
        P("stream", "et"),
        P(),
        P(),
        P(),
        P(None, "et"),
        P(None, "et"),
        P(None, "et"),
        P(("stream", "et"), None, None, None),
        P("stream"),
        P("et"),
        P("stream", None),
        P("stream", None),
        P("stream", None, "et", None),
        P("stream", None, "et"),
    )
    return jax.shard_map(
        functools.partial(on_device, mesh.shape["stream"], mesh.shape["et"]),
        mesh=mesh,
        in_specs=placed,
        out_specs=P("stream", "et"),
        check_vma=False,
    )
```

```python
import functools
import math

import jax
import jax.numpy as jnp
from jax import lax
from jax.experimental import pallas as pl
from jax.experimental.pallas import tpu as pltpu
from jax.sharding import PartitionSpec as P

EPS = 1e-06
ROPE_BASE = 1000000.0
CAP = 2
LANES = 128
MESH = pl.DeviceIdType.MESH
F32 = jnp.float32
BF16 = jnp.bfloat16

FEATURES, HEADS, MIXED, PAIRS, HIDDEN = 0, 1, 2, 3, 7
OUTWARD, HOME = range(2)


def parts_of(n_stream):
    return 4 if n_stream % 16 == 0 else 2


def iota(shape, dim):
    return lax.broadcasted_iota(jnp.int32, shape, dim)


def dot(a, b):
    return jnp.dot(a, b, preferred_element_type=F32)


def dot_nt(a, b):
    return lax.dot_general(a, b, (((1,), (1,)), ((), ())), preferred_element_type=F32)


def dot_tn(a, b):
    return lax.dot_general(a, b, (((0,), (0,)), ((), ())), preferred_element_type=F32)


def kernel(
    n_stream,
    n_et,
    res_hbm,
    attn_gain_hbm,
    q_gain_hbm,
    key_gain_hbm,
    w_q_hbm,
    w_kv_hbm,
    w_o_hbm,
    cache_hbm,
    length_hbm,
    moe_gain_hbm,
    ids_hbm,
    gates_hbm,
    w_gu_hbm,
    w_down_hbm,
    out_ref,
    attn_gain,
    q_gain,
    key_gain,
    w_q,
    w_kv,
    w_o,
    cache,
    length,
    moe_gain,
    ids,
    gates,
    w_gu,
    w_down,
    cache_f,
    split,
    features,
    heads_out,
    heads_in,
    mixed_out,
    mixed_in,
    mixed_f,
    rows_out,
    rows_in,
    rows_f,
    expert_rows,
    expert_squares,
    pairs_even,
    pairs_odd,
    pairs_own,
    pairs_in_even,
    pairs_in_odd,
    hidden_out,
    hidden_in,
    results_f,
    results_out,
    results_in,
    load_sem,
    et_send,
    et_recv,
    stream_send,
    stream_recv,
    known,
):
    me_s = lax.axis_index("stream")
    me = lax.axis_index("et")
    tokens = res_hbm.shape[0]
    local = tokens // n_et
    head_dim = q_gain_hbm.shape[1]
    own_heads = w_q_hbm.shape[1] // head_dim
    n_heads = own_heads * n_et
    kv_heads = n_et // 2
    group = n_heads // kv_heads
    width = res_hbm.shape[1] * n_et
    n_local = w_gu_hbm.shape[0]
    slots = n_stream * n_local * CAP
    scale = head_dim**-0.5

    def et_peer(step):
        return lax.rem(me + step, n_et)

    def stream_peer(step):
        return lax.rem(me_s + step, n_stream)

    n_y, n_z, n_core = (2, n_stream // 4, 2) if n_stream % 4 == 0 else (1, 1, n_stream)
    y, z, core = lax.div(me_s, n_z * n_core), lax.rem(lax.div(me_s, n_core), n_z), lax.rem(me_s, n_core)

    def stream_at(dy, dz, dc):
        return (
            lax.rem(y + dy, n_y) * (n_z * n_core)
            + lax.rem(z + dz, n_z) * n_core
            + lax.rem(core + dc, n_core)
        )

    across = [(dy, 0, dc) for dy in range(n_y) for dc in range(n_core) if dy or dc]

    def along(reach):
        return [(0, dz, 0) for dz in sorted({reach % n_z, -reach % n_z} - {0})]

    rounds = []
    reach = 1
    while reach < n_z // 2:
        rounds.append(along(reach))
        reach *= 2
    rounds.append(across)

    def tell(number):
        for away in rounds[number] if number < len(rounds) else ():
            pl.semaphore_signal(
                known.at[number],
                inc=1,
                device_id=(stream_at(*away), me),
                device_id_type=MESH,
            )

    def hear(number):
        if number < len(rounds):
            pl.semaphore_wait(known.at[number], len(rounds[number]))

    parts = parts_of(n_stream)
    n_waves = parts // 2
    share, small = n_stream // n_waves, n_stream // parts
    deep = n_z // parts
    own_part = lax.div(z, deep)

    def slot_of(stream):
        y, z, core = stream // (n_z * n_core), stream // n_core % n_z, stream % n_core
        return z // deep * small + (y * deep + z % deep) * n_core + core

    stream_in = {slot_of(i): i for i in range(n_stream)}
    at_home = own_part * small + (y * deep + lax.rem(z, deep)) * n_core + core

    def members(part):
        found = []
        for dy in reversed(range(n_y)):
            for dz in reversed(range(deep)):
                for dc in reversed(range(n_core)):
                    at_y, at_z, at_core = (
                        lax.rem(y + dy, n_y),
                        lax.rem(z + dz, deep),
                        lax.rem(core + dc, n_core),
                    )
                    found.append(
                        (
                            at_y * (n_z * n_core) + (part * deep + at_z) * n_core + at_core,
                            part * small + (at_y * deep + at_z) * n_core + at_core,
                        )
                    )
        return found

    n_x = n_et // 2
    x, y_low = lax.div(me, 2), lax.rem(me, 2)
    et_far_first = [
        lax.rem(x + dx, n_x) * 2 + lax.rem(y_low + dy, 2)
        for dx in sorted(range(n_x), key=lambda i: -min(i, n_x - i))
        for dy in (1, 0)
        if dx or dy
    ]

    def et_copy(exchange, source, target, peer):
        return pltpu.make_async_remote_copy(
            src_ref=source,
            dst_ref=target,
            send_sem=et_send.at[exchange, peer],
            recv_sem=et_recv.at[exchange, me],
            device_id=(me_s, peer),
            device_id_type=MESH,
        )

    def et_arrival(exchange, source, target, peer):
        return pltpu.make_async_remote_copy(
            src_ref=source,
            dst_ref=target,
            send_sem=et_send.at[exchange, peer],
            recv_sem=et_recv.at[exchange, peer],
            device_id=(me_s, peer),
            device_id_type=MESH,
        )

    def stream_copy(exchange, number, source, target, peer):
        return pltpu.make_async_remote_copy(
            src_ref=source,
            dst_ref=target,
            send_sem=stream_send.at[exchange, number],
            recv_sem=stream_recv.at[exchange, at_home],
            device_id=(peer, me),
            device_id_type=MESH,
        )

    def stream_arrival(exchange, source, target, slot):
        return pltpu.make_async_copy(source, target, stream_recv.at[exchange, slot])

    def unless_home(part, body):
        pl.when(own_part != part)(body)

    def loop(n, body):
        def step(i, carry):
            body(i)
            return carry

        lax.fori_loop(1, n, step, 0)

    loads = {}

    def load(name, source, target):
        loads[name] = pltpu.make_async_copy(source, target, load_sem.at[len(loads)])
        loads[name].start()

    load("own", res_hbm, features.at[me])

    barrier = pltpu.get_barrier_semaphore()
    greeted = [(me_s, peer) for peer in et_far_first]
    greeted += [(stream_at(*away), me) for away in along(1) + across]
    for device in greeted:
        pl.semaphore_signal(barrier, inc=1, device_id=device, device_id_type=MESH)

    pl.semaphore_wait(barrier, len(greeted))

    loads["own"].wait()
    for peer in et_far_first:
        et_copy(FEATURES, features.at[me], features.at[me], peer).start()
    tell(0)

    load("length", length_hbm, length)
    load("w_q", w_q_hbm, w_q)
    load("w_kv", w_kv_hbm, w_kv)
    load("attn_gain", attn_gain_hbm, attn_gain)
    load("q_gain", q_gain_hbm, q_gain)
    load("key_gain", key_gain_hbm, key_gain)
    load("cache", cache_hbm, cache)

    loads["length"].wait()
    lengths = jnp.broadcast_to(length[...], (tokens, tokens)).astype(F32)
    diagonal = iota((tokens, tokens), 0) == iota((tokens, tokens), 1)
    positions = jnp.sum(jnp.where(diagonal, lengths, 0.0), axis=1, keepdims=True)
    turn = head_dim // 2
    lane = iota((tokens, head_dim), 1)
    steps = jnp.where(lane < turn, lane, lane - turn).astype(F32)
    angle = positions * jnp.exp(steps * (-2.0 * math.log(ROPE_BASE) / head_dim))
    cosine = jnp.cos(angle)
    sine = jnp.where(lane < turn, -jnp.sin(angle), jnp.sin(angle))

    pad = 16
    row = iota((n_et * pad, LANES), 0)
    col = iota((n_et * pad, LANES), 1)
    peer_of, at = lax.div(row, pad), lax.rem(row, pad)
    n_q = local * own_heads
    picked = jnp.where(
        at < n_q,
        lax.rem(at, own_heads) * tokens + peer_of * local + lax.div(at, own_heads),
        jnp.where(
            at < n_q + local, own_heads * tokens + peer_of * local + at - n_q, -1
        ),
    )
    order_out = jnp.where(col == picked, 1.0, 0.0).astype(BF16)

    loads["attn_gain"].wait()
    loop(
        n_et,
        lambda i: et_arrival(
            FEATURES, res_hbm, features.at[et_peer(i)], et_peer(i)
        ).wait_recv(),
    )
    full = jnp.concatenate([features[i].astype(F32) for i in range(n_et)], axis=1)
    gain = attn_gain[...].astype(F32)
    gain = jnp.concatenate([gain[i : i + 1] for i in range(gain.shape[0])], axis=1)
    normed = (
        full
        * lax.rsqrt(jnp.sum(full * full, axis=1, keepdims=True) * (1.0 / width) + EPS)
        * gain
    ).astype(BF16)

    def rotated(v, g):
        v = v * lax.rsqrt(jnp.mean(v * v, axis=1, keepdims=True) + EPS) * g
        return v * cosine + pltpu.roll(v, turn, 1) * sine

    loads["q_gain"].wait()
    loads["key_gain"].wait()
    loads["w_q"].wait()
    query = dot(normed, w_q[...])
    loads["w_kv"].wait()
    key_value = dot(normed, w_kv[...])
    query_gain = q_gain[...].astype(F32)
    made = [
        rotated(query[:, i * head_dim : (i + 1) * head_dim], query_gain)
        for i in range(own_heads)
    ]
    made.append(
        jnp.where(me < kv_heads, rotated(key_value, key_gain[...].astype(F32)), key_value)
    )
    made.append(jnp.zeros((LANES - (own_heads + 1) * tokens, head_dim), F32))
    made = jnp.concatenate(made, axis=0).astype(BF16)
    heads_out[...] = dot(order_out, made).astype(BF16).reshape(heads_out.shape)
    heads_in[me] = heads_out[me]
    for peer in et_far_first:
        et_copy(HEADS, heads_out.at[peer], heads_in.at[me], peer).start()
    hear(0)
    tell(1)
    load("w_o", w_o_hbm, w_o)
    load("ids", ids_hbm, ids)
    load("gates", gates_hbm, gates)
    load("moe_gain", moe_gain_hbm, moe_gain)
    load("w_gu", w_gu_hbm, w_gu)
    load("w_down", w_down_hbm, w_down)

    per = local * n_heads
    row = iota((3 * per, n_et * pad), 0)
    col = iota((3 * per, n_et * pad), 1)
    kind, at = lax.div(row, per), lax.rem(row, per)
    token, head = lax.div(at, n_heads), lax.rem(at, n_heads)
    picked = jnp.where(
        kind == 0,
        lax.div(head, own_heads) * pad + token * own_heads + lax.rem(head, own_heads),
        (lax.div(head, group) + jnp.where(kind == 2, kv_heads, 0)) * pad + n_q + token,
    )
    order_in = jnp.where(col == picked, 1.0, 0.0).astype(BF16)

    loads["cache"].wait()
    rows_of = cache_hbm.shape[0] // local
    span = rows_of // (2 * kv_heads)
    for t in range(local):
        cache_f[...] = cache[t * rows_of : (t + 1) * rows_of, :].astype(F32)
        for kind in range(2):
            for h in range(kv_heads):
                split[t, kind, h // 2, :, h % 2 * head_dim : (h % 2 + 1) * head_dim] = cache_f[
                    pl.ds(2 * h + kind, span, stride=2 * kv_heads), :
                ].astype(BF16)

    own_lane = iota((1, tokens), 1)
    lengths = length[...].astype(F32)
    pairs = kv_heads // 2
    column = iota((2 * group, span), 1)
    live = []
    for t in range(local):
        limit = jnp.sum(
            jnp.where(own_lane == me * local + t, lengths, 0.0), axis=1, keepdims=True
        ).astype(jnp.int32)
        live.append(column < limit)
    empty = jnp.zeros((group, head_dim), F32)
    loop(
        n_et,
        lambda i: et_arrival(
            HEADS, heads_out.at[et_peer(i)], heads_in.at[et_peer(i)], et_peer(i)
        ).wait_recv(),
    )
    ordered = dot(order_in, heads_in[...].reshape(n_et * pad, head_dim))
    q = ordered[:per]
    blocks = []
    for i in range(local * pairs):
        at = i * 2 * group
        upper = jnp.concatenate([q[at : at + group], empty], axis=1)
        lower = jnp.concatenate([empty, q[at + group : at + 2 * group]], axis=1)
        blocks.append(jnp.concatenate([upper, lower], axis=0).astype(BF16))
    scores = [
        dot_nt(block, split[i // pairs, 0, i % pairs]) for i, block in enumerate(blocks)
    ]
    weights = [
        jnp.where(live[i // pairs], jnp.exp(score * scale), 0.0)
        for i, score in enumerate(scores)
    ]
    summed = [
        dot(weight.astype(BF16), split[i // pairs, 1, i % pairs])
        for i, weight in enumerate(weights)
    ]
    fresh = jnp.exp(jnp.sum(q * ordered[per : 2 * per], axis=1, keepdims=True) * scale)
    total = fresh + jnp.concatenate(
        [jnp.sum(weight, axis=1, keepdims=True) for weight in weights], axis=0
    )
    summed = jnp.concatenate(
        [
            part
            for both in summed
            for part in (both[:group, :head_dim], both[group:, head_dim:])
        ],
        axis=0,
    )
    mixed_out[...] = ((summed + fresh * ordered[2 * per :]) / total).astype(BF16)
    mixed_in[me] = mixed_out[...]
    for peer in et_far_first:
        et_copy(MIXED, mixed_out, mixed_in.at[me], peer).start()
    hear(1)
    tell(2)

    loads["ids"].wait()
    loads["gates"].wait()
    at = iota((slots, tokens), 0)
    place = lax.rem(at, n_local * CAP)
    expert = lax.div(at, n_local * CAP) * n_local + lax.rem(place, n_local)
    which = lax.div(place, n_local)
    gate = gates[...]
    gate = gate / jnp.sum(gate, axis=0, keepdims=True)
    named = jnp.zeros((slots, tokens), F32)
    weight = jnp.zeros((slots, tokens), F32)
    for k in range(ids_hbm.shape[0]):
        hit = expert == ids[k : k + 1, :]
        named = jnp.where(hit, 1.0, named)
        weight = jnp.where(hit, gate[k : k + 1, :], weight)
    before = jnp.where(
        iota((tokens, tokens), 0) < iota((tokens, tokens), 1), 1.0, 0.0
    ).astype(BF16)
    earlier = dot(named.astype(BF16), before)
    placed = jnp.where(earlier == which.astype(F32), named, 0.0)
    mixing = placed * weight
    placed = placed.astype(BF16)
    mixing_high = mixing.astype(BF16)
    mixing_low = (mixing - mixing_high.astype(F32)).astype(BF16)

    loads["w_o"].wait()
    loop(
        n_et,
        lambda i: et_arrival(
            MIXED, mixed_out, mixed_in.at[et_peer(i)], et_peer(i)
        ).wait_recv(),
    )
    mixed_f[...] = mixed_in[...].reshape(tokens * n_heads, head_dim).astype(F32)
    attended = jnp.concatenate(
        [mixed_f[pl.ds(h, tokens, stride=n_heads), :] for h in range(n_heads)], axis=1
    ).astype(BF16)
    resid = (features[me].astype(F32) + dot(attended, w_o[...])).astype(BF16)

    sent = dot(placed, resid)
    sent = sent.reshape(n_stream, n_local * CAP, 2 * LANES)
    rows_out[...] = jnp.concatenate(
        [sent[:, :, :LANES], sent[:, :, LANES:]], axis=1
    ).astype(BF16)
    hear(2)
    beside = own_part + 1 - 2 * lax.rem(own_part, 2)
    order = [beside, own_part]
    if parts == 4:
        order = [lax.rem(part + 2, parts) for part in order] + order
    outward = [peer for part in order for peer, _ in members(part)][:-1]
    for number, peer in enumerate(outward):
        stream_copy(OUTWARD, number, rows_out.at[peer], rows_in.at[at_home], peer).start()
    stream_arrival(OUTWARD, rows_out.at[me_s], rows_in.at[at_home], at_home).start()
    loads["moe_gain"].wait()
    gain = moe_gain[...].astype(F32)
    gain = jnp.concatenate([gain[0:1], gain[1:2]], axis=1)
    loads["w_gu"].wait()
    chunk = 2 * n_local * CAP
    hidden_width = w_down_hbm.shape[1]

    left_lanes = iota((CAP * small, LANES), 1) < LANES // 2
    for part in range(parts):
        w, odd = part // 2, part % 2
        for slot in range(part * small, (part + 1) * small):
            stream_arrival(OUTWARD, rows_out.at[0], rows_in.at[slot], slot).wait()
        rows_f[part * small * chunk : (part + 1) * small * chunk, :] = (
            rows_in[part * small : (part + 1) * small].reshape(small * chunk, LANES).astype(F32)
        )
        for j in range(n_local):
            taken = []
            for c in range(CAP):
                first = part * small * chunk + c * n_local + j
                taken.append(
                    jnp.concatenate(
                        [
                            rows_f[pl.ds(first + h * n_local * CAP, small, stride=chunk), :]
                            for h in range(2)
                        ],
                        axis=1,
                    )
                )
            taken = jnp.concatenate(taken, axis=0)
            expert_squares[part, j] = jnp.broadcast_to(
                jnp.sum(taken * taken, axis=1, keepdims=True), (CAP * small, LANES)
            )
            expert_rows[part, j] = (taken * gain).astype(BF16)
        sent, received = (pairs_odd, pairs_in_odd) if odd else (pairs_even, pairs_in_even)
        for i in range(n_local):
            j = lax.rem(lax.div(me, CAP) + (2, 1, 3, 0)[i], n_local)
            taken = expert_rows[part, j]
            halves = [dot(taken, w_gu[j, 0]), dot(taken, w_gu[j, 1])]
            if odd:
                squares = jnp.where(
                    left_lanes, expert_squares[part - 1, j], expert_squares[part, j]
                )
                high = squares.astype(BF16).astype(F32)
                halves = [
                    jnp.concatenate([halves[0], high], axis=1),
                    jnp.concatenate([halves[1], squares - high], axis=1),
                ]
            for c in range(CAP):
                products = jnp.concatenate(
                    [value[c * small : (c + 1) * small] for value in halves], axis=0
                )
                sent[w, i, c] = products.astype(BF16)
                if i == n_local - 1:
                    pairs_own[part, c, :, : products.shape[1]] = products
            for c in (y_low, 1 - y_low) if i < n_local - 1 else (1 - y_low,):
                et_copy(
                    PAIRS + part, sent.at[w, i, c], received.at[w, me], CAP * j + c
                ).start()
    for w in range(n_waves):
        sums = []
        for part in (2 * w, 2 * w + 1):
            odd = part % 2
            sent, received = (pairs_odd, pairs_in_odd) if odd else (pairs_even, pairs_in_even)
            pair = pairs_own[part, y_low, :, : received.shape[3]]
            for i in range(1, n_et):
                et_arrival(
                    PAIRS + part, sent.at[w, 0, 0], received.at[w, et_peer(i)], et_peer(i)
                ).wait_recv()
                pair = pair + received[w, et_peer(i)].astype(F32)
            sums.append(pair)
        squares = sums[1][:small, hidden_width:] + sums[1][small:, hidden_width:]
        left = iota((small, LANES), 1) < LANES // 2
        made = []
        for pair, lanes in zip(sums, (left, ~left)):
            level = lax.rsqrt(
                jnp.sum(jnp.where(lanes, squares, 0.0), axis=1, keepdims=True)
                * (2.0 / LANES / width)
                + EPS
            )
            first = pair[:small, :hidden_width] * level
            second = pair[small:, :hidden_width] * level
            made.append(first / (1.0 + jnp.exp(-first)) * second)
        hidden_out[w] = jnp.concatenate(made, axis=0).astype(BF16)
        for peer in et_far_first:
            et_copy(HIDDEN + w, hidden_out.at[w], hidden_in.at[w, me], peer).start()
        hidden_in[w, me] = hidden_out[w]

    loads["w_down"].wait()
    for w in range(n_waves):
        loop(
            n_et,
            lambda i: et_arrival(
                HIDDEN + w, hidden_out.at[w], hidden_in.at[w, et_peer(i)], et_peer(i)
            ).wait_recv(),
        )
        for j in range(n_local):
            hidden = hidden_in[w, CAP * j : CAP * (j + 1)].reshape(CAP * share, hidden_width)
            result = dot(hidden, w_down[j])
            for c in range(CAP):
                for h in range(2):
                    first = w * share * chunk + h * n_local * CAP + c * n_local + j
                    results_f[pl.ds(first, share, stride=chunk), :] = result[
                        c * share : (c + 1) * share, h * LANES : (h + 1) * LANES
                    ]
        results_out[w * share : (w + 1) * share] = (
            results_f[w * share * chunk : (w + 1) * share * chunk, :]
            .astype(BF16)
            .reshape(share, chunk, LANES)
        )
        for part in (2 * w, 2 * w + 1):
            *rest, (last, place) = members(part)
            for number, (peer, slot) in enumerate(rest):
                stream_copy(
                    HOME, part * small + number, results_out.at[slot], results_in.at[me_s], peer
                ).start()
            unless_home(
                part,
                lambda: stream_copy(
                    HOME, (part + 1) * small - 1, results_out.at[place], results_in.at[me_s], last
                ).start(),
            )
    stream_arrival(HOME, results_out.at[at_home], results_in.at[me_s], at_home).start()

    def sent_et(exchange, source, target):
        loop(
            n_et,
            lambda i: et_copy(exchange, source, target, et_peer(i)).wait_send(),
        )

    sent_et(FEATURES, features.at[me], features.at[me])
    sent_et(HEADS, heads_out.at[0], heads_in.at[me])
    sent_et(MIXED, mixed_out, mixed_in.at[me])
    for part in range(parts):
        sent, received = (pairs_odd, pairs_in_odd) if part % 2 else (pairs_even, pairs_in_even)
        sent_et(PAIRS + part, sent.at[part // 2, 0, 0], received.at[part // 2, me])
    for w in range(n_waves):
        sent_et(HIDDEN + w, hidden_out.at[w], hidden_in.at[w, me])
    for number, peer in enumerate(outward):
        stream_copy(OUTWARD, number, rows_out.at[0], rows_in.at[at_home], peer).wait_send()
    for part in range(parts):
        *rest, (last, _) = members(part)
        for number, (peer, _) in enumerate(rest):
            stream_copy(
                HOME, part * small + number, results_out.at[0], results_in.at[me_s], peer
            ).wait_send()
        unless_home(
            part,
            lambda: stream_copy(
                HOME, (part + 1) * small - 1, results_out.at[0], results_in.at[me_s], last
            ).wait_send(),
        )

    for slot in range(n_stream):
        stream_arrival(
            HOME, results_out.at[0], results_in.at[stream_in[slot]], slot
        ).wait()
    returned = results_in[...].astype(F32)
    returned = (
        jnp.concatenate(
            [returned[:, : n_local * CAP], returned[:, n_local * CAP :]], axis=2
        )
        .reshape(slots, 2 * LANES)
        .astype(BF16)
    )
    routed = dot_tn(mixing_high, returned) + dot_tn(mixing_low, returned)
    out_ref[...] = (resid.astype(F32) + routed).astype(BF16)


def on_device(
    n_stream,
    n_et,
    residual_in,
    attn_gain,
    q_gain,
    key_norm_gain,
    w_q,
    key_value_weight,
    w_o,
    key_value_cache,
    cache_length,
    moe_gain,
    route_ids,
    route_gates,
    w_gate_up,
    w_down,
):
    tokens, features = residual_in.shape
    head_dim = q_gain.shape[0]
    local, span, _, kv_width = key_value_cache.shape
    kv_heads = kv_width // head_dim
    n_heads = w_q.shape[1] // head_dim * n_et
    n_local = w_gate_up.shape[0]
    hidden = w_down.shape[1]
    cache = (
        key_value_cache.reshape(local, span, 2, kv_heads, head_dim)
        .transpose(0, 1, 3, 2, 4)
        .reshape(local * span * kv_heads * 2, head_dim)
    )
    args = (
        residual_in,
        attn_gain.reshape(-1, LANES),
        q_gain.reshape(1, -1),
        key_norm_gain.reshape(1, -1),
        w_q,
        key_value_weight,
        w_o,
        cache,
        cache_length.reshape(1, -1),
        moe_gain.reshape(-1, LANES),
        route_ids.T,
        route_gates.T,
        w_gate_up,
        w_down,
    )
    chunk = 2 * n_local * CAP
    vmem = pltpu.VMEM
    row_blocks = (n_stream, chunk, LANES)
    flat_rows = (n_stream * chunk, LANES)
    parts = parts_of(n_stream)
    n_waves = parts // 2
    share, small = n_stream // n_waves, n_stream // parts
    scratch = [vmem(a.shape, a.dtype) for a in args[1:]] + [
        vmem((span * kv_heads * 2, head_dim), F32),
        vmem((local, 2, kv_heads // 2, span, 2 * head_dim), BF16),
        vmem((n_et, tokens, features), BF16),
        vmem((n_et, 16, head_dim), BF16),
        vmem((n_et, 16, head_dim), BF16),
        vmem((local * n_heads, head_dim), BF16),
        vmem((n_et, local * n_heads, head_dim), BF16),
        vmem((tokens * n_heads, head_dim), F32),
        vmem(row_blocks, BF16),
        vmem(row_blocks, BF16),
        vmem(flat_rows, F32),
        vmem((parts, n_local, CAP * small, features), BF16),
        vmem((parts, n_local, CAP * small, LANES), F32),
        vmem((n_waves, n_local, CAP, 2 * small, hidden), BF16),
        vmem((n_waves, n_local, CAP, 2 * small, hidden + LANES), BF16),
        vmem((parts, CAP, 2 * small, hidden + LANES), F32),
        vmem((n_waves, n_et, 2 * small, hidden), BF16),
        vmem((n_waves, n_et, 2 * small, hidden + LANES), BF16),
        vmem((n_waves, share, hidden), BF16),
        vmem((n_waves, n_et, share, hidden), BF16),
        vmem(flat_rows, F32),
        vmem(row_blocks, BF16),
        vmem(row_blocks, BF16),
        pltpu.SemaphoreType.DMA((len(args),)),
        pltpu.SemaphoreType.DMA((9, n_et)),
        pltpu.SemaphoreType.DMA((9, n_et)),
        pltpu.SemaphoreType.DMA((2, n_stream)),
        pltpu.SemaphoreType.DMA((2, n_stream)),
        pltpu.SemaphoreType.REGULAR((3,)),
    ]
    return pl.pallas_call(
        functools.partial(kernel, n_stream, n_et),
        out_shape=pltpu.VMEM(residual_in.shape, residual_in.dtype),
        in_specs=[pl.BlockSpec(memory_space=pl.ANY)] * len(args),
        out_specs=pl.BlockSpec(memory_space=pltpu.VMEM),
        scratch_shapes=scratch,
        compiler_params=pltpu.CompilerParams(
            collective_id=0, has_side_effects=True, vmem_limit_bytes=56 * 1024 * 1024
        ),
    )(*args)


def solution(mesh):
    placed = (
        P("stream", "et"),
        P(),
        P(),
        P(),
        P(None, "et"),
        P(None, "et"),
        P(None, "et"),
        P(("stream", "et"), None, None, None),
        P("stream"),
        P("et"),
        P("stream", None),
        P("stream", None),
        P("stream", None, "et", None),
        P("stream", None, "et"),
    )
    return jax.shard_map(
        functools.partial(on_device, mesh.shape["stream"], mesh.shape["et"]),
        mesh=mesh,
        in_specs=placed,
        out_specs=P("stream", "et"),
        check_vma=False,
    )
```

```python
import functools
import math

import jax
import jax.numpy as jnp
from jax import lax
from jax.experimental import pallas as pl
from jax.experimental.pallas import tpu as pltpu
from jax.sharding import PartitionSpec as P

EPS = 1e-06
ROPE_BASE = 1000000.0
CAP = 2
LANES = 128
MESH = pl.DeviceIdType.MESH
F32 = jnp.float32
BF16 = jnp.bfloat16

FEATURES, HEADS, MIXED, PAIRS, HIDDEN = 0, 1, 2, 3, 7
OUTWARD, HOME = range(2)


def parts_of(n_stream):
    return 4 if n_stream % 16 == 0 else 2


def iota(shape, dim):
    return lax.broadcasted_iota(jnp.int32, shape, dim)


def dot(a, b):
    return jnp.dot(a, b, preferred_element_type=F32)


def dot_nt(a, b):
    return lax.dot_general(a, b, (((1,), (1,)), ((), ())), preferred_element_type=F32)


def dot_tn(a, b):
    return lax.dot_general(a, b, (((0,), (0,)), ((), ())), preferred_element_type=F32)


def kernel(
    n_stream,
    n_et,
    res_hbm,
    attn_gain_hbm,
    q_gain_hbm,
    key_gain_hbm,
    w_q_hbm,
    w_kv_hbm,
    w_o_hbm,
    cache_hbm,
    length_hbm,
    moe_gain_hbm,
    ids_hbm,
    gates_hbm,
    w_gu_hbm,
    w_down_hbm,
    out_ref,
    attn_gain,
    q_gain,
    key_gain,
    w_q,
    w_kv,
    w_o,
    cache,
    length,
    moe_gain,
    ids,
    gates,
    w_gu,
    w_down,
    cache_f,
    split,
    features,
    heads_out,
    heads_in,
    mixed_out,
    mixed_in,
    mixed_f,
    rows_out,
    rows_in,
    rows_f,
    expert_rows,
    expert_squares,
    pairs_even,
    pairs_odd,
    pairs_own,
    pairs_in_even,
    pairs_in_odd,
    hidden_out,
    hidden_in,
    results_f,
    results_out,
    results_in,
    load_sem,
    et_send,
    et_recv,
    stream_send,
    stream_recv,
    known,
):
    me_s = lax.axis_index("stream")
    me = lax.axis_index("et")
    tokens = res_hbm.shape[0]
    local = tokens // n_et
    head_dim = q_gain_hbm.shape[1]
    own_heads = w_q_hbm.shape[1] // head_dim
    n_heads = own_heads * n_et
    kv_heads = n_et // 2
    group = n_heads // kv_heads
    width = res_hbm.shape[1] * n_et
    n_local = w_gu_hbm.shape[0]
    slots = n_stream * n_local * CAP
    scale = head_dim**-0.5

    def et_peer(step):
        return lax.rem(me + step, n_et)

    def stream_peer(step):
        return lax.rem(me_s + step, n_stream)

    n_y, n_z, n_core = (2, n_stream // 4, 2) if n_stream % 4 == 0 else (1, 1, n_stream)
    y, z, core = lax.div(me_s, n_z * n_core), lax.rem(lax.div(me_s, n_core), n_z), lax.rem(me_s, n_core)

    def stream_at(dy, dz, dc):
        return (
            lax.rem(y + dy, n_y) * (n_z * n_core)
            + lax.rem(z + dz, n_z) * n_core
            + lax.rem(core + dc, n_core)
        )

    across = [(dy, 0, dc) for dy in range(n_y) for dc in range(n_core) if dy or dc]

    def along(reach):
        return [(0, dz, 0) for dz in sorted({reach % n_z, -reach % n_z} - {0})]

    rounds = []
    reach = 1
    while reach < n_z // 2:
        rounds.append(along(reach))
        reach *= 2
    rounds.append(across)

    def tell(number):
        for away in rounds[number] if number < len(rounds) else ():
            pl.semaphore_signal(
                known.at[number],
                inc=1,
                device_id=(stream_at(*away), me),
                device_id_type=MESH,
            )

    def hear(number):
        if number < len(rounds):
            pl.semaphore_wait(known.at[number], len(rounds[number]))

    parts = parts_of(n_stream)
    n_waves = parts // 2
    share, small = n_stream // n_waves, n_stream // parts
    deep = n_z // parts
    own_part = lax.div(z, deep)

    def slot_of(stream):
        y, z, core = stream // (n_z * n_core), stream // n_core % n_z, stream % n_core
        return z // deep * small + (y * deep + z % deep) * n_core + core

    stream_in = {slot_of(i): i for i in range(n_stream)}
    at_home = own_part * small + (y * deep + lax.rem(z, deep)) * n_core + core

    def members(part):
        found = []
        for dy in reversed(range(n_y)):
            for dz in reversed(range(deep)):
                for dc in reversed(range(n_core)):
                    at_y, at_z, at_core = (
                        lax.rem(y + dy, n_y),
                        lax.rem(z + dz, deep),
                        lax.rem(core + dc, n_core),
                    )
                    found.append(
                        (
                            at_y * (n_z * n_core) + (part * deep + at_z) * n_core + at_core,
                            part * small + (at_y * deep + at_z) * n_core + at_core,
                        )
                    )
        return found

    n_x = n_et // 2
    x, y_low = lax.div(me, 2), lax.rem(me, 2)
    et_far_first = [
        lax.rem(x + dx, n_x) * 2 + lax.rem(y_low + dy, 2)
        for dx in sorted(range(n_x), key=lambda i: -min(i, n_x - i))
        for dy in (1, 0)
        if dx or dy
    ]

    def et_copy(exchange, source, target, peer):
        return pltpu.make_async_remote_copy(
            src_ref=source,
            dst_ref=target,
            send_sem=et_send.at[exchange, peer],
            recv_sem=et_recv.at[exchange, me],
            device_id=(me_s, peer),
            device_id_type=MESH,
        )

    def et_arrival(exchange, source, target, peer):
        return pltpu.make_async_remote_copy(
            src_ref=source,
            dst_ref=target,
            send_sem=et_send.at[exchange, peer],
            recv_sem=et_recv.at[exchange, peer],
            device_id=(me_s, peer),
            device_id_type=MESH,
        )

    def stream_copy(exchange, number, source, target, peer):
        return pltpu.make_async_remote_copy(
            src_ref=source,
            dst_ref=target,
            send_sem=stream_send.at[exchange, number],
            recv_sem=stream_recv.at[exchange, at_home],
            device_id=(peer, me),
            device_id_type=MESH,
        )

    def stream_arrival(exchange, source, target, slot):
        return pltpu.make_async_copy(source, target, stream_recv.at[exchange, slot])

    def unless_home(part, body):
        pl.when(own_part != part)(body)

    def loop(n, body):
        def step(i, carry):
            body(i)
            return carry

        lax.fori_loop(1, n, step, 0)

    loads = {}

    def load(name, source, target):
        loads[name] = pltpu.make_async_copy(source, target, load_sem.at[len(loads)])
        loads[name].start()

    load("own", res_hbm, features.at[me])

    barrier = pltpu.get_barrier_semaphore()
    greeted = [(me_s, peer) for peer in et_far_first]
    greeted += [(stream_at(*away), me) for away in along(1) + across]
    for device in greeted:
        pl.semaphore_signal(barrier, inc=1, device_id=device, device_id_type=MESH)

    pl.semaphore_wait(barrier, len(greeted))

    loads["own"].wait()
    for peer in et_far_first:
        et_copy(FEATURES, features.at[me], features.at[me], peer).start()
    tell(0)

    load("length", length_hbm, length)
    load("w_q", w_q_hbm, w_q)
    load("w_kv", w_kv_hbm, w_kv)
    load("attn_gain", attn_gain_hbm, attn_gain)
    load("q_gain", q_gain_hbm, q_gain)
    load("key_gain", key_gain_hbm, key_gain)
    load("cache", cache_hbm, cache)

    loads["length"].wait()
    lengths = jnp.broadcast_to(length[...], (tokens, tokens)).astype(F32)
    diagonal = iota((tokens, tokens), 0) == iota((tokens, tokens), 1)
    positions = jnp.sum(jnp.where(diagonal, lengths, 0.0), axis=1, keepdims=True)
    turn = head_dim // 2
    lane = iota((tokens, head_dim), 1)
    steps = jnp.where(lane < turn, lane, lane - turn).astype(F32)
    angle = positions * jnp.exp(steps * (-2.0 * math.log(ROPE_BASE) / head_dim))
    cosine = jnp.cos(angle)
    sine = jnp.where(lane < turn, -jnp.sin(angle), jnp.sin(angle))

    pad = 16
    row = iota((n_et * pad, LANES), 0)
    col = iota((n_et * pad, LANES), 1)
    peer_of, at = lax.div(row, pad), lax.rem(row, pad)
    n_q = local * own_heads
    picked = jnp.where(
        at < n_q,
        lax.rem(at, own_heads) * tokens + peer_of * local + lax.div(at, own_heads),
        jnp.where(
            at < n_q + local, own_heads * tokens + peer_of * local + at - n_q, -1
        ),
    )
    order_out = jnp.where(col == picked, 1.0, 0.0).astype(BF16)

    loads["attn_gain"].wait()
    loop(
        n_et,
        lambda i: et_arrival(
            FEATURES, res_hbm, features.at[et_peer(i)], et_peer(i)
        ).wait_recv(),
    )
    full = jnp.concatenate([features[i].astype(F32) for i in range(n_et)], axis=1)
    gain = attn_gain[...].astype(F32)
    gain = jnp.concatenate([gain[i : i + 1] for i in range(gain.shape[0])], axis=1)
    normed = (
        full
        * lax.rsqrt(jnp.sum(full * full, axis=1, keepdims=True) * (1.0 / width) + EPS)
        * gain
    ).astype(BF16)

    def rotated(v, g):
        v = v * lax.rsqrt(jnp.mean(v * v, axis=1, keepdims=True) + EPS) * g
        return v * cosine + pltpu.roll(v, turn, 1) * sine

    loads["q_gain"].wait()
    loads["key_gain"].wait()
    loads["w_q"].wait()
    query = dot(normed, w_q[...])
    loads["w_kv"].wait()
    key_value = dot(normed, w_kv[...])
    query_gain = q_gain[...].astype(F32)
    made = [
        rotated(query[:, i * head_dim : (i + 1) * head_dim], query_gain)
        for i in range(own_heads)
    ]
    made.append(
        jnp.where(me < kv_heads, rotated(key_value, key_gain[...].astype(F32)), key_value)
    )
    made.append(jnp.zeros((LANES - (own_heads + 1) * tokens, head_dim), F32))
    made = jnp.concatenate(made, axis=0).astype(BF16)
    heads_out[...] = dot(order_out, made).astype(BF16).reshape(heads_out.shape)
    heads_in[me] = heads_out[me]
    for peer in et_far_first:
        et_copy(HEADS, heads_out.at[peer], heads_in.at[me], peer).start()
    hear(0)
    tell(1)
    load("w_o", w_o_hbm, w_o)
    load("ids", ids_hbm, ids)
    load("gates", gates_hbm, gates)
    load("moe_gain", moe_gain_hbm, moe_gain)
    load("w_gu", w_gu_hbm, w_gu)
    load("w_down", w_down_hbm, w_down)

    per = local * n_heads
    row = iota((3 * per, n_et * pad), 0)
    col = iota((3 * per, n_et * pad), 1)
    kind, at = lax.div(row, per), lax.rem(row, per)
    token, head = lax.div(at, n_heads), lax.rem(at, n_heads)
    picked = jnp.where(
        kind == 0,
        lax.div(head, own_heads) * pad + token * own_heads + lax.rem(head, own_heads),
        (lax.div(head, group) + jnp.where(kind == 2, kv_heads, 0)) * pad + n_q + token,
    )
    order_in = jnp.where(col == picked, 1.0, 0.0).astype(BF16)

    loads["cache"].wait()
    rows_of = cache_hbm.shape[0] // local
    span = rows_of // (2 * kv_heads)
    for t in range(local):
        cache_f[:rows_of, :] = cache[t * rows_of : (t + 1) * rows_of, :].astype(F32)
        for kind in range(2):
            for h in range(kv_heads):
                split[t, kind, h // 2, :, h % 2 * head_dim : (h % 2 + 1) * head_dim] = cache_f[
                    pl.ds(2 * h + kind, span, stride=2 * kv_heads), :
                ].astype(BF16)

    own_lane = iota((1, tokens), 1)
    lengths = length[...].astype(F32)
    pairs = kv_heads // 2
    column = iota((2 * group, span), 1)
    live = []
    for t in range(local):
        limit = jnp.sum(
            jnp.where(own_lane == me * local + t, lengths, 0.0), axis=1, keepdims=True
        ).astype(jnp.int32)
        live.append(column < limit)
    empty = jnp.zeros((group, head_dim), F32)
    loop(
        n_et,
        lambda i: et_arrival(
            HEADS, heads_out.at[et_peer(i)], heads_in.at[et_peer(i)], et_peer(i)
        ).wait_recv(),
    )
    ordered = dot(order_in, heads_in[...].reshape(n_et * pad, head_dim))
    q = ordered[:per]
    blocks = []
    for i in range(local * pairs):
        at = i * 2 * group
        upper = jnp.concatenate([q[at : at + group], empty], axis=1)
        lower = jnp.concatenate([empty, q[at + group : at + 2 * group]], axis=1)
        blocks.append(jnp.concatenate([upper, lower], axis=0).astype(BF16))
    scores = [
        dot_nt(block, split[i // pairs, 0, i % pairs]) for i, block in enumerate(blocks)
    ]
    weights = [
        jnp.where(live[i // pairs], jnp.exp(score * scale), 0.0)
        for i, score in enumerate(scores)
    ]
    summed = [
        dot(weight.astype(BF16), split[i // pairs, 1, i % pairs])
        for i, weight in enumerate(weights)
    ]
    fresh = jnp.exp(jnp.sum(q * ordered[per : 2 * per], axis=1, keepdims=True) * scale)
    total = fresh + jnp.concatenate(
        [jnp.sum(weight, axis=1, keepdims=True) for weight in weights], axis=0
    )
    summed = jnp.concatenate(
        [
            part
            for both in summed
            for part in (both[:group, :head_dim], both[group:, head_dim:])
        ],
        axis=0,
    )
    mixed_out[...] = ((summed + fresh * ordered[2 * per :]) / total).astype(BF16)
    mixed_in[me] = mixed_out[...]
    for peer in et_far_first:
        et_copy(MIXED, mixed_out, mixed_in.at[me], peer).start()
    hear(1)
    tell(2)

    loads["ids"].wait()
    loads["gates"].wait()
    at = iota((slots, tokens), 0)
    place = lax.rem(at, n_local * CAP)
    expert = lax.div(at, n_local * CAP) * n_local + lax.rem(place, n_local)
    which = lax.div(place, n_local)
    gate = gates[...]
    gate = gate / jnp.sum(gate, axis=0, keepdims=True)
    named = jnp.zeros((slots, tokens), F32)
    weight = jnp.zeros((slots, tokens), F32)
    for k in range(ids_hbm.shape[0]):
        hit = expert == ids[k : k + 1, :]
        named = jnp.where(hit, 1.0, named)
        weight = jnp.where(hit, gate[k : k + 1, :], weight)
    before = jnp.where(
        iota((tokens, tokens), 0) < iota((tokens, tokens), 1), 1.0, 0.0
    ).astype(BF16)
    earlier = dot(named.astype(BF16), before)
    placed = jnp.where(earlier == which.astype(F32), named, 0.0)
    mixing = placed * weight
    placed = placed.astype(BF16)
    mixing_high = mixing.astype(BF16)
    mixing_low = (mixing - mixing_high.astype(F32)).astype(BF16)

    loads["w_o"].wait()
    loop(
        n_et,
        lambda i: et_arrival(
            MIXED, mixed_out, mixed_in.at[et_peer(i)], et_peer(i)
        ).wait_recv(),
    )
    mixed_f[: tokens * n_heads, :] = (
        mixed_in[...].reshape(tokens * n_heads, head_dim).astype(F32)
    )
    attended = jnp.concatenate(
        [mixed_f[pl.ds(h, tokens, stride=n_heads), :] for h in range(n_heads)], axis=1
    ).astype(BF16)
    resid = (features[me].astype(F32) + dot(attended, w_o[...])).astype(BF16)

    sent = dot(placed, resid)
    sent = sent.reshape(n_stream, n_local * CAP, 2 * LANES)
    rows_out[...] = jnp.concatenate(
        [sent[:, :, :LANES], sent[:, :, LANES:]], axis=1
    ).astype(BF16)
    hear(2)
    beside = own_part + 1 - 2 * lax.rem(own_part, 2)
    order = [beside, own_part]
    if parts == 4:
        order = [lax.rem(part + 2, parts) for part in order] + order
    outward = [peer for part in order for peer, _ in members(part)][:-1]
    for number, peer in enumerate(outward):
        stream_copy(OUTWARD, number, rows_out.at[peer], rows_in.at[at_home], peer).start()
    stream_arrival(OUTWARD, rows_out.at[me_s], rows_in.at[at_home], at_home).start()
    loads["moe_gain"].wait()
    gain = moe_gain[...].astype(F32)
    gain = jnp.concatenate([gain[0:1], gain[1:2]], axis=1)
    loads["w_gu"].wait()
    chunk = 2 * n_local * CAP
    hidden_width = w_down_hbm.shape[1]

    left_lanes = iota((CAP * small, LANES), 1) < LANES // 2
    for part in range(parts):
        w, odd = part // 2, part % 2
        for slot in range(part * small, (part + 1) * small):
            stream_arrival(OUTWARD, rows_out.at[0], rows_in.at[slot], slot).wait()
        rows_f[part * small * chunk : (part + 1) * small * chunk, :] = (
            rows_in[part * small : (part + 1) * small].reshape(small * chunk, LANES).astype(F32)
        )
        for j in range(n_local):
            taken = []
            for c in range(CAP):
                first = part * small * chunk + c * n_local + j
                taken.append(
                    jnp.concatenate(
                        [
                            rows_f[pl.ds(first + h * n_local * CAP, small, stride=chunk), :]
                            for h in range(2)
                        ],
                        axis=1,
                    )
                )
            taken = jnp.concatenate(taken, axis=0)
            expert_squares[part, j] = jnp.broadcast_to(
                jnp.sum(taken * taken, axis=1, keepdims=True), (CAP * small, LANES)
            )
            expert_rows[part, j] = (taken * gain).astype(BF16)
        sent, received = (pairs_odd, pairs_in_odd) if odd else (pairs_even, pairs_in_even)
        for i in range(n_local):
            j = lax.rem(lax.div(me, CAP) + (2, 1, 3, 0)[i], n_local)
            taken = expert_rows[part, j]
            halves = [dot(taken, w_gu[j, 0]), dot(taken, w_gu[j, 1])]
            if odd:
                squares = jnp.where(
                    left_lanes, expert_squares[part - 1, j], expert_squares[part, j]
                )
                high = squares.astype(BF16).astype(F32)
                halves = [
                    jnp.concatenate([halves[0], high], axis=1),
                    jnp.concatenate([halves[1], squares - high], axis=1),
                ]
            for c in range(CAP):
                products = jnp.concatenate(
                    [value[c * small : (c + 1) * small] for value in halves], axis=0
                )
                sent[w, i, c] = products.astype(BF16)
                if i == n_local - 1:
                    pairs_own[part, c, :, : products.shape[1]] = products
            for c in (y_low, 1 - y_low) if i < n_local - 1 else (1 - y_low,):
                et_copy(
                    PAIRS + part, sent.at[w, i, c], received.at[w, me], CAP * j + c
                ).start()
    for w in range(n_waves):
        sums = []
        for part in (2 * w, 2 * w + 1):
            odd = part % 2
            sent, received = (pairs_odd, pairs_in_odd) if odd else (pairs_even, pairs_in_even)
            pair = pairs_own[part, y_low, :, : received.shape[3]]
            for i in range(1, n_et):
                et_arrival(
                    PAIRS + part, sent.at[w, 0, 0], received.at[w, et_peer(i)], et_peer(i)
                ).wait_recv()
                pair = pair + received[w, et_peer(i)].astype(F32)
            sums.append(pair)
        squares = sums[1][:small, hidden_width:] + sums[1][small:, hidden_width:]
        left = iota((small, LANES), 1) < LANES // 2
        made = []
        for pair, lanes in zip(sums, (left, ~left)):
            level = lax.rsqrt(
                jnp.sum(jnp.where(lanes, squares, 0.0), axis=1, keepdims=True)
                * (2.0 / LANES / width)
                + EPS
            )
            first = pair[:small, :hidden_width] * level
            second = pair[small:, :hidden_width] * level
            made.append(first / (1.0 + jnp.exp(-first)) * second)
        hidden_out[w] = jnp.concatenate(made, axis=0).astype(BF16)
        for peer in et_far_first:
            et_copy(HIDDEN + w, hidden_out.at[w], hidden_in.at[w, me], peer).start()
        hidden_in[w, me] = hidden_out[w]

    loads["w_down"].wait()
    for w in range(n_waves):
        loop(
            n_et,
            lambda i: et_arrival(
                HIDDEN + w, hidden_out.at[w], hidden_in.at[w, et_peer(i)], et_peer(i)
            ).wait_recv(),
        )
        for j in range(n_local):
            hidden = hidden_in[w, CAP * j : CAP * (j + 1)].reshape(CAP * share, hidden_width)
            result = dot(hidden, w_down[j])
            for c in range(CAP):
                for h in range(2):
                    first = w * share * chunk + h * n_local * CAP + c * n_local + j
                    results_f[pl.ds(first, share, stride=chunk), :] = result[
                        c * share : (c + 1) * share, h * LANES : (h + 1) * LANES
                    ]
        results_out[w * share : (w + 1) * share] = (
            results_f[w * share * chunk : (w + 1) * share * chunk, :]
            .astype(BF16)
            .reshape(share, chunk, LANES)
        )
        for part in (2 * w, 2 * w + 1):
            *rest, (last, place) = members(part)
            for number, (peer, slot) in enumerate(rest):
                stream_copy(
                    HOME, part * small + number, results_out.at[slot], results_in.at[me_s], peer
                ).start()
            unless_home(
                part,
                lambda: stream_copy(
                    HOME, (part + 1) * small - 1, results_out.at[place], results_in.at[me_s], last
                ).start(),
            )
    stream_arrival(HOME, results_out.at[at_home], results_in.at[me_s], at_home).start()

    def sent_et(exchange, source, target):
        loop(
            n_et,
            lambda i: et_copy(exchange, source, target, et_peer(i)).wait_send(),
        )

    sent_et(FEATURES, features.at[me], features.at[me])
    sent_et(HEADS, heads_out.at[0], heads_in.at[me])
    sent_et(MIXED, mixed_out, mixed_in.at[me])
    for part in range(parts):
        sent, received = (pairs_odd, pairs_in_odd) if part % 2 else (pairs_even, pairs_in_even)
        sent_et(PAIRS + part, sent.at[part // 2, 0, 0], received.at[part // 2, me])
    for w in range(n_waves):
        sent_et(HIDDEN + w, hidden_out.at[w], hidden_in.at[w, me])
    for number, peer in enumerate(outward):
        stream_copy(OUTWARD, number, rows_out.at[0], rows_in.at[at_home], peer).wait_send()
    for part in range(parts):
        *rest, (last, _) = members(part)
        for number, (peer, _) in enumerate(rest):
            stream_copy(
                HOME, part * small + number, results_out.at[0], results_in.at[me_s], peer
            ).wait_send()
        unless_home(
            part,
            lambda: stream_copy(
                HOME, (part + 1) * small - 1, results_out.at[0], results_in.at[me_s], last
            ).wait_send(),
        )

    for slot in range(n_stream):
        stream_arrival(
            HOME, results_out.at[0], results_in.at[stream_in[slot]], slot
        ).wait()
    returned = results_in[...].astype(F32)
    returned = (
        jnp.concatenate(
            [returned[:, : n_local * CAP], returned[:, n_local * CAP :]], axis=2
        )
        .reshape(slots, 2 * LANES)
        .astype(BF16)
    )
    routed = dot_tn(mixing_high, returned) + dot_tn(mixing_low, returned)
    out_ref[...] = (resid.astype(F32) + routed).astype(BF16)


def on_device(
    n_stream,
    n_et,
    residual_in,
    attn_gain,
    q_gain,
    key_norm_gain,
    w_q,
    key_value_weight,
    w_o,
    key_value_cache,
    cache_length,
    moe_gain,
    route_ids,
    route_gates,
    w_gate_up,
    w_down,
):
    tokens, features = residual_in.shape
    head_dim = q_gain.shape[0]
    local, span, _, kv_width = key_value_cache.shape
    kv_heads = kv_width // head_dim
    n_heads = w_q.shape[1] // head_dim * n_et
    n_local = w_gate_up.shape[0]
    hidden = w_down.shape[1]
    cache = (
        key_value_cache.reshape(local, span, 2, kv_heads, head_dim)
        .transpose(0, 1, 3, 2, 4)
        .reshape(local * span * kv_heads * 2, head_dim)
    )
    args = (
        residual_in,
        attn_gain.reshape(-1, LANES),
        q_gain.reshape(1, -1),
        key_norm_gain.reshape(1, -1),
        w_q,
        key_value_weight,
        w_o,
        cache,
        cache_length.reshape(1, -1),
        moe_gain.reshape(-1, LANES),
        route_ids.T,
        route_gates.T,
        w_gate_up,
        w_down,
    )
    chunk = 2 * n_local * CAP
    vmem = pltpu.VMEM
    row_blocks = (n_stream, chunk, LANES)
    flat_rows = ((n_stream + 1) * chunk, LANES)
    parts = parts_of(n_stream)
    n_waves = parts // 2
    share, small = n_stream // n_waves, n_stream // parts
    scratch = [vmem(a.shape, a.dtype) for a in args[1:]] + [
        vmem(((span + 1) * kv_heads * 2, head_dim), F32),
        vmem((local, 2, kv_heads // 2, span, 2 * head_dim), BF16),
        vmem((n_et, tokens, features), BF16),
        vmem((n_et, 16, head_dim), BF16),
        vmem((n_et, 16, head_dim), BF16),
        vmem((local * n_heads, head_dim), BF16),
        vmem((n_et, local * n_heads, head_dim), BF16),
        vmem(((tokens + 1) * n_heads, head_dim), F32),
        vmem(row_blocks, BF16),
        vmem(row_blocks, BF16),
        vmem(flat_rows, F32),
        vmem((parts, n_local, CAP * small, features), BF16),
        vmem((parts, n_local, CAP * small, LANES), F32),
        vmem((n_waves, n_local, CAP, 2 * small, hidden), BF16),
        vmem((n_waves, n_local, CAP, 2 * small, hidden + LANES), BF16),
        vmem((parts, CAP, 2 * small, hidden + LANES), F32),
        vmem((n_waves, n_et, 2 * small, hidden), BF16),
        vmem((n_waves, n_et, 2 * small, hidden + LANES), BF16),
        vmem((n_waves, share, hidden), BF16),
        vmem((n_waves, n_et, share, hidden), BF16),
        vmem(flat_rows, F32),
        vmem(row_blocks, BF16),
        vmem(row_blocks, BF16),
        pltpu.SemaphoreType.DMA((len(args),)),
        pltpu.SemaphoreType.DMA((9, n_et)),
        pltpu.SemaphoreType.DMA((9, n_et)),
        pltpu.SemaphoreType.DMA((2, n_stream)),
        pltpu.SemaphoreType.DMA((2, n_stream)),
        pltpu.SemaphoreType.REGULAR((3,)),
    ]
    return pl.pallas_call(
        functools.partial(kernel, n_stream, n_et),
        out_shape=pltpu.VMEM(residual_in.shape, residual_in.dtype),
        in_specs=[pl.BlockSpec(memory_space=pl.ANY)] * len(args),
        out_specs=pl.BlockSpec(memory_space=pltpu.VMEM),
        scratch_shapes=scratch,
        compiler_params=pltpu.CompilerParams(
            collective_id=0, has_side_effects=True, vmem_limit_bytes=56 * 1024 * 1024
        ),
    )(*args)


def solution(mesh):
    placed = (
        P("stream", "et"),
        P(),
        P(),
        P(),
        P(None, "et"),
        P(None, "et"),
        P(None, "et"),
        P(("stream", "et"), None, None, None),
        P("stream"),
        P("et"),
        P("stream", None),
        P("stream", None),
        P("stream", None, "et", None),
        P("stream", None, "et"),
    )
    return jax.shard_map(
        functools.partial(on_device, mesh.shape["stream"], mesh.shape["et"]),
        mesh=mesh,
        in_specs=placed,
        out_specs=P("stream", "et"),
        check_vma=False,
    )
```

```python
import functools
import math

import jax
import jax.numpy as jnp
from jax import lax
from jax.experimental import pallas as pl
from jax.experimental.pallas import tpu as pltpu
from jax.sharding import PartitionSpec as P

EPS = 1e-06
ROPE_BASE = 1000000.0
CAP = 2
LANES = 128
MESH = pl.DeviceIdType.MESH
F32 = jnp.float32
BF16 = jnp.bfloat16

FEATURES, HEADS, MIXED, PAIRS, HIDDEN = 0, 1, 2, 3, 7
OUTWARD, HOME = range(2)


def parts_of(n_stream):
    return 4 if n_stream % 16 == 0 else 2


def iota(shape, dim):
    return lax.broadcasted_iota(jnp.int32, shape, dim)


def dot(a, b):
    return jnp.dot(a, b, preferred_element_type=F32)


def dot_nt(a, b):
    return lax.dot_general(a, b, (((1,), (1,)), ((), ())), preferred_element_type=F32)


def dot_tn(a, b):
    return lax.dot_general(a, b, (((0,), (0,)), ((), ())), preferred_element_type=F32)


def kernel(
    n_stream,
    n_et,
    res_hbm,
    attn_gain_hbm,
    q_gain_hbm,
    key_gain_hbm,
    w_q_hbm,
    w_kv_hbm,
    w_o_hbm,
    cache_hbm,
    length_hbm,
    moe_gain_hbm,
    ids_hbm,
    gates_hbm,
    w_gu_hbm,
    w_down_hbm,
    out_ref,
    attn_gain,
    q_gain,
    key_gain,
    w_q,
    w_kv,
    w_o,
    cache,
    length,
    moe_gain,
    ids,
    gates,
    w_gu,
    w_down,
    cache_f,
    split,
    features,
    heads_out,
    heads_in,
    mixed_out,
    mixed_in,
    mixed_f,
    rows_out,
    rows_in,
    rows_f,
    expert_rows,
    expert_squares,
    pairs_even,
    pairs_odd,
    pairs_own,
    pairs_in_even,
    pairs_in_odd,
    hidden_out,
    hidden_in,
    results_f,
    results_out,
    results_in,
    load_sem,
    et_send,
    et_recv,
    stream_send,
    stream_recv,
    known,
):
    me_s = lax.axis_index("stream")
    me = lax.axis_index("et")
    tokens = res_hbm.shape[0]
    local = tokens // n_et
    head_dim = q_gain_hbm.shape[1]
    own_heads = w_q_hbm.shape[1] // head_dim
    n_heads = own_heads * n_et
    kv_heads = n_et // 2
    group = n_heads // kv_heads
    width = res_hbm.shape[1] * n_et
    n_local = w_gu_hbm.shape[0]
    slots = n_stream * n_local * CAP
    scale = head_dim**-0.5

    def et_peer(step):
        return lax.rem(me + step, n_et)

    def stream_peer(step):
        return lax.rem(me_s + step, n_stream)

    n_y, n_z, n_core = (2, n_stream // 4, 2) if n_stream % 4 == 0 else (1, 1, n_stream)
    y, z, core = lax.div(me_s, n_z * n_core), lax.rem(lax.div(me_s, n_core), n_z), lax.rem(me_s, n_core)

    def stream_at(dy, dz, dc):
        return (
            lax.rem(y + dy, n_y) * (n_z * n_core)
            + lax.rem(z + dz, n_z) * n_core
            + lax.rem(core + dc, n_core)
        )

    across = [(dy, 0, dc) for dy in range(n_y) for dc in range(n_core) if dy or dc]

    def along(reach):
        return [(0, dz, 0) for dz in sorted({reach % n_z, -reach % n_z} - {0})]

    rounds = []
    reach = 1
    while reach < n_z // 2:
        rounds.append(along(reach))
        reach *= 2
    rounds.append(across)

    def tell(number):
        for away in rounds[number] if number < len(rounds) else ():
            pl.semaphore_signal(
                known.at[number],
                inc=1,
                device_id=(stream_at(*away), me),
                device_id_type=MESH,
            )

    def hear(number):
        if number < len(rounds):
            pl.semaphore_wait(known.at[number], len(rounds[number]))

    parts = parts_of(n_stream)
    n_waves = parts // 2
    share, small = n_stream // n_waves, n_stream // parts
    deep = n_z // parts
    own_part = lax.div(z, deep)

    def slot_of(stream):
        y, z, core = stream // (n_z * n_core), stream // n_core % n_z, stream % n_core
        return z // deep * small + (y * deep + z % deep) * n_core + core

    stream_in = {slot_of(i): i for i in range(n_stream)}
    at_home = own_part * small + (y * deep + lax.rem(z, deep)) * n_core + core

    def members(part):
        found = []
        for dy in reversed(range(n_y)):
            for dz in reversed(range(deep)):
                for dc in reversed(range(n_core)):
                    at_y, at_z, at_core = (
                        lax.rem(y + dy, n_y),
                        lax.rem(z + dz, deep),
                        lax.rem(core + dc, n_core),
                    )
                    found.append(
                        (
                            at_y * (n_z * n_core) + (part * deep + at_z) * n_core + at_core,
                            part * small + (at_y * deep + at_z) * n_core + at_core,
                        )
                    )
        return found

    n_x = n_et // 2
    x, y_low = lax.div(me, 2), lax.rem(me, 2)
    et_far_first = [
        lax.rem(x + dx, n_x) * 2 + lax.rem(y_low + dy, 2)
        for dx in sorted(range(n_x), key=lambda i: -min(i, n_x - i))
        for dy in (1, 0)
        if dx or dy
    ]

    def et_copy(exchange, source, target, peer):
        return pltpu.make_async_remote_copy(
            src_ref=source,
            dst_ref=target,
            send_sem=et_send.at[exchange, peer],
            recv_sem=et_recv.at[exchange, me],
            device_id=(me_s, peer),
            device_id_type=MESH,
        )

    def et_arrival(exchange, source, target, peer):
        return pltpu.make_async_remote_copy(
            src_ref=source,
            dst_ref=target,
            send_sem=et_send.at[exchange, peer],
            recv_sem=et_recv.at[exchange, peer],
            device_id=(me_s, peer),
            device_id_type=MESH,
        )

    def stream_copy(exchange, number, source, target, peer):
        return pltpu.make_async_remote_copy(
            src_ref=source,
            dst_ref=target,
            send_sem=stream_send.at[exchange, number],
            recv_sem=stream_recv.at[exchange, at_home],
            device_id=(peer, me),
            device_id_type=MESH,
        )

    def stream_arrival(exchange, source, target, slot):
        return pltpu.make_async_copy(source, target, stream_recv.at[exchange, slot])

    def unless_home(part, body):
        pl.when(own_part != part)(body)

    def loop(n, body):
        def step(i, carry):
            body(i)
            return carry

        lax.fori_loop(1, n, step, 0)

    loads = {}

    def load(name, source, target):
        loads[name] = pltpu.make_async_copy(source, target, load_sem.at[len(loads)])
        loads[name].start()

    load("own", res_hbm, features.at[me])

    barrier = pltpu.get_barrier_semaphore()
    greeted = [(me_s, peer) for peer in et_far_first]
    greeted += [(stream_at(*away), me) for away in along(1) + across]
    for device in greeted:
        pl.semaphore_signal(barrier, inc=1, device_id=device, device_id_type=MESH)

    pl.semaphore_wait(barrier, len(greeted))

    loads["own"].wait()
    for peer in et_far_first:
        et_copy(FEATURES, features.at[me], features.at[me], peer).start()
    tell(0)

    load("length", length_hbm, length)
    load("w_q", w_q_hbm, w_q)
    load("w_kv", w_kv_hbm, w_kv)
    load("attn_gain", attn_gain_hbm, attn_gain)
    load("q_gain", q_gain_hbm, q_gain)
    load("key_gain", key_gain_hbm, key_gain)
    load("cache", cache_hbm, cache)

    loads["length"].wait()
    lengths = jnp.broadcast_to(length[...], (tokens, tokens)).astype(F32)
    diagonal = iota((tokens, tokens), 0) == iota((tokens, tokens), 1)
    positions = jnp.sum(jnp.where(diagonal, lengths, 0.0), axis=1, keepdims=True)
    turn = head_dim // 2
    lane = iota((tokens, head_dim), 1)
    steps = jnp.where(lane < turn, lane, lane - turn).astype(F32)
    angle = positions * jnp.exp(steps * (-2.0 * math.log(ROPE_BASE) / head_dim))
    cosine = jnp.cos(angle)
    sine = jnp.where(lane < turn, -jnp.sin(angle), jnp.sin(angle))

    pad = 16
    row = iota((n_et * pad, LANES), 0)
    col = iota((n_et * pad, LANES), 1)
    peer_of, at = lax.div(row, pad), lax.rem(row, pad)
    n_q = local * own_heads
    picked = jnp.where(
        at < n_q,
        lax.rem(at, own_heads) * tokens + peer_of * local + lax.div(at, own_heads),
        jnp.where(
            at < n_q + local, own_heads * tokens + peer_of * local + at - n_q, -1
        ),
    )
    order_out = jnp.where(col == picked, 1.0, 0.0).astype(BF16)

    loads["attn_gain"].wait()
    loop(
        n_et,
        lambda i: et_arrival(
            FEATURES, res_hbm, features.at[et_peer(i)], et_peer(i)
        ).wait_recv(),
    )
    full = jnp.concatenate([features[i].astype(F32) for i in range(n_et)], axis=1)
    gain = attn_gain[...].astype(F32)
    gain = jnp.concatenate([gain[i : i + 1] for i in range(gain.shape[0])], axis=1)
    normed = (
        full
        * lax.rsqrt(jnp.sum(full * full, axis=1, keepdims=True) * (1.0 / width) + EPS)
        * gain
    ).astype(BF16)

    def rotated(v, g):
        v = v * lax.rsqrt(jnp.mean(v * v, axis=1, keepdims=True) + EPS) * g
        return v * cosine + pltpu.roll(v, turn, 1) * sine

    loads["q_gain"].wait()
    loads["key_gain"].wait()
    loads["w_q"].wait()
    query = dot(normed, w_q[...])
    loads["w_kv"].wait()
    key_value = dot(normed, w_kv[...])
    query_gain = q_gain[...].astype(F32)
    made = [
        rotated(query[:, i * head_dim : (i + 1) * head_dim], query_gain)
        for i in range(own_heads)
    ]
    made.append(
        jnp.where(me < kv_heads, rotated(key_value, key_gain[...].astype(F32)), key_value)
    )
    made.append(jnp.zeros((LANES - (own_heads + 1) * tokens, head_dim), F32))
    made = jnp.concatenate(made, axis=0).astype(BF16)
    heads_out[...] = dot(order_out, made).astype(BF16).reshape(heads_out.shape)
    heads_in[me] = heads_out[me]
    for peer in et_far_first:
        et_copy(HEADS, heads_out.at[peer], heads_in.at[me], peer).start()
    hear(0)
    tell(1)
    load("w_o", w_o_hbm, w_o)
    load("ids", ids_hbm, ids)
    load("gates", gates_hbm, gates)
    load("moe_gain", moe_gain_hbm, moe_gain)
    load("w_gu", w_gu_hbm, w_gu)
    load("w_down", w_down_hbm, w_down)

    per = local * n_heads
    row = iota((3 * per, n_et * pad), 0)
    col = iota((3 * per, n_et * pad), 1)
    kind, at = lax.div(row, per), lax.rem(row, per)
    token, head = lax.div(at, n_heads), lax.rem(at, n_heads)
    picked = jnp.where(
        kind == 0,
        lax.div(head, own_heads) * pad + token * own_heads + lax.rem(head, own_heads),
        (lax.div(head, group) + jnp.where(kind == 2, kv_heads, 0)) * pad + n_q + token,
    )
    order_in = jnp.where(col == picked, 1.0, 0.0).astype(BF16)

    loads["cache"].wait()
    rows_of = cache_hbm.shape[0] // local
    span = rows_of // (2 * kv_heads)
    for t in range(local):
        cache_f[:rows_of, :] = cache[t * rows_of : (t + 1) * rows_of, :].astype(F32)
        for kind in range(2):
            for h in range(kv_heads):
                split[t, kind, h // 2, :, h % 2 * head_dim : (h % 2 + 1) * head_dim] = cache_f[
                    pl.ds(2 * h + kind, span, stride=2 * kv_heads), :
                ].astype(BF16)

    own_lane = iota((1, tokens), 1)
    lengths = length[...].astype(F32)
    pairs = kv_heads // 2
    column = iota((2 * group, span), 1)
    live = []
    for t in range(local):
        limit = jnp.sum(
            jnp.where(own_lane == me * local + t, lengths, 0.0), axis=1, keepdims=True
        ).astype(jnp.int32)
        live.append(column < limit)
    empty = jnp.zeros((group, head_dim), F32)
    loop(
        n_et,
        lambda i: et_arrival(
            HEADS, heads_out.at[et_peer(i)], heads_in.at[et_peer(i)], et_peer(i)
        ).wait_recv(),
    )
    ordered = dot(order_in, heads_in[...].reshape(n_et * pad, head_dim))
    q = ordered[:per]
    blocks = []
    for i in range(local * pairs):
        at = i * 2 * group
        upper = jnp.concatenate([q[at : at + group], empty], axis=1)
        lower = jnp.concatenate([empty, q[at + group : at + 2 * group]], axis=1)
        blocks.append(jnp.concatenate([upper, lower], axis=0).astype(BF16))
    scores = [
        dot_nt(block, split[i // pairs, 0, i % pairs]) for i, block in enumerate(blocks)
    ]
    weights = [
        jnp.where(live[i // pairs], jnp.exp(score * scale), 0.0)
        for i, score in enumerate(scores)
    ]
    summed = [
        dot(weight.astype(BF16), split[i // pairs, 1, i % pairs])
        for i, weight in enumerate(weights)
    ]
    fresh = jnp.exp(jnp.sum(q * ordered[per : 2 * per], axis=1, keepdims=True) * scale)
    total = fresh + jnp.concatenate(
        [jnp.sum(weight, axis=1, keepdims=True) for weight in weights], axis=0
    )
    summed = jnp.concatenate(
        [
            part
            for both in summed
            for part in (both[:group, :head_dim], both[group:, head_dim:])
        ],
        axis=0,
    )
    mixed_out[...] = ((summed + fresh * ordered[2 * per :]) / total).astype(BF16)
    mixed_in[me] = mixed_out[...]
    for peer in et_far_first:
        et_copy(MIXED, mixed_out, mixed_in.at[me], peer).start()
    hear(1)
    tell(2)

    loads["ids"].wait()
    loads["gates"].wait()
    at = iota((slots, tokens), 0)
    place = lax.rem(at, n_local * CAP)
    expert = lax.div(at, n_local * CAP) * n_local + lax.rem(place, n_local)
    which = lax.div(place, n_local)
    gate = gates[...]
    gate = gate / jnp.sum(gate, axis=0, keepdims=True)
    named = jnp.zeros((slots, tokens), F32)
    weight = jnp.zeros((slots, tokens), F32)
    for k in range(ids_hbm.shape[0]):
        hit = expert == ids[k : k + 1, :]
        named = jnp.where(hit, 1.0, named)
        weight = jnp.where(hit, gate[k : k + 1, :], weight)
    before = jnp.where(
        iota((tokens, tokens), 0) < iota((tokens, tokens), 1), 1.0, 0.0
    ).astype(BF16)
    earlier = dot(named.astype(BF16), before)
    placed = jnp.where(earlier == which.astype(F32), named, 0.0)
    mixing = placed * weight
    placed = placed.astype(BF16)
    mixing_high = mixing.astype(BF16)
    mixing_low = (mixing - mixing_high.astype(F32)).astype(BF16)

    loads["w_o"].wait()
    loop(
        n_et,
        lambda i: et_arrival(
            MIXED, mixed_out, mixed_in.at[et_peer(i)], et_peer(i)
        ).wait_recv(),
    )
    mixed_f[: tokens * n_heads, :] = (
        mixed_in[...].reshape(tokens * n_heads, head_dim).astype(F32)
    )
    attended = jnp.concatenate(
        [mixed_f[pl.ds(h, tokens, stride=n_heads), :] for h in range(n_heads)], axis=1
    ).astype(BF16)
    resid = (features[me].astype(F32) + dot(attended, w_o[...])).astype(BF16)

    sent = dot(placed, resid)
    sent = sent.reshape(n_stream, n_local * CAP, 2 * LANES)
    rows_out[...] = jnp.concatenate(
        [sent[:, :, :LANES], sent[:, :, LANES:]], axis=1
    ).astype(BF16)
    hear(2)
    beside = own_part + 1 - 2 * lax.rem(own_part, 2)
    order = [beside, own_part]
    if parts == 4:
        order = [lax.rem(part + 2, parts) for part in order] + order
    outward = [peer for part in order for peer, _ in members(part)][:-1]
    for number, peer in enumerate(outward):
        stream_copy(OUTWARD, number, rows_out.at[peer], rows_in.at[at_home], peer).start()
    stream_arrival(OUTWARD, rows_out.at[me_s], rows_in.at[at_home], at_home).start()
    loads["moe_gain"].wait()
    gain = moe_gain[...].astype(F32)
    gain = jnp.concatenate([gain[0:1], gain[1:2]], axis=1)
    loads["w_gu"].wait()
    chunk = 2 * n_local * CAP
    hidden_width = w_down_hbm.shape[1]

    left_lanes = iota((CAP * small, LANES), 1) < LANES // 2
    for part in range(parts):
        w, odd = part // 2, part % 2
        for slot in range(part * small, (part + 1) * small):
            stream_arrival(OUTWARD, rows_out.at[0], rows_in.at[slot], slot).wait()
        rows_f[part * small * chunk : (part + 1) * small * chunk, :] = (
            rows_in[part * small : (part + 1) * small].reshape(small * chunk, LANES).astype(F32)
        )
        for j in range(n_local):
            taken = []
            for c in range(CAP):
                first = part * small * chunk + c * n_local + j
                taken.append(
                    jnp.concatenate(
                        [
                            rows_f[pl.ds(first + h * n_local * CAP, small, stride=chunk), :]
                            for h in range(2)
                        ],
                        axis=1,
                    )
                )
            taken = jnp.concatenate(taken, axis=0)
            expert_squares[part, j] = jnp.broadcast_to(
                jnp.sum(taken * taken, axis=1, keepdims=True), (CAP * small, LANES)
            )
            expert_rows[part, j] = (taken * gain).astype(BF16)
        sent, received = (pairs_odd, pairs_in_odd) if odd else (pairs_even, pairs_in_even)
        for i in range(n_local):
            j = lax.rem(lax.div(me, CAP) + (2, 1, 3, 0)[i], n_local)
            taken = expert_rows[part, j]
            halves = [dot(taken, w_gu[j, 0]), dot(taken, w_gu[j, 1])]
            if odd:
                squares = jnp.where(
                    left_lanes, expert_squares[part - 1, j], expert_squares[part, j]
                )
                high = squares.astype(BF16).astype(F32)
                halves = [
                    jnp.concatenate([halves[0], high], axis=1),
                    jnp.concatenate([halves[1], squares - high], axis=1),
                ]
            for c in range(CAP):
                products = jnp.concatenate(
                    [value[c * small : (c + 1) * small] for value in halves], axis=0
                )
                sent[w, i, c] = products.astype(BF16)
                if i == n_local - 1:
                    pairs_own[part, c, :, : products.shape[1]] = products
            for c in (y_low, 1 - y_low) if i < n_local - 1 else (1 - y_low,):
                et_copy(
                    PAIRS + part, sent.at[w, i, c], received.at[w, me], CAP * j + c
                ).start()
    for w in range(n_waves):
        sums = []
        for part in (2 * w, 2 * w + 1):
            odd = part % 2
            sent, received = (pairs_odd, pairs_in_odd) if odd else (pairs_even, pairs_in_even)
            pair = pairs_own[part, y_low, :, : received.shape[3]]
            for i in range(1, n_et):
                et_arrival(
                    PAIRS + part, sent.at[w, 0, 0], received.at[w, et_peer(i)], et_peer(i)
                ).wait_recv()
                pair = pair + received[w, et_peer(i)].astype(F32)
            sums.append(pair)
        squares = sums[1][:small, hidden_width:] + sums[1][small:, hidden_width:]
        left = iota((small, LANES), 1) < LANES // 2
        made = []
        for pair, lanes in zip(sums, (left, ~left)):
            level = lax.rsqrt(
                jnp.sum(jnp.where(lanes, squares, 0.0), axis=1, keepdims=True)
                * (2.0 / LANES / width)
                + EPS
            )
            first = pair[:small, :hidden_width] * level
            second = pair[small:, :hidden_width] * level
            made.append(first / (1.0 + jnp.exp(-first)) * second)
        hidden_out[w] = jnp.concatenate(made, axis=0).astype(BF16)
        for peer in et_far_first:
            et_copy(HIDDEN + w, hidden_out.at[w], hidden_in.at[w, me], peer).start()
        hidden_in[w, me] = hidden_out[w]

    loads["w_down"].wait()
    for w in range(n_waves):
        loop(
            n_et,
            lambda i: et_arrival(
                HIDDEN + w, hidden_out.at[w], hidden_in.at[w, et_peer(i)], et_peer(i)
            ).wait_recv(),
        )
        for j in range(n_local):
            hidden = hidden_in[w, CAP * j : CAP * (j + 1)].reshape(CAP * share, hidden_width)
            result = dot(hidden, w_down[j])
            for c in range(CAP):
                for h in range(2):
                    first = w * share * chunk + h * n_local * CAP + c * n_local + j
                    results_f[pl.ds(first, share, stride=chunk), :] = result[
                        c * share : (c + 1) * share, h * LANES : (h + 1) * LANES
                    ]
        results_out[w * share : (w + 1) * share] = (
            results_f[w * share * chunk : (w + 1) * share * chunk, :]
            .astype(BF16)
            .reshape(share, chunk, LANES)
        )
        ahead = lax.rem(own_part + jnp.where(lax.div(own_part, 2) == w, 1, 0), 2)
        for part in (2 * w + ahead, 2 * w + 1 - ahead):
            *rest, (last, place) = members(part)
            for number, (peer, slot) in enumerate(rest):
                stream_copy(
                    HOME, part * small + number, results_out.at[slot], results_in.at[me_s], peer
                ).start()
            unless_home(
                part,
                lambda: stream_copy(
                    HOME, (part + 1) * small - 1, results_out.at[place], results_in.at[me_s], last
                ).start(),
            )
    stream_arrival(HOME, results_out.at[at_home], results_in.at[me_s], at_home).start()

    def sent_et(exchange, source, target):
        loop(
            n_et,
            lambda i: et_copy(exchange, source, target, et_peer(i)).wait_send(),
        )

    sent_et(FEATURES, features.at[me], features.at[me])
    sent_et(HEADS, heads_out.at[0], heads_in.at[me])
    sent_et(MIXED, mixed_out, mixed_in.at[me])
    for part in range(parts):
        sent, received = (pairs_odd, pairs_in_odd) if part % 2 else (pairs_even, pairs_in_even)
        sent_et(PAIRS + part, sent.at[part // 2, 0, 0], received.at[part // 2, me])
    for w in range(n_waves):
        sent_et(HIDDEN + w, hidden_out.at[w], hidden_in.at[w, me])
    for number, peer in enumerate(outward):
        stream_copy(OUTWARD, number, rows_out.at[0], rows_in.at[at_home], peer).wait_send()
    for part in range(parts):
        *rest, (last, _) = members(part)
        for number, (peer, _) in enumerate(rest):
            stream_copy(
                HOME, part * small + number, results_out.at[0], results_in.at[me_s], peer
            ).wait_send()
        unless_home(
            part,
            lambda: stream_copy(
                HOME, (part + 1) * small - 1, results_out.at[0], results_in.at[me_s], last
            ).wait_send(),
        )

    for slot in range(n_stream):
        stream_arrival(
            HOME, results_out.at[0], results_in.at[stream_in[slot]], slot
        ).wait()
    returned = results_in[...].astype(F32)
    returned = (
        jnp.concatenate(
            [returned[:, : n_local * CAP], returned[:, n_local * CAP :]], axis=2
        )
        .reshape(slots, 2 * LANES)
        .astype(BF16)
    )
    routed = dot_tn(mixing_high, returned) + dot_tn(mixing_low, returned)
    out_ref[...] = (resid.astype(F32) + routed).astype(BF16)


def on_device(
    n_stream,
    n_et,
    residual_in,
    attn_gain,
    q_gain,
    key_norm_gain,
    w_q,
    key_value_weight,
    w_o,
    key_value_cache,
    cache_length,
    moe_gain,
    route_ids,
    route_gates,
    w_gate_up,
    w_down,
):
    tokens, features = residual_in.shape
    head_dim = q_gain.shape[0]
    local, span, _, kv_width = key_value_cache.shape
    kv_heads = kv_width // head_dim
    n_heads = w_q.shape[1] // head_dim * n_et
    n_local = w_gate_up.shape[0]
    hidden = w_down.shape[1]
    cache = (
        key_value_cache.reshape(local, span, 2, kv_heads, head_dim)
        .transpose(0, 1, 3, 2, 4)
        .reshape(local * span * kv_heads * 2, head_dim)
    )
    args = (
        residual_in,
        attn_gain.reshape(-1, LANES),
        q_gain.reshape(1, -1),
        key_norm_gain.reshape(1, -1),
        w_q,
        key_value_weight,
        w_o,
        cache,
        cache_length.reshape(1, -1),
        moe_gain.reshape(-1, LANES),
        route_ids.T,
        route_gates.T,
        w_gate_up,
        w_down,
    )
    chunk = 2 * n_local * CAP
    vmem = pltpu.VMEM
    row_blocks = (n_stream, chunk, LANES)
    flat_rows = ((n_stream + 1) * chunk, LANES)
    parts = parts_of(n_stream)
    n_waves = parts // 2
    share, small = n_stream // n_waves, n_stream // parts
    scratch = [vmem(a.shape, a.dtype) for a in args[1:]] + [
        vmem(((span + 1) * kv_heads * 2, head_dim), F32),
        vmem((local, 2, kv_heads // 2, span, 2 * head_dim), BF16),
        vmem((n_et, tokens, features), BF16),
        vmem((n_et, 16, head_dim), BF16),
        vmem((n_et, 16, head_dim), BF16),
        vmem((local * n_heads, head_dim), BF16),
        vmem((n_et, local * n_heads, head_dim), BF16),
        vmem(((tokens + 1) * n_heads, head_dim), F32),
        vmem(row_blocks, BF16),
        vmem(row_blocks, BF16),
        vmem(flat_rows, F32),
        vmem((parts, n_local, CAP * small, features), BF16),
        vmem((parts, n_local, CAP * small, LANES), F32),
        vmem((n_waves, n_local, CAP, 2 * small, hidden), BF16),
        vmem((n_waves, n_local, CAP, 2 * small, hidden + LANES), BF16),
        vmem((parts, CAP, 2 * small, hidden + LANES), F32),
        vmem((n_waves, n_et, 2 * small, hidden), BF16),
        vmem((n_waves, n_et, 2 * small, hidden + LANES), BF16),
        vmem((n_waves, share, hidden), BF16),
        vmem((n_waves, n_et, share, hidden), BF16),
        vmem(flat_rows, F32),
        vmem(row_blocks, BF16),
        vmem(row_blocks, BF16),
        pltpu.SemaphoreType.DMA((len(args),)),
        pltpu.SemaphoreType.DMA((9, n_et)),
        pltpu.SemaphoreType.DMA((9, n_et)),
        pltpu.SemaphoreType.DMA((2, n_stream)),
        pltpu.SemaphoreType.DMA((2, n_stream)),
        pltpu.SemaphoreType.REGULAR((3,)),
    ]
    return pl.pallas_call(
        functools.partial(kernel, n_stream, n_et),
        out_shape=pltpu.VMEM(residual_in.shape, residual_in.dtype),
        in_specs=[pl.BlockSpec(memory_space=pl.ANY)] * len(args),
        out_specs=pl.BlockSpec(memory_space=pltpu.VMEM),
        scratch_shapes=scratch,
        compiler_params=pltpu.CompilerParams(
            collective_id=0, has_side_effects=True, vmem_limit_bytes=56 * 1024 * 1024
        ),
    )(*args)


def solution(mesh):
    placed = (
        P("stream", "et"),
        P(),
        P(),
        P(),
        P(None, "et"),
        P(None, "et"),
        P(None, "et"),
        P(("stream", "et"), None, None, None),
        P("stream"),
        P("et"),
        P("stream", None),
        P("stream", None),
        P("stream", None, "et", None),
        P("stream", None, "et"),
    )
    return jax.shard_map(
        functools.partial(on_device, mesh.shape["stream"], mesh.shape["et"]),
        mesh=mesh,
        in_specs=placed,
        out_specs=P("stream", "et"),
        check_vma=False,
    )
```
